32 devices in a mesh: node: 8 (over y, x, core), local: 4 (over z).
Axes of the slice: x: 2, y: 2, z: 4, core: 2. Of those that a mesh axis runs over, the one named last changes fastest.
Arguments:
- tokens: bfloat16 [512, 4096], P('local', 'node'), may hold values from -6 to 6
- cotangent: bfloat16 [512, 4096], P('local', 'node'), may hold values from -0.25 to 0.25
- gain: bfloat16 [1, 4096], P(None, 'node'), may hold values from 0.099609375 to 1.8984375
- up_q: bfloat16 [4096, 14336], P('local', 'node'), may hold values from -4 to 4
- up_scale: bfloat16 [32, 14336], P('local', 'node'), may hold values from 0.0078125 to 0.0390625
- down_q: bfloat16 [14336, 4096], P('node', 'local'), may hold values from -4 to 4
- down_scale: bfloat16 [14336, 32], P('node', 'local'), may hold values from 0.005004883 to 0.025024414
Outputs:
- states: bfloat16 [512, 4096], P('local', 'node')
- grad_down: bfloat16 [14336, 4096], P('node', 'local')
The draws below stay inside these ranges and needn't reach their ends.
All inputs are finite; a program needn't handle non-finite values.
Results may differ from the reference program's by a relative error of at most 0.035.
Values may be sent and summed in bfloat16 or wider, within the bound.
No kernel may reach another device: no remote copies, remote signals or barrier semaphores. Data moves between devices by JAX's collectives and lax.ppermute only.
A program may use at most 128 MiB of HBM per device.

```python
import math
import jax
import jax.numpy as jnp
from jax import lax

BLOCK = 128
D = 4096
FF = 14336
LOOPS = 2
TOK_DEV = 128
TOKENS = 512
N_NODE = 8
N_LOCAL = 4


def raised(values, own_key, source, target, shards_of, factor):
    def block_of(dim):
        return (jnp.arange(values.shape[dim]) // (values.shape[dim] // shards_of)).reshape((-1,) + (1,) * (values.ndim - 1 - dim))

    one_side = jax.random.permutation(own_key, shards_of)[block_of(target)]
    second = (block_of(target) + shards_of // 2) % shards_of
    return jnp.where((block_of(source) == one_side) | (block_of(source) == second), factor * values, values)


def block_scale(rng, extent, cuts, low, top_value):
    level = 1.0
    for position, blocks in cuts:
        steps = jax.random.uniform(jax.random.fold_in(jax.random.fold_in(rng, 6), position), (blocks,), jnp.float32, low / len(cuts), top_value / len(cuts))
        level = level * jnp.repeat(jnp.exp(steps), extent[position] // blocks).reshape((-1,) + (1,) * (len(extent) - 1 - position))
    return level


def centred(rng, dims, spread, reach, shards=(), dtype=jnp.bfloat16):
    level = block_scale(rng, dims, shards, -0.22, 0.18) if shards else 1.0
    result = jax.random.normal(rng, dims, jnp.float32) * spread * level
    return jnp.minimum(jnp.maximum(result, -reach), reach).astype(dtype)


def noise_with(own_key, dims, spread, most, pieces, heavy, kind=jnp.bfloat16):
    drawn = spread * jax.random.normal(own_key, dims, jnp.float32)
    if pieces:
        drawn = drawn * block_scale(own_key, dims, pieces, -0.22, 0.18)
    return jnp.clip(raised(drawn, jax.random.fold_in(own_key, 3), *heavy), -most, most).astype(kind)


def setup_inputs(seed: int = 0) -> dict:
    seeds = jax.random.split(jax.random.key(seed), 8)
    return {
        "tokens": centred(seeds[0], (TOKENS, D), 1.0, 6.0, ((0, 4), (1, 8))),
        "cotangent": noise_with(seeds[1], (TOKENS, D), (1.0 / (TOKENS * LOOPS) ** 0.5), 0.25, ((0, 4), (1, 8)), (0, 1, 8, 2.0)),
        "gain": jnp.clip(1.0 + 0.18 * jax.random.normal(seeds[2], (1, D), jnp.float32), 0.099609375, 1.8984375).astype(jnp.bfloat16),
        "up_q": centred(seeds[3], (D, FF), 1.0, 4.0, ((0, 4), (1, 8))),
        "up_scale": jnp.clip(jnp.exp(math.log(0.0390625) - 1.609438 * jax.random.uniform(seeds[4], (D // BLOCK, FF), jnp.float32) ** block_scale(seeds[4], (D // BLOCK, FF), ((0, 4), (1, 8)), -0.2, 0.2)), 0.0078125, 0.0390625).astype(jnp.bfloat16),
        "down_q": centred(seeds[5], (FF, D), 1.0, 4.0, ((0, 8), (1, 4))),
        "down_scale": jnp.clip(jnp.exp(math.log(0.025024414) - 1.609438 * jax.random.uniform(seeds[6], (FF, D // BLOCK), jnp.float32) ** block_scale(seeds[6], (FF, D // BLOCK), ((0, 8), (1, 4)), -0.2, 0.2)), 0.005004883, 0.025024414).astype(jnp.bfloat16),
    }


epsilon = 1e-05

def dequant_rows(quanta, scales):
    blocks = scales.shape[0]
    widened = quanta.astype(jnp.float32).reshape(blocks, quanta.shape[0] // blocks, quanta.shape[1])
    return (widened * scales.astype(jnp.float32)[:, None, :]).reshape(quanta.shape).astype(jnp.bfloat16)

def dequant_cols(quanta, scales):
    blocks = scales.shape[1]
    widened = quanta.astype(jnp.float32).reshape(quanta.shape[0], blocks, quanta.shape[1] // blocks)
    return (widened * scales.astype(jnp.float32)[:, :, None]).reshape(quanta.shape).astype(jnp.bfloat16)

def normalize(values, gains):
    widened = values.astype(jnp.float32)
    meansq = lax.optimization_barrier(jnp.mean(widened * widened, axis=-1, keepdims=True)) + epsilon
    factor = lax.rsqrt(meansq)
    return ((widened * factor * gains).astype(jnp.bfloat16), factor)

def norm_backward(values, factor, gains, upstream):
    widened = values.astype(jnp.float32)
    scaled = upstream * gains
    inner = lax.optimization_barrier(jnp.mean(scaled * widened, axis=-1, keepdims=True))
    return factor * scaled - widened * factor * factor * factor * inner

def silu_slope(pre):
    sigma = jax.nn.sigmoid(pre)
    return sigma * (1.0 + pre * (1.0 - sigma))

def grouped_product(left, right, groups):
    width = left.shape[1] // groups
    left_blocks = left.reshape(left.shape[0], groups, width).transpose(1, 0, 2)
    right_blocks = right.reshape(groups, width, right.shape[1])

    def accumulate(total, pair):
        part = jnp.dot(pair[0], pair[1], preferred_element_type=jnp.float32)
        kept = lax.optimization_barrier(part.astype(jnp.bfloat16))
        return (total + kept.astype(jnp.float32), None)
    start = jnp.zeros((left.shape[0], right.shape[1]), jnp.float32)
    total, _ = lax.scan(accumulate, start, (left_blocks, right_blocks))
    return total

def reference(tokens, cotangent, gain, up_q, up_scale, down_q, down_scale):
    up_weight = dequant_rows(up_q, up_scale)
    down_weight = dequant_cols(down_q, down_scale)
    gains = gain.astype(jnp.float32)
    values = tokens
    saved = []
    for loop_index in range(LOOPS):
        normed, factor = normalize(values, gains)
        pre = jnp.dot(normed, up_weight, preferred_element_type=jnp.float32)
        hidden = jax.nn.silu(pre).astype(jnp.bfloat16)
        update = grouped_product(hidden, down_weight, N_NODE)
        saved.append((values, factor, pre, hidden))
        values = (values.astype(jnp.float32) + update).astype(jnp.bfloat16)
    carried = cotangent
    activations = []
    gradients = []
    for loop_index in reversed(range(LOOPS)):
        before, factor, pre, hidden = saved[loop_index]
        activations.append(hidden)
        gradients.append(carried)
        if loop_index > 0:
            slope = jnp.dot(carried, down_weight.T, preferred_element_type=jnp.float32)
            pre_grad = (slope * silu_slope(pre)).astype(jnp.bfloat16)
            normed_grad = grouped_product(pre_grad, up_weight.T, N_NODE)
            carried = (carried.astype(jnp.float32) + norm_backward(before, factor, gains, normed_grad)).astype(jnp.bfloat16)
    stacked_acts = jnp.stack(activations).reshape(LOOPS, N_LOCAL, TOK_DEV, FF)
    stacked_acts = stacked_acts.transpose(1, 0, 2, 3).reshape(N_LOCAL, LOOPS * TOK_DEV, FF)
    stacked_grads = jnp.stack(gradients).reshape(LOOPS, N_LOCAL, TOK_DEV, D)
    stacked_grads = stacked_grads.transpose(1, 0, 2, 3).reshape(N_LOCAL, LOOPS * TOK_DEV, D)

    def add_group(total, pair):
        part = lax.dot_general(pair[0], pair[1], (((0,), (0,)), ((), ())), preferred_element_type=jnp.float32)
        kept = lax.optimization_barrier(part.astype(jnp.bfloat16))
        return (total + kept.astype(jnp.float32), None)
    grad_total, _ = lax.scan(add_group, jnp.zeros((FF, D), jnp.float32), (stacked_acts, stacked_grads))
    return (values, grad_total.astype(jnp.bfloat16))
```

```python
import jax
import jax.numpy as jnp
from jax import lax
from jax.sharding import PartitionSpec as P

LOOPS = 2
epsilon = 1e-05
F32 = jnp.float32
BF16 = jnp.bfloat16


def dequant_rows(quanta, scales):
    blocks = scales.shape[0]
    widened = quanta.astype(F32).reshape(blocks, quanta.shape[0] // blocks, quanta.shape[1])
    return (widened * scales.astype(F32)[:, None, :]).reshape(quanta.shape).astype(BF16)


def dequant_cols(quanta, scales):
    blocks = scales.shape[1]
    widened = quanta.astype(F32).reshape(quanta.shape[0], blocks, quanta.shape[1] // blocks)
    return (widened * scales.astype(F32)[:, :, None]).reshape(quanta.shape).astype(BF16)


def dot(left, right, dims):
    return lax.dot_general(left, right, (dims, ((), ())), preferred_element_type=F32)


def body(n_node, n_local, tokens, cotangent, gain, up_q, up_scale, down_q, down_scale):
    rows, cols = tokens.shape
    halves = n_node // n_local
    features = cols * n_node
    total_rows = rows * n_local

    swap = [
        ((halves * c + j) * n_local + l, (halves * l + j) * n_local + c)
        for c in range(n_local)
        for j in range(halves)
        for l in range(n_local)
    ]

    def exchange(block):
        return lax.ppermute(block, ("node", "local"), swap)

    def gather_node(block):
        parts = lax.all_gather(block, "node", axis=0, tiled=False)
        parts = parts.reshape((n_local, halves) + block.shape)
        return parts.transpose(0, 2, 1, 3).reshape(total_rows, halves * cols)

    def scatter_node(partial):
        parts = partial.reshape(n_local, rows, halves, cols).transpose(0, 2, 1, 3)
        parts = parts.reshape(n_node, rows, cols)
        return lax.psum_scatter(parts, "node", scatter_dimension=0, tiled=False)

    def scatter_local(partial):
        return lax.psum_scatter(partial, "local", scatter_dimension=0, tiled=True)

    def gather_local(block):
        return lax.all_gather(block, "local", axis=0, tiled=True)

    local_index = lax.axis_index("local")
    node_index = lax.axis_index("node")

    def factor_of(values):
        widened = values.astype(F32)
        sums = lax.psum(jnp.sum(widened * widened, axis=-1, keepdims=True), "local")
        return lax.rsqrt(sums / features + epsilon)

    def own_local(column):
        return lax.dynamic_slice_in_dim(column, local_index * rows, rows, 0)

    gains_all = lax.all_gather(gain, "node", axis=1, tiled=True).astype(F32)
    gains = lax.dynamic_slice_in_dim(gains_all, local_index * halves * cols, halves * cols, 1)
    gains_home = lax.dynamic_slice_in_dim(gains, (node_index % halves) * cols, cols, 1)

    x_home = exchange(tokens)
    g_home = exchange(cotangent)
    up_weight = dequant_rows(up_q, up_scale)
    down_weight = dequant_cols(down_q, down_scale)

    x = gather_node(x_home)
    hiddens = []
    for loop_index in range(LOOPS):
        factor = factor_of(x)
        scaled = (x.astype(F32) * gains).astype(BF16)
        raw = dot(scaled, up_weight, ((1,), (0,))).astype(BF16)
        raw = scatter_local(raw).astype(F32)
        pre = (raw * own_local(factor)).astype(BF16)
        if loop_index == 0:
            hidden = gather_local(jax.nn.silu(pre.astype(F32)).astype(BF16))
        else:
            pre = gather_local(pre).astype(F32)
            hidden = jax.nn.silu(pre).astype(BF16)
        hiddens.append(hidden)
        update = dot(hidden, down_weight, ((1,), (0,))).astype(BF16)
        update = scatter_node(update).astype(F32)
        before_home = x_home
        x_home = (x_home.astype(F32) + update).astype(BF16)
        if loop_index < LOOPS - 1:
            x = gather_node(x_home)
    result = exchange(x_home)

    g = gather_node(g_home)
    slope = dot(g, down_weight, ((1,), (1,))).astype(BF16)
    slope = gather_local(scatter_local(slope)).astype(F32)
    sigma = jax.nn.sigmoid(pre)
    pre_grad = slope * sigma * (1.0 + pre * (1.0 - sigma))
    inner = jnp.sum(pre_grad * pre, axis=-1, keepdims=True)
    inner = lax.psum(inner, "node") / (features * factor)
    normed_grad = dot(pre_grad.astype(BF16), up_weight, ((1,), (1,))).astype(BF16)
    normed_grad = scatter_node(normed_grad).astype(F32)
    start = (node_index // halves) * rows
    factor_home = lax.dynamic_slice_in_dim(factor, start, rows, 0)
    inner_home = lax.dynamic_slice_in_dim(inner, start, rows, 0)
    back = factor_home * (normed_grad * gains_home) - before_home.astype(F32) * (
        factor_home * factor_home * factor_home * inner_home
    )
    below = (g_home.astype(F32) + back).astype(BF16)
    below = gather_node(below)
    grad_down = dot(
        jnp.concatenate(hiddens, axis=0), jnp.concatenate([below, g], axis=0), ((0,), (0,))
    ).astype(BF16)
    return (result, grad_down)


def solution(mesh):
    n_node, n_local = mesh.shape["node"], mesh.shape["local"]

    def per_device(*arrays):
        return body(n_node, n_local, *arrays)

    in_specs = (
        P("local", "node"),
        P("local", "node"),
        P(None, "node"),
        P("local", "node"),
        P("local", "node"),
        P("node", "local"),
        P("node", "local"),
    )
    out_specs = (P("local", "node"), P("node", "local"))
    return jax.shard_map(
        per_device, mesh=mesh, in_specs=in_specs, out_specs=out_specs, check_vma=False
    )
```

```python
import jax
import jax.numpy as jnp
from jax import lax
from jax.sharding import PartitionSpec as P

LOOPS = 2
LANES = 128
PAD = 16
epsilon = 1e-05
F32 = jnp.float32
BF16 = jnp.bfloat16


def dequant_rows(quanta, scales):
    blocks = scales.shape[0]
    widened = quanta.astype(F32).reshape(blocks, quanta.shape[0] // blocks, quanta.shape[1])
    return (widened * scales.astype(F32)[:, None, :]).reshape(quanta.shape).astype(BF16)


def dequant_cols(quanta, scales):
    blocks = scales.shape[1]
    widened = quanta.astype(F32).reshape(quanta.shape[0], blocks, quanta.shape[1] // blocks)
    return (widened * scales.astype(F32)[:, :, None]).reshape(quanta.shape).astype(BF16)


def dot(left, right, dims):
    return lax.dot_general(left, right, (dims, ((), ())), preferred_element_type=F32)


def body(n_node, n_local, tokens, cotangent, gain, up_q, up_scale, down_q, down_scale):
    rows, cols = tokens.shape
    halves = n_node // n_local
    chips = n_local
    features = cols * n_node
    z = lax.axis_index("local")
    node = lax.axis_index("node")
    chip, core = node // halves, node % halves

    swap = [
        ((halves * c + j) * n_local + l, (halves * l + j) * n_local + c)
        for c in range(n_local)
        for j in range(halves)
        for l in range(n_local)
    ]

    def exchange(block):
        return lax.ppermute(block, ("node", "local"), swap)

    def core_swap(block):
        return lax.ppermute(block, "node", [(n, n ^ 1) for n in range(n_node)])

    def chip_swap(block, shift):
        return lax.ppermute(block, "node", [(n, n ^ (2 * shift)) for n in range(n_node)])

    def take(array, index):
        return lax.dynamic_slice_in_dim(array, index * rows, rows, 0)

    def put(array, block, index):
        return lax.dynamic_update_slice_in_dim(array, block, index * rows, 0)

    def gather_chips(block):
        out = jnp.zeros((rows * chips, block.shape[1]), block.dtype)
        out = put(out, block, chip)
        for shift in range(1, chips):
            out = put(out, chip_swap(block, shift), chip ^ shift)
        return out

    def gather_node(block):
        mine = gather_chips(block)
        other = core_swap(mine)
        return jnp.where(
            core == 0,
            jnp.concatenate([mine, other], axis=1),
            jnp.concatenate([other, mine], axis=1),
        )

    def scatter_node(partial, column=None):
        parts = [partial[:, :cols], partial[:, cols:]]
        keep = jnp.where(core == 0, parts[0], parts[1])
        send = jnp.where(core == 0, parts[1], parts[0])
        if column is not None:
            high = column.astype(BF16)
            low = (column - high.astype(F32)).astype(BF16)
            shape = (column.shape[0], LANES // 2)
            tail = [jnp.broadcast_to(high, shape), jnp.broadcast_to(low, shape)]
            keep = jnp.concatenate([keep] + tail, axis=1)
            send = jnp.concatenate([send] + tail, axis=1)
        both = (keep.astype(F32) + core_swap(send).astype(F32)).astype(BF16)
        total = take(both, chip).astype(F32)
        for shift in range(1, chips):
            total = total + chip_swap(take(both, chip ^ shift), shift).astype(F32)
        if column is None:
            return total
        return total[:, :cols], total[:, cols : cols + 1] + total[:, -1:]

    def scatter_local(partial):
        right = left = None
        for step in range(1, n_local):
            send_right = take(partial, jnp.minimum(z + n_local - step, n_local - 1))
            send_left = take(partial, jnp.maximum(z - n_local + step, 0))
            if step > 1:
                send_right = (send_right.astype(F32) + right.astype(F32)).astype(BF16)
                send_left = (send_left.astype(F32) + left.astype(F32)).astype(BF16)
            right = lax.ppermute(send_right, "local", [(s, s + 1) for s in range(step)])
            left = lax.ppermute(
                send_left, "local", [(n_local - 1 - s, n_local - 2 - s) for s in range(step)]
            )
        return take(partial, z).astype(F32) + right.astype(F32) + left.astype(F32)

    def gather_local(block):
        right, left = [block], [block]
        for step in range(1, n_local):
            right.append(
                lax.ppermute(right[-1], "local", [(s, s + 1) for s in range(step - 1, n_local - 1)])
            )
            left.append(
                lax.ppermute(
                    left[-1],
                    "local",
                    [(n_local - 1 - s, n_local - 2 - s) for s in range(step - 1, n_local - 1)],
                )
            )
        out = jnp.zeros((rows * n_local, block.shape[1]), block.dtype)
        out = put(out, block, z)
        for ahead in range(1, n_local):
            behind = n_local - ahead
            piece = jnp.where(z >= behind, right[behind], left[ahead])
            out = put(out, piece, (z + ahead) % n_local)
        return out

    def factor_of(values):
        widened = values.astype(F32)
        own = jnp.sum(widened * widened, axis=-1).reshape(n_local, rows)
        sums = own
        for shift in range(1, n_local):
            sums = sums + lax.ppermute(
                own, "local", [(s, (s + shift) % n_local) for s in range(n_local)]
            )
        return lax.rsqrt(sums.reshape(n_local * rows, 1) / features + epsilon)

    first = exchange(
        jnp.concatenate([tokens, jnp.broadcast_to(gain, (PAD, cols))], axis=0)
    )
    x_home, gains_home = first[:rows], first[rows : rows + 1]
    g_home = exchange(cotangent)
    up_weight = dequant_rows(up_q, up_scale)
    down_weight = dequant_cols(down_q, down_scale)

    gains_other = core_swap(first[rows:])[:1]
    gains = jnp.where(
        core == 0,
        jnp.concatenate([gains_home, gains_other], axis=1),
        jnp.concatenate([gains_other, gains_home], axis=1),
    ).astype(F32)
    gains_home = gains_home.astype(F32)
    x = gather_node(x_home)
    hiddens = []
    for loop_index in range(LOOPS):
        factor = factor_of(x)
        scaled = (x.astype(F32) * gains).astype(BF16)
        raw = dot(scaled, up_weight, ((1,), (0,))).astype(BF16)
        pre = scatter_local(raw) * take(factor, z)
        if loop_index == 0:
            hidden = gather_local(jax.nn.silu(pre).astype(BF16))
        else:
            pre = gather_local(pre.astype(BF16)).astype(F32)
            hidden = jax.nn.silu(pre).astype(BF16)
        hiddens.append(hidden)
        update = dot(hidden, down_weight, ((1,), (0,))).astype(BF16)
        update = scatter_node(update)
        before_home = x_home
        x_home = (x_home.astype(F32) + update).astype(BF16)
        if loop_index < LOOPS - 1:
            x = gather_node(x_home)
    result = exchange(x_home)

    g = gather_node(g_home)
    slope = dot(g, down_weight, ((1,), (1,))).astype(BF16)
    slope = gather_local(scatter_local(slope).astype(BF16)).astype(F32)
    sigma = jax.nn.sigmoid(pre)
    pre_grad = slope * sigma * (1.0 + pre * (1.0 - sigma))
    inner = jnp.sum(pre_grad * pre, axis=-1, keepdims=True) / (features * factor)
    normed_grad = dot(pre_grad.astype(BF16), up_weight, ((1,), (1,))).astype(BF16)
    normed_grad, inner_home = scatter_node(normed_grad, inner)
    factor_home = take(factor, chip)
    back = factor_home * (normed_grad * gains_home) - before_home.astype(F32) * (
        factor_home * factor_home * factor_home * inner_home
    )
    below = gather_node((g_home.astype(F32) + back).astype(BF16))
    grad_down = dot(
        jnp.concatenate(hiddens, axis=0), jnp.concatenate([below, g], axis=0), ((0,), (0,))
    ).astype(BF16)
    return (result, grad_down)


def solution(mesh):
    n_node, n_local = mesh.shape["node"], mesh.shape["local"]

    def per_device(*arrays):
        return body(n_node, n_local, *arrays)

    in_specs = (
        P("local", "node"),
        P("local", "node"),
        P(None, "node"),
        P("local", "node"),
        P("local", "node"),
        P("node", "local"),
        P("node", "local"),
    )
    out_specs = (P("local", "node"), P("node", "local"))
    return jax.shard_map(
        per_device, mesh=mesh, in_specs=in_specs, out_specs=out_specs, check_vma=False
    )
```

```python
import jax
import jax.numpy as jnp
from jax import lax
from jax.sharding import PartitionSpec as P

LANES = 128
PAD = 16
CHUNKS = 2
epsilon = 1e-05
F32 = jnp.float32
BF16 = jnp.bfloat16


def dequant_rows(quanta, scales):
    blocks = scales.shape[0]
    widened = quanta.astype(F32).reshape(blocks, quanta.shape[0] // blocks, quanta.shape[1])
    return (widened * scales.astype(F32)[:, None, :]).reshape(quanta.shape).astype(BF16)


def dequant_cols(quanta, scales):
    blocks = scales.shape[1]
    widened = quanta.astype(F32).reshape(quanta.shape[0], blocks, quanta.shape[1] // blocks)
    return (widened * scales.astype(F32)[:, :, None]).reshape(quanta.shape).astype(BF16)


def dot(left, right, dims):
    return lax.dot_general(left, right, (dims, ((), ())), preferred_element_type=F32)


def split_pair(column):
    high = column.astype(BF16)
    low = (column - high.astype(F32)).astype(BF16)
    shape = (column.shape[0], LANES // 2)
    return [jnp.broadcast_to(high, shape), jnp.broadcast_to(low, shape)]


def join_pair(lanes):
    lanes = lanes.astype(F32)
    return lanes[:, :1] + lanes[:, -1:]


def body(n_node, n_local, tokens, cotangent, gain, up_q, up_scale, down_q, down_scale):
    rows, cols = tokens.shape
    part = rows // CHUNKS
    hidden_units = up_q.shape[1]
    halves = n_node // n_local
    chips = n_local
    features = cols * n_node
    z = lax.axis_index("local")
    node = lax.axis_index("node")
    chip, core = node // halves, node % halves
    last = n_local - 1

    swap = [
        ((halves * c + j) * n_local + l, (halves * l + j) * n_local + c)
        for c in range(n_local)
        for j in range(halves)
        for l in range(n_local)
    ]

    def exchange(block):
        return lax.ppermute(block, ("node", "local"), swap)

    def core_swap(block):
        return lax.ppermute(block, "node", [(n, n ^ 1) for n in range(n_node)])

    def chip_swap(block, shift):
        return lax.ppermute(block, "node", [(n, n ^ (2 * shift)) for n in range(n_node)])

    def send_right(block, senders):
        return lax.ppermute(block, "local", [(s, s + 1) for s in senders])

    def send_left(block, senders):
        return lax.ppermute(block, "local", [(last - s, last - 1 - s) for s in senders])

    def take(array, index):
        width = array.shape[1]
        array = array.reshape(-1, n_local, part, width)
        return lax.dynamic_slice_in_dim(array, index, 1, 1).reshape(-1, width)

    def put(array, block, index):
        width = array.shape[1]
        stacked = array.reshape(-1, n_local, part, width)
        block = block.reshape(-1, 1, part, width)
        return lax.dynamic_update_slice_in_dim(stacked, block, index, 1).reshape(array.shape)

    def order(own, other):
        return jnp.where(
            core == 0,
            jnp.concatenate([own, other], axis=1),
            jnp.concatenate([other, own], axis=1),
        )

    def gather_node(block):
        mine = jnp.zeros((block.shape[0] * chips, block.shape[1]), block.dtype)
        mine = put(mine, block, chip)
        for shift in range(1, chips):
            mine = put(mine, chip_swap(block, shift), chip ^ shift)
        return order(mine, core_swap(mine))

    def scatter_node(partial, tail=None):
        first, second = partial[:, :cols], partial[:, cols:]
        keep = jnp.where(core == 0, first, second)
        send = jnp.where(core == 0, second, first)
        if tail is not None:
            keep = jnp.concatenate([keep] + tail, axis=1)
            send = jnp.concatenate([send] + tail, axis=1)
        both = (keep.astype(F32) + core_swap(send).astype(F32)).astype(BF16)
        total = take(both, chip).astype(F32)
        for shift in range(1, chips):
            total = total + chip_swap(take(both, chip ^ shift), shift).astype(F32)
        return total

    def line(block, partial):
        right = left = None
        rights, lefts = [], []
        everyone = range(last)
        if block is not None:
            right, left = send_right(block, everyone), send_left(block, everyone)
            rights.append(right)
            lefts.append(left)
            if partial is None:
                for step in range(1, last):
                    right = send_right(right, range(step, last))
                    left = send_left(left, range(step, last))
                    rights.append(right)
                    lefts.append(left)
        total = None
        if partial is not None:
            for step in range(1, n_local):
                to_right = take(partial, jnp.minimum(z + n_local - step, last))
                to_left = take(partial, jnp.maximum(z - n_local + step, 0))
                if right is not None:
                    zero = jnp.zeros((), F32)
                    to_right = jnp.where(z < step, to_right.astype(F32), zero)
                    to_left = jnp.where(last - z < step, to_left.astype(F32), zero)
                    to_right = (right.astype(F32) + to_right).astype(BF16)
                    to_left = (left.astype(F32) + to_left).astype(BF16)
                senders = everyone if block is not None else range(step)
                right, left = send_right(to_right, senders), send_left(to_left, senders)
                rights.append(right)
                lefts.append(left)
            total = take(partial, z).astype(F32) + right.astype(F32) + left.astype(F32)
        out = None
        if block is not None:
            out = jnp.zeros((part * n_local, block.shape[1]), block.dtype)
            out = put(out, block, z)
            for ahead in range(1, n_local):
                behind = n_local - ahead
                piece = jnp.where(z >= behind, rights[behind - 1], lefts[ahead - 1])
                out = put(out, piece, (z + ahead) % n_local)
        return out, total

    def widen(block):
        return jnp.pad(block, ((0, 0), (0, LANES)))

    def chunk_of(array, h):
        size = part * n_local
        return array[h * size : (h + 1) * size]

    def up_partial(values):
        widened = values.astype(F32)
        squares = jnp.sum((widened * widened).reshape(values.shape[0], -1, LANES), axis=1)
        product = dot((widened * gains).astype(BF16), up_weight, ((1,), (0,)))
        return jnp.concatenate([product.astype(BF16), squares.astype(BF16)], axis=1)

    def finish_pre(total):
        mean = jnp.sum(total[:, hidden_units:], axis=-1, keepdims=True) / features
        factor = lax.rsqrt(mean + epsilon)
        return total[:, :hidden_units] * factor, factor

    first = exchange(jnp.concatenate([tokens, jnp.broadcast_to(gain, (PAD, cols))], axis=0))
    up_weight = dequant_rows(up_q, up_scale)
    down_weight = dequant_cols(down_q, down_scale)
    first, up_weight, down_weight = lax.optimization_barrier((first, up_weight, down_weight))
    x_home, gain_rows = first[:rows], first[rows:]
    gains = order(gain_rows, core_swap(gain_rows))[:1].astype(F32)
    gains_home = gain_rows[:1].astype(F32)
    g_home = exchange(cotangent)

    x = gather_node(x_home)
    partials = [up_partial(chunk_of(x, h)) for h in range(CHUNKS)]
    _, total = line(None, partials[0])
    hidden_own = jax.nn.silu(finish_pre(total)[0]).astype(BF16)
    hidden_a, total = line(widen(hidden_own), partials[1])
    hidden_a = hidden_a[:, :hidden_units]
    hidden_own = jax.nn.silu(finish_pre(total)[0]).astype(BF16)

    g = gather_node(g_home)
    slopes = [
        dot(chunk_of(g, h), down_weight, ((1,), (1,))).astype(BF16) for h in range(CHUNKS)
    ]
    hidden_b, total = line(hidden_own, slopes[0])
    hidden_first = [hidden_a, hidden_b]
    updates = [dot(hidden, down_weight, ((1,), (0,))).astype(BF16) for hidden in hidden_first]
    update = scatter_node(jnp.concatenate(updates, axis=0))
    x1_home = (x_home.astype(F32) + update).astype(BF16)
    slope_a, total = line(total.astype(BF16), slopes[1])

    x = gather_node(x1_home)
    partials = [up_partial(chunk_of(x, h)) for h in range(CHUNKS)]
    slope_b, total = line(widen(total.astype(BF16)), partials[0])
    slope_b = slope_b[:, :hidden_units]

    def pack_pre(total):
        pre, factor = finish_pre(total)
        return jnp.concatenate([pre.astype(BF16)] + split_pair(factor), axis=1)

    packed_a, total = line(pack_pre(total), partials[1])
    packed_b, _ = line(pack_pre(total), None)

    hidden_second, below = [], []
    for h, (packed, slope) in enumerate([(packed_a, slope_a), (packed_b, slope_b)]):
        pre = packed[:, :hidden_units].astype(F32)
        sigma = jax.nn.sigmoid(pre)
        hidden_second.append((pre * sigma).astype(BF16))
        pre_grad = slope.astype(F32) * sigma * (1.0 + pre * (1.0 - sigma))
        inner = jnp.sum(pre_grad * pre, axis=-1, keepdims=True)
        normed_grad = dot(pre_grad.astype(BF16), up_weight, ((1,), (1,))).astype(BF16)
        total = scatter_node(normed_grad, split_pair(inner))
        factor = join_pair(take(packed[:, hidden_units:], chip))
        inner = join_pair(total[:, cols:]) / (features * factor)
        back = factor * (total[:, :cols] * gains_home) - chunk_home(x1_home, h, part).astype(F32) * (
            factor * factor * factor * inner
        )
        grad_home = (chunk_home(g_home, h, part).astype(F32) + back).astype(BF16)
        below.append(gather_node(grad_home))
    updates = [dot(hidden, down_weight, ((1,), (0,))).astype(BF16) for hidden in hidden_second]
    update = scatter_node(jnp.concatenate(updates, axis=0))
    result = exchange((x1_home.astype(F32) + update).astype(BF16))
    grad_down = dot(
        jnp.concatenate(hidden_first + hidden_second, axis=0),
        jnp.concatenate(below + [g], axis=0),
        ((0,), (0,)),
    ).astype(BF16)
    return (result, grad_down)


def chunk_home(array, h, part):
    return array[h * part : (h + 1) * part]


def solution(mesh):
    n_node, n_local = mesh.shape["node"], mesh.shape["local"]

    def per_device(*arrays):
        return body(n_node, n_local, *arrays)

    in_specs = (
        P("local", "node"),
        P("local", "node"),
        P(None, "node"),
        P("local", "node"),
        P("local", "node"),
        P("node", "local"),
        P("node", "local"),
    )
    out_specs = (P("local", "node"), P("node", "local"))
    return jax.shard_map(
        per_device, mesh=mesh, in_specs=in_specs, out_specs=out_specs, check_vma=False
    )
```

```python
import jax
import jax.numpy as jnp
from jax import lax
from jax.sharding import PartitionSpec as P

LANES = 128
PAD = 16
CHUNKS = 1
epsilon = 1e-05
F32 = jnp.float32
BF16 = jnp.bfloat16


def dequant_rows(quanta, scales):
    blocks = scales.shape[0]
    widened = quanta.astype(F32).reshape(blocks, quanta.shape[0] // blocks, quanta.shape[1])
    return (widened * scales.astype(F32)[:, None, :]).reshape(quanta.shape).astype(BF16)


def dequant_cols(quanta, scales):
    blocks = scales.shape[1]
    widened = quanta.astype(F32).reshape(quanta.shape[0], blocks, quanta.shape[1] // blocks)
    return (widened * scales.astype(F32)[:, :, None]).reshape(quanta.shape).astype(BF16)


def dot(left, right, dims):
    return lax.dot_general(left, right, (dims, ((), ())), preferred_element_type=F32)


def split_pair(column):
    high = column.astype(BF16)
    low = (column - high.astype(F32)).astype(BF16)
    shape = (column.shape[0], LANES // 2)
    return [jnp.broadcast_to(high, shape), jnp.broadcast_to(low, shape)]


def join_pair(lanes):
    lanes = lanes.astype(F32)
    return lanes[:, :1] + lanes[:, -1:]


def body(n_node, n_local, tokens, cotangent, gain, up_q, up_scale, down_q, down_scale):
    rows, cols = tokens.shape
    part = rows // CHUNKS
    hidden_units = up_q.shape[1]
    halves = n_node // n_local
    chips = n_local
    features = cols * n_node
    z = lax.axis_index("local")
    node = lax.axis_index("node")
    chip, core = node // halves, node % halves

    swap = [
        ((halves * c + j) * n_local + l, (halves * l + j) * n_local + c)
        for c in range(n_local)
        for j in range(halves)
        for l in range(n_local)
    ]

    def exchange(block):
        return lax.ppermute(block, ("node", "local"), swap)

    def core_swap(block):
        return lax.ppermute(block, "node", [(n, n ^ 1) for n in range(n_node)])

    def chip_swap(block, shift):
        return lax.ppermute(block, "node", [(n, n ^ (2 * shift)) for n in range(n_node)])

    def take(array, index):
        width = array.shape[1]
        array = array.reshape(-1, n_local, part, width)
        return lax.dynamic_slice_in_dim(array, index, 1, 1).reshape(-1, width)

    def put(array, block, index):
        width = array.shape[1]
        stacked = array.reshape(-1, n_local, part, width)
        block = block.reshape(-1, 1, part, width)
        return lax.dynamic_update_slice_in_dim(stacked, block, index, 1).reshape(array.shape)

    def order(own, other):
        return jnp.where(
            core == 0,
            jnp.concatenate([own, other], axis=1),
            jnp.concatenate([other, own], axis=1),
        )

    def gather_node(block):
        mine = jnp.zeros((block.shape[0] * chips, block.shape[1]), block.dtype)
        mine = put(mine, block, chip)
        for shift in range(1, chips):
            mine = put(mine, chip_swap(block, shift), chip ^ shift)
        return order(mine, core_swap(mine))

    def scatter_node(partial, tail=None):
        first, second = partial[:, :cols], partial[:, cols:]
        keep = jnp.where(core == 0, first, second)
        send = jnp.where(core == 0, second, first)
        if tail is not None:
            keep = jnp.concatenate([keep] + tail, axis=1)
            send = jnp.concatenate([send] + tail, axis=1)
        both = (keep.astype(F32) + core_swap(send).astype(F32)).astype(BF16)
        total = take(both, chip).astype(F32)
        for shift in range(1, chips):
            total = total + chip_swap(take(both, chip ^ shift), shift).astype(F32)
        return total

    def ring(block):
        return lax.ppermute(block, "local", [(s, (s + 1) % n_local) for s in range(n_local)])

    def ring_reduce(partial):
        moving = take(partial, (z - 1) % n_local)
        for step in range(2, n_local + 1):
            moving = ring(moving).astype(F32) + take(partial, (z - step) % n_local).astype(F32)
            if step < n_local:
                moving = moving.astype(BF16)
        return moving

    def ring_gather(block):
        out = jnp.zeros((part * n_local, block.shape[1]), block.dtype)
        out = put(out, block, z)
        for step in range(1, n_local):
            block = ring(block)
            out = put(out, block, (z - step) % n_local)
        return out

    def chunk_of(array, h):
        size = part * n_local
        return array[h * size : (h + 1) * size]

    def up_partial(values):
        widened = values.astype(F32)
        squares = jnp.sum((widened * widened).reshape(values.shape[0], -1, LANES), axis=1)
        product = dot((widened * gains).astype(BF16), up_weight, ((1,), (0,)))
        return jnp.concatenate([product.astype(BF16), squares.astype(BF16)], axis=1)

    def finish_pre(total):
        mean = jnp.sum(total[:, hidden_units:], axis=-1, keepdims=True) / features
        factor = lax.rsqrt(mean + epsilon)
        return total[:, :hidden_units] * factor, factor

    first = exchange(jnp.concatenate([tokens, jnp.broadcast_to(gain, (PAD, cols))], axis=0))
    up_weight = dequant_rows(up_q, up_scale)
    down_weight = dequant_cols(down_q, down_scale)
    first, up_weight, down_weight = lax.optimization_barrier((first, up_weight, down_weight))
    x_home, gain_rows = first[:rows], first[rows:]
    gains = order(gain_rows, core_swap(gain_rows))[:1].astype(F32)
    gains_home = gain_rows[:1].astype(F32)
    g_home = exchange(cotangent)

    x = gather_node(x_home)
    g = gather_node(g_home)
    slopes = [
        dot(chunk_of(g, h), down_weight, ((1,), (1,))).astype(BF16) for h in range(CHUNKS)
    ]
    hidden_first, updates = [], []
    for h in range(CHUNKS):
        pre, _ = finish_pre(ring_reduce(up_partial(chunk_of(x, h))))
        hidden = jax.nn.silu(pre).astype(BF16)
        hidden, slopes[h] = lax.optimization_barrier((hidden, slopes[h]))
        slopes[h] = lax.psum_scatter(slopes[h], "local", scatter_dimension=0, tiled=True)
        hidden = ring_gather(hidden)
        hidden_first.append(hidden)
        updates.append(dot(hidden, down_weight, ((1,), (0,))).astype(BF16))
    update = scatter_node(jnp.concatenate(updates, axis=0))
    x1_home = (x_home.astype(F32) + update).astype(BF16)
    x1_home, slopes = lax.optimization_barrier((x1_home, slopes))
    slopes = [lax.all_gather(slope, "local", axis=0, tiled=True) for slope in slopes]

    x = gather_node(x1_home)
    hidden_second, grads, updates = [], [], []
    for h in range(CHUNKS):
        pre, factor = finish_pre(ring_reduce(up_partial(chunk_of(x, h))))
        packed = jnp.concatenate([pre.astype(BF16)] + split_pair(factor), axis=1)
        packed = ring_gather(packed)
        pre = packed[:, :hidden_units].astype(F32)
        sigma = jax.nn.sigmoid(pre)
        hidden_second.append((pre * sigma).astype(BF16))
        pre_grad = slopes[h].astype(F32) * sigma * (1.0 + pre * (1.0 - sigma))
        inner = jnp.sum(pre_grad * pre, axis=-1, keepdims=True)
        normed_grad = dot(pre_grad.astype(BF16), up_weight, ((1,), (1,))).astype(BF16)
        total = scatter_node(normed_grad, split_pair(inner))
        factor = join_pair(take(packed[:, hidden_units:], chip))
        inner = join_pair(total[:, cols:]) / (features * factor)
        before = chunk_home(x1_home, h, part).astype(F32)
        back = factor * (total[:, :cols] * gains_home) - before * (factor**3 * inner)
        grads.append((chunk_home(g_home, h, part).astype(F32) + back).astype(BF16))
        updates.append(dot(hidden_second[h], down_weight, ((1,), (0,))).astype(BF16))
    update = scatter_node(jnp.concatenate(updates, axis=0))
    x2_home = (x1_home.astype(F32) + update).astype(BF16)
    x2_home, grads = lax.optimization_barrier((x2_home, grads))
    result = exchange(x2_home)
    below = [gather_node(grad) for grad in grads]
    result, below = lax.optimization_barrier((result, below))
    grad_down = dot(
        jnp.concatenate(hidden_first + hidden_second, axis=0),
        jnp.concatenate(below + [g], axis=0),
        ((0,), (0,)),
    ).astype(BF16)
    return (result, grad_down)


def chunk_home(array, h, part):
    return array[h * part : (h + 1) * part]


def solution(mesh):
    n_node, n_local = mesh.shape["node"], mesh.shape["local"]

    def per_device(*arrays):
        return body(n_node, n_local, *arrays)

    in_specs = (
        P("local", "node"),
        P("local", "node"),
        P(None, "node"),
        P("local", "node"),
        P("local", "node"),
        P("node", "local"),
        P("node", "local"),
    )
    out_specs = (P("local", "node"), P("node", "local"))
    return jax.shard_map(
        per_device, mesh=mesh, in_specs=in_specs, out_specs=out_specs, check_vma=False
    )
```

```python
import jax
import jax.numpy as jnp
from jax import lax
from jax.sharding import PartitionSpec as P

LANES = 128
PAD = 16
CHUNKS = 2
epsilon = 1e-05
F32 = jnp.float32
BF16 = jnp.bfloat16


def dequant_rows(quanta, scales):
    blocks = scales.shape[0]
    widened = quanta.astype(F32).reshape(blocks, quanta.shape[0] // blocks, quanta.shape[1])
    return (widened * scales.astype(F32)[:, None, :]).reshape(quanta.shape).astype(BF16)


def dequant_cols(quanta, scales):
    blocks = scales.shape[1]
    widened = quanta.astype(F32).reshape(quanta.shape[0], blocks, quanta.shape[1] // blocks)
    return (widened * scales.astype(F32)[:, :, None]).reshape(quanta.shape).astype(BF16)


def dot(left, right, dims):
    return lax.dot_general(left, right, (dims, ((), ())), preferred_element_type=F32)


def split_pair(column):
    high = column.astype(BF16)
    low = (column - high.astype(F32)).astype(BF16)
    shape = (column.shape[0], LANES // 2)
    return [jnp.broadcast_to(high, shape), jnp.broadcast_to(low, shape)]


def join_pair(lanes):
    lanes = lanes.astype(F32)
    return lanes[:, :1] + lanes[:, -1:]


def body(n_node, n_local, tokens, cotangent, gain, up_q, up_scale, down_q, down_scale):
    rows, cols = tokens.shape
    part = rows // CHUNKS
    hidden_units = up_q.shape[1]
    halves = n_node // n_local
    chips = n_local
    features = cols * n_node
    z = lax.axis_index("local")
    node = lax.axis_index("node")
    chip, core = node // halves, node % halves

    swap = [
        ((halves * c + j) * n_local + l, (halves * l + j) * n_local + c)
        for c in range(n_local)
        for j in range(halves)
        for l in range(n_local)
    ]

    def exchange(block):
        return lax.ppermute(block, ("node", "local"), swap)

    def core_swap(block):
        return lax.ppermute(block, "node", [(n, n ^ 1) for n in range(n_node)])

    def chip_swap(block, shift):
        return lax.ppermute(block, "node", [(n, n ^ (2 * shift)) for n in range(n_node)])

    def take(array, index):
        width = array.shape[1]
        array = array.reshape(-1, n_local, part, width)
        return lax.dynamic_slice_in_dim(array, index, 1, 1).reshape(-1, width)

    def put(array, block, index):
        width = array.shape[1]
        stacked = array.reshape(-1, n_local, part, width)
        block = block.reshape(-1, 1, part, width)
        return lax.dynamic_update_slice_in_dim(stacked, block, index, 1).reshape(array.shape)

    def order(own, other):
        return jnp.where(
            core == 0,
            jnp.concatenate([own, other], axis=1),
            jnp.concatenate([other, own], axis=1),
        )

    def gather_node(block):
        mine = jnp.zeros((block.shape[0] * chips, block.shape[1]), block.dtype)
        mine = put(mine, block, chip)
        for shift in range(1, chips):
            mine = put(mine, chip_swap(block, shift), chip ^ shift)
        return order(mine, core_swap(mine))

    def scatter_node(partial, tail=None):
        first, second = partial[:, :cols], partial[:, cols:]
        keep = jnp.where(core == 0, first, second)
        send = jnp.where(core == 0, second, first)
        if tail is not None:
            keep = jnp.concatenate([keep] + tail, axis=1)
            send = jnp.concatenate([send] + tail, axis=1)
        both = (keep.astype(F32) + core_swap(send).astype(F32)).astype(BF16)
        total = take(both, chip).astype(F32)
        for shift in range(1, chips):
            total = total + chip_swap(take(both, chip ^ shift), shift).astype(F32)
        return total

    def after(value, *others):
        return lax.optimization_barrier((value,) + others)[0]

    def ring(block):
        return lax.ppermute(block, "local", [(s, (s + 1) % n_local) for s in range(n_local)])

    def ring_reduce(partial):
        moving = take(partial, (z - 1) % n_local)
        for step in range(2, n_local + 1):
            moving = ring(moving).astype(F32) + take(partial, (z - step) % n_local).astype(F32)
            if step < n_local:
                moving = moving.astype(BF16)
        return moving

    def ring_gather(block):
        out = jnp.zeros((part * n_local, block.shape[1]), block.dtype)
        out = put(out, block, z)
        for step in range(1, n_local):
            block = ring(block)
            out = put(out, block, (z - step) % n_local)
        return out

    def local_reduce(partial, h):
        if h % 2:
            return ring_reduce(partial)
        return lax.psum_scatter(partial, "local", scatter_dimension=0, tiled=True).astype(F32)

    def local_gather(block, h):
        if h % 2:
            return ring_gather(block)
        return lax.all_gather(block, "local", axis=0, tiled=True)

    def chunk_of(array, h):
        size = part * n_local
        return array[h * size : (h + 1) * size]

    def up_partial(values):
        widened = values.astype(F32)
        squares = jnp.sum((widened * widened).reshape(values.shape[0], -1, LANES), axis=1)
        product = dot((widened * gains).astype(BF16), up_weight, ((1,), (0,)))
        return jnp.concatenate([product.astype(BF16), squares.astype(BF16)], axis=1)

    def finish_pre(total):
        mean = jnp.sum(total[:, hidden_units:], axis=-1, keepdims=True) / features
        factor = lax.rsqrt(mean + epsilon)
        return total[:, :hidden_units] * factor, factor

    first = exchange(jnp.concatenate([tokens, jnp.broadcast_to(gain, (PAD, cols))], axis=0))
    up_weight = dequant_rows(up_q, up_scale)
    down_weight = dequant_cols(down_q, down_scale)
    first, up_weight, down_weight = lax.optimization_barrier((first, up_weight, down_weight))
    x_home, gain_rows = first[:rows], first[rows:]
    gains = order(gain_rows, core_swap(gain_rows))[:1].astype(F32)
    gains_home = gain_rows[:1].astype(F32)

    x = gather_node(x_home)
    g_home = exchange(after(cotangent, x))
    partials = [up_partial(chunk_of(x, h)) for h in range(CHUNKS)]
    g = gather_node(after(g_home, *partials))
    slopes = [
        dot(chunk_of(g, h), down_weight, ((1,), (1,))).astype(BF16) for h in range(CHUNKS)
    ]
    hidden_first, x1_homes = [], []
    for h in range(CHUNKS):
        pre, _ = finish_pre(local_reduce(partials[h], h))
        hidden = local_gather(jax.nn.silu(pre).astype(BF16), h)
        hidden_first.append(hidden)
        slopes[h] = local_reduce(slopes[h], h).astype(BF16)
        update = scatter_node(dot(hidden, down_weight, ((1,), (0,))).astype(BF16))
        x1_homes.append((chunk_home(x_home, h, part).astype(F32) + update).astype(BF16))

    hidden_second, grads, updates, below = [], [], [], []
    for h in range(CHUNKS):
        x = gather_node(x1_homes[h])
        pre, factor = finish_pre(local_reduce(up_partial(x), h))
        packed = jnp.concatenate([pre.astype(BF16)] + split_pair(factor), axis=1)
        slopes[h] = local_gather(slopes[h], h)
        packed = local_gather(packed, h)
        pre = packed[:, :hidden_units].astype(F32)
        sigma = jax.nn.sigmoid(pre)
        hidden_second.append((pre * sigma).astype(BF16))
        pre_grad = slopes[h].astype(F32) * sigma * (1.0 + pre * (1.0 - sigma))
        inner = jnp.sum(pre_grad * pre, axis=-1, keepdims=True)
        normed_grad = dot(pre_grad.astype(BF16), up_weight, ((1,), (1,))).astype(BF16)
        total = scatter_node(normed_grad, split_pair(inner))
        factor = join_pair(take(packed[:, hidden_units:], chip))
        inner = join_pair(total[:, cols:]) / (features * factor)
        before = x1_homes[h].astype(F32)
        back = factor * (total[:, :cols] * gains_home) - before * (factor**3 * inner)
        grads.append((chunk_home(g_home, h, part).astype(F32) + back).astype(BF16))
        updates.append(dot(hidden_second[h], down_weight, ((1,), (0,))).astype(BF16))
    update = scatter_node(jnp.concatenate(updates, axis=0))
    x1_home = jnp.concatenate(x1_homes, axis=0)
    x2_home = (x1_home.astype(F32) + update).astype(BF16)
    result = exchange(x2_home)
    below = [gather_node(grad) for grad in grads[:-1]]
    below.append(gather_node(after(grads[-1], x2_home)))
    result, below = lax.optimization_barrier((result, below))
    grad_down = dot(
        jnp.concatenate(hidden_first + hidden_second, axis=0),
        jnp.concatenate(below + [g], axis=0),
        ((0,), (0,)),
    ).astype(BF16)
    return (result, grad_down)


def chunk_home(array, h, part):
    return array[h * part : (h + 1) * part]


def solution(mesh):
    n_node, n_local = mesh.shape["node"], mesh.shape["local"]

    def per_device(*arrays):
        return body(n_node, n_local, *arrays)

    in_specs = (
        P("local", "node"),
        P("local", "node"),
        P(None, "node"),
        P("local", "node"),
        P("local", "node"),
        P("node", "local"),
        P("node", "local"),
    )
    out_specs = (P("local", "node"), P("node", "local"))
    return jax.shard_map(
        per_device, mesh=mesh, in_specs=in_specs, out_specs=out_specs, check_vma=False
    )
```

```python
import jax
import jax.numpy as jnp
from jax import lax
from jax.sharding import PartitionSpec as P

LANES = 128
PAD = 16
CHUNKS = 2
epsilon = 1e-05
F32 = jnp.float32
BF16 = jnp.bfloat16


def dequant_rows(quanta, scales):
    blocks = scales.shape[0]
    widened = quanta.astype(F32).reshape(blocks, quanta.shape[0] // blocks, quanta.shape[1])
    return (widened * scales.astype(F32)[:, None, :]).reshape(quanta.shape).astype(BF16)


def dequant_cols(quanta, scales):
    blocks = scales.shape[1]
    widened = quanta.astype(F32).reshape(quanta.shape[0], blocks, quanta.shape[1] // blocks)
    return (widened * scales.astype(F32)[:, :, None]).reshape(quanta.shape).astype(BF16)


def dot(left, right, dims):
    return lax.dot_general(left, right, (dims, ((), ())), preferred_element_type=F32)


def split_pair(column):
    high = column.astype(BF16)
    low = (column - high.astype(F32)).astype(BF16)
    shape = (column.shape[0], LANES // 2)
    return [jnp.broadcast_to(high, shape), jnp.broadcast_to(low, shape)]


def join_pair(lanes):
    lanes = lanes.astype(F32)
    return lanes[:, :1] + lanes[:, -1:]


def body(n_node, n_local, tokens, cotangent, gain, up_q, up_scale, down_q, down_scale):
    rows, cols = tokens.shape
    part = rows // CHUNKS
    hidden_units = up_q.shape[1]
    halves = n_node // n_local
    chips = n_local
    features = cols * n_node
    z = lax.axis_index("local")
    node = lax.axis_index("node")
    chip, core = node // halves, node % halves
    last = n_local - 1

    swap = [
        ((halves * c + j) * n_local + l, (halves * l + j) * n_local + c)
        for c in range(n_local)
        for j in range(halves)
        for l in range(n_local)
    ]

    def exchange(block):
        return lax.ppermute(block, ("node", "local"), swap)

    def core_swap(block):
        return lax.ppermute(block, "node", [(n, n ^ 1) for n in range(n_node)])

    def chip_swap(block, shift):
        return lax.ppermute(block, "node", [(n, n ^ (2 * shift)) for n in range(n_node)])

    even = z % 2 == 0

    def pair_swap(block, low):
        pairs = [(s, s + 1) for s in range(low, last, 2)]
        return lax.ppermute(block, "local", pairs + [(t, s) for s, t in pairs])

    def after(value, *others):
        return lax.optimization_barrier((value,) + others)[0]

    def take(array, index):
        width = array.shape[1]
        array = array.reshape(-1, n_local, part, width)
        return lax.dynamic_slice_in_dim(array, index, 1, 1).reshape(-1, width)

    def put(array, block, index):
        width = array.shape[1]
        stacked = array.reshape(-1, n_local, part, width)
        block = block.reshape(-1, 1, part, width)
        return lax.dynamic_update_slice_in_dim(stacked, block, index, 1).reshape(array.shape)

    def order(own, other):
        return jnp.where(
            core == 0,
            jnp.concatenate([own, other], axis=1),
            jnp.concatenate([other, own], axis=1),
        )

    def gather_chips(block):
        mine = jnp.zeros((block.shape[0] * chips, block.shape[1]), block.dtype)
        mine = put(mine, block, chip)
        for shift in range(1, chips):
            mine = put(mine, chip_swap(block, shift), chip ^ shift)
        return mine

    def gather_core(mine):
        return order(mine, core_swap(mine))

    def gather_node(block):
        return gather_core(gather_chips(block))

    def scatter_core(partial, tail=()):
        first, second = partial[:, :cols], partial[:, cols:]
        keep = jnp.where(core == 0, first, second)
        send = jnp.where(core == 0, second, first)
        if tail:
            keep = jnp.concatenate([keep, *tail], axis=1)
            send = jnp.concatenate([send, *tail], axis=1)
        return (keep.astype(F32) + core_swap(send).astype(F32)).astype(BF16)

    def scatter_chips(both):
        total = take(both, chip).astype(F32)
        for shift in range(1, chips):
            total = total + chip_swap(take(both, chip ^ shift), shift).astype(F32)
        return total

    def scatter_node(partial):
        return scatter_chips(scatter_core(partial))

    def line(block, partial, between=()):
        first = second = None
        firsts, seconds = [], []
        if block is not None:
            first, second = pair_swap(block, 0), pair_swap(block, 1)
            firsts.append(first)
            seconds.append(second)
        for step in range(1, n_local if partial is not None else last):
            to_first, to_second = second, first
            if partial is not None:
                right = jnp.minimum(z + n_local - step, last)
                left = jnp.maximum(z - n_local + step, 0)
                to_first = take(partial, jnp.where(even, right, left))
                to_second = take(partial, jnp.where(even, left, right))
                if first is not None:
                    zero = jnp.zeros((), F32)
                    adds_right, adds_left = z < step, last - z < step
                    adds = jnp.where(even, adds_right, adds_left)
                    to_first = jnp.where(adds, to_first.astype(F32), zero)
                    to_first = (second.astype(F32) + to_first).astype(BF16)
                    adds = jnp.where(even, adds_left, adds_right)
                    to_second = jnp.where(adds, to_second.astype(F32), zero)
                    to_second = (first.astype(F32) + to_second).astype(BF16)
            if step <= len(between):
                to_first = after(to_first, between[step - 1])
            first, second = pair_swap(to_first, 0), pair_swap(to_second, 1)
            firsts.append(first)
            seconds.append(second)
        total = None
        if partial is not None:
            total = take(partial, z).astype(F32) + first.astype(F32) + second.astype(F32)
        out = None
        if block is not None:
            out = jnp.zeros((part * n_local, block.shape[1]), block.dtype)
            out = put(out, block, z)
            for ahead in range(1, n_local):
                behind = n_local - ahead
                right = jnp.where(even, seconds[behind - 1], firsts[behind - 1])
                left = jnp.where(even, firsts[ahead - 1], seconds[ahead - 1])
                piece = jnp.where(z >= behind, right, left)
                out = put(out, piece, (z + ahead) % n_local)
        return out, total

    def widen(block):
        return jnp.pad(block, ((0, 0), (0, LANES)))

    def chunk_of(array, h):
        size = part * n_local
        return array[h * size : (h + 1) * size]

    def up_partial(values):
        widened = values.astype(F32)
        squares = jnp.sum((widened * widened).reshape(values.shape[0], -1, LANES), axis=1)
        product = dot((widened * gains).astype(BF16), up_weight, ((1,), (0,)))
        return jnp.concatenate([product.astype(BF16), squares.astype(BF16)], axis=1)

    def finish_pre(total):
        mean = jnp.sum(total[:, hidden_units:], axis=-1, keepdims=True) / features
        factor = lax.rsqrt(mean + epsilon)
        return total[:, :hidden_units] * factor, factor

    first = exchange(jnp.concatenate([tokens, jnp.broadcast_to(gain, (PAD, cols))], axis=0))
    g_home = exchange(cotangent)
    up_weight = dequant_rows(up_q, up_scale)
    down_weight = dequant_cols(down_q, down_scale)
    first, up_weight, down_weight = lax.optimization_barrier((first, up_weight, down_weight))
    x_home, gain_rows = first[:rows], first[rows:]
    gains = order(gain_rows, core_swap(gain_rows))[:1].astype(F32)
    gains_home = gain_rows[:1].astype(F32)

    x = gather_node(x_home)
    partials = [up_partial(chunk_of(x, h)) for h in range(CHUNKS)]
    _, total = line(None, partials[0])
    hidden_own = jax.nn.silu(finish_pre(total)[0]).astype(BF16)
    hidden_a, total = line(widen(hidden_own), partials[1])
    hidden_a = hidden_a[:, :hidden_units]
    hidden_own = jax.nn.silu(finish_pre(total)[0]).astype(BF16)

    g = gather_node(after(g_home, partials[0]))
    slopes = [
        dot(chunk_of(g, h), down_weight, ((1,), (1,))).astype(BF16) for h in range(CHUNKS)
    ]
    hidden_b, total = line(hidden_own, slopes[0])
    hidden_first = [hidden_a, hidden_b]
    updates = [dot(hidden, down_weight, ((1,), (0,))).astype(BF16) for hidden in hidden_first]
    update = scatter_node(jnp.concatenate(updates, axis=0))
    x1_home = (x_home.astype(F32) + update).astype(BF16)
    slope_a, total = line(total.astype(BF16), slopes[1])

    x = gather_node(x1_home)
    partials = [up_partial(chunk_of(x, h)) for h in range(CHUNKS)]
    slope_b, total = line(widen(total.astype(BF16)), partials[0])
    slope_b = slope_b[:, :hidden_units]

    def pack_pre(total):
        pre, factor = finish_pre(total)
        return jnp.concatenate([pre.astype(BF16)] + split_pair(factor), axis=1)

    packed_a, total = line(pack_pre(total), partials[1])
    packed_own = pack_pre(total)

    def back_units(packed, slope):
        pre = packed[:, :hidden_units].astype(F32)
        sigma = jax.nn.sigmoid(pre)
        pre_grad = slope.astype(F32) * sigma * (1.0 + pre * (1.0 - sigma))
        inner = jnp.sum(pre_grad * pre, axis=-1, keepdims=True)
        product = dot(pre_grad.astype(BF16), up_weight, ((1,), (1,))).astype(BF16)
        return (pre * sigma).astype(BF16), scatter_core(product, split_pair(inner))

    def back_home(total, packed, h):
        factor = join_pair(take(packed[:, hidden_units:], chip))
        inner = join_pair(total[:, cols:]) / (features * factor)
        before = chunk_home(x1_home, h, part).astype(F32)
        back = factor * (total[:, :cols] * gains_home) - before * (factor**3 * inner)
        return (chunk_home(g_home, h, part).astype(F32) + back).astype(BF16)

    hidden_2a, both = back_units(packed_a, slope_a)
    total_a = scatter_chips(both)
    packed_b, _ = line(packed_own, None, (both, total_a))
    below_a = gather_node(back_home(total_a, packed_a, 0))
    hidden_2b, both = back_units(packed_b, slope_b)
    total_b = scatter_chips(both)
    hidden_second = [hidden_2a, hidden_2b]
    updates = [dot(hidden, down_weight, ((1,), (0,))).astype(BF16) for hidden in hidden_second]
    update = scatter_node(jnp.concatenate(updates, axis=0))
    result = exchange((x1_home.astype(F32) + update).astype(BF16))
    mine = gather_chips(back_home(total_b, packed_b, 1))
    below_b = gather_core(after(mine, result))
    grad_down = dot(
        jnp.concatenate(hidden_first + hidden_second, axis=0),
        jnp.concatenate([below_a, below_b, g], axis=0),
        ((0,), (0,)),
    ).astype(BF16)
    return (result, grad_down)


def chunk_home(array, h, part):
    return array[h * part : (h + 1) * part]


def solution(mesh):
    n_node, n_local = mesh.shape["node"], mesh.shape["local"]

    def per_device(*arrays):
        return body(n_node, n_local, *arrays)

    in_specs = (
        P("local", "node"),
        P("local", "node"),
        P(None, "node"),
        P("local", "node"),
        P("local", "node"),
        P("node", "local"),
        P("node", "local"),
    )
    out_specs = (P("local", "node"), P("node", "local"))
    return jax.shard_map(
        per_device, mesh=mesh, in_specs=in_specs, out_specs=out_specs, check_vma=False
    )
```

```python
import jax
import jax.numpy as jnp
from jax import lax
from jax.sharding import PartitionSpec as P

LANES = 128
PAD = 16
CHUNKS = 1
epsilon = 1e-05
F32 = jnp.float32
BF16 = jnp.bfloat16


def dequant_rows(quanta, scales):
    blocks = scales.shape[0]
    widened = quanta.astype(F32).reshape(blocks, quanta.shape[0] // blocks, quanta.shape[1])
    return (widened * scales.astype(F32)[:, None, :]).reshape(quanta.shape).astype(BF16)


def dequant_cols(quanta, scales):
    blocks = scales.shape[1]
    widened = quanta.astype(F32).reshape(quanta.shape[0], blocks, quanta.shape[1] // blocks)
    return (widened * scales.astype(F32)[:, :, None]).reshape(quanta.shape).astype(BF16)


def dot(left, right, dims):
    return lax.dot_general(left, right, (dims, ((), ())), preferred_element_type=F32)


def split_pair(column):
    high = column.astype(BF16)
    low = (column - high.astype(F32)).astype(BF16)
    shape = (column.shape[0], LANES // 2)
    return [jnp.broadcast_to(high, shape), jnp.broadcast_to(low, shape)]


def join_pair(lanes):
    lanes = lanes.astype(F32)
    return lanes[:, :1] + lanes[:, -1:]


def body(n_node, n_local, tokens, cotangent, gain, up_q, up_scale, down_q, down_scale):
    rows, cols = tokens.shape
    part = rows // CHUNKS
    hidden_units = up_q.shape[1]
    halves = n_node // n_local
    chips = n_local
    features = cols * n_node
    z = lax.axis_index("local")
    node = lax.axis_index("node")
    chip, core = node // halves, node % halves

    swap = [
        ((halves * c + j) * n_local + l, (halves * l + j) * n_local + c)
        for c in range(n_local)
        for j in range(halves)
        for l in range(n_local)
    ]

    def exchange(block):
        return lax.ppermute(block, ("node", "local"), swap)

    def core_swap(block):
        return lax.ppermute(block, "node", [(n, n ^ 1) for n in range(n_node)])

    def chip_swap(block, shift):
        return lax.ppermute(block, "node", [(n, n ^ (2 * shift)) for n in range(n_node)])

    def after(value, *others):
        return lax.optimization_barrier((value,) + others)[0]

    def take(array, index):
        width = array.shape[1]
        array = array.reshape(-1, n_local, part, width)
        return lax.dynamic_slice_in_dim(array, index, 1, 1).reshape(-1, width)

    def put(array, block, index):
        width = array.shape[1]
        stacked = array.reshape(-1, n_local, part, width)
        block = block.reshape(-1, 1, part, width)
        return lax.dynamic_update_slice_in_dim(stacked, block, index, 1).reshape(array.shape)

    def order(own, other):
        return jnp.where(
            core == 0,
            jnp.concatenate([own, other], axis=1),
            jnp.concatenate([other, own], axis=1),
        )

    def gather_chips(block):
        mine = jnp.zeros((block.shape[0] * chips, block.shape[1]), block.dtype)
        mine = put(mine, block, chip)
        for shift in range(1, chips):
            mine = put(mine, chip_swap(block, shift), chip ^ shift)
        return mine

    def gather_core(mine):
        return order(mine, core_swap(mine))

    def gather_node(block):
        return gather_core(gather_chips(block))

    def scatter_core(partial, tail=()):
        first, second = partial[:, :cols], partial[:, cols:]
        keep = jnp.where(core == 0, first, second)
        send = jnp.where(core == 0, second, first)
        if tail:
            keep = jnp.concatenate([keep, *tail], axis=1)
            send = jnp.concatenate([send, *tail], axis=1)
        return (keep.astype(F32) + core_swap(send).astype(F32)).astype(BF16)

    def scatter_chips(both):
        total = take(both, chip).astype(F32)
        for shift in range(1, chips):
            total = total + chip_swap(take(both, chip ^ shift), shift).astype(F32)
        return total

    def scatter_node(partial):
        return scatter_chips(scatter_core(partial))

    def ring(block):
        return lax.ppermute(block, "local", [(s, (s + 1) % n_local) for s in range(n_local)])

    def reduce_local(partial):
        return lax.psum_scatter(partial, "local", scatter_dimension=0, tiled=True).astype(F32)

    def gather_local(block):
        return lax.all_gather(block, "local", axis=0, tiled=True)

    def up_partial(values):
        widened = values.astype(F32)
        squares = jnp.sum((widened * widened).reshape(values.shape[0], -1, LANES), axis=1)
        product = dot((widened * gains).astype(BF16), up_weight, ((1,), (0,)))
        return jnp.concatenate([product.astype(BF16), squares.astype(BF16)], axis=1)

    def finish_pre(total):
        mean = jnp.sum(total[:, hidden_units:], axis=-1, keepdims=True) / features
        factor = lax.rsqrt(mean + epsilon)
        return total[:, :hidden_units] * factor, factor

    first = exchange(
        jnp.concatenate([tokens, cotangent, jnp.broadcast_to(gain, (PAD, cols))], axis=0)
    )
    up_weight = dequant_rows(up_q, up_scale)
    down_weight = dequant_cols(down_q, down_scale)
    first, up_weight, down_weight = lax.optimization_barrier((first, up_weight, down_weight))
    x_home, g_home, gain_rows = first[:rows], first[rows : 2 * rows], first[2 * rows :]
    gains = order(gain_rows, core_swap(gain_rows))[:1].astype(F32)
    gains_home = gain_rows[:1].astype(F32)

    x_mine = gather_chips(x_home)
    g_mine = gather_chips(after(g_home, x_mine))
    partial = after(up_partial(gather_core(x_mine)), g_mine)
    total = reduce_local(partial)
    g = gather_core(after(g_mine, partial))
    slope_part = dot(g, down_weight, ((1,), (1,))).astype(BF16)
    moving = take(slope_part, (z - 1) % n_local)
    moving = ring(moving).astype(F32) + take(slope_part, (z - 2) % n_local).astype(F32)
    moving = moving.astype(BF16)
    total = after(total, moving)
    hidden_own = jax.nn.silu(finish_pre(total)[0]).astype(BF16)

    hidden_1 = gather_local(hidden_own)
    moving = after(moving, hidden_own)
    for step in range(3, n_local + 1):
        moving = ring(moving).astype(F32) + take(slope_part, (z - step) % n_local).astype(F32)
        moving = moving.astype(BF16)
    slope = put(jnp.zeros((rows * n_local, hidden_units), BF16), moving, z)
    hidden_1 = after(hidden_1, moving)
    update = scatter_node(dot(hidden_1, down_weight, ((1,), (0,))).astype(BF16))
    x1_home = (x_home.astype(F32) + update).astype(BF16)
    moving = ring(moving)
    slope = put(slope, moving, (z - 1) % n_local)

    x = after(gather_node(x1_home), moving)
    partial = up_partial(x)
    total = reduce_local(partial)
    moving = after(moving, partial)
    for step in range(2, n_local):
        moving = ring(moving)
        slope = put(slope, moving, (z - step) % n_local)
    total = after(total, moving)
    pre, factor = finish_pre(total)
    packed = gather_local(jnp.concatenate([pre.astype(BF16)] + split_pair(factor), axis=1))

    pre = packed[:, :hidden_units].astype(F32)
    sigma = jax.nn.sigmoid(pre)
    hidden_2 = (pre * sigma).astype(BF16)
    update = dot(hidden_2, down_weight, ((1,), (0,))).astype(BF16)
    slope = after(slope, update).astype(F32)
    pre_grad = slope * sigma * (1.0 + pre * (1.0 - sigma))
    inner = jnp.sum(pre_grad * pre, axis=-1, keepdims=True)
    normed_grad = dot(pre_grad.astype(BF16), up_weight, ((1,), (1,))).astype(BF16)
    update = scatter_core(update)
    both = after(scatter_core(normed_grad, split_pair(inner)), update)
    x2_home = (x1_home.astype(F32) + scatter_chips(update)).astype(BF16)
    result = exchange(x2_home)
    total = scatter_chips(both)
    factor = join_pair(take(packed[:, hidden_units:], chip))
    inner = join_pair(total[:, cols:]) / (features * factor)
    back = factor * (total[:, :cols] * gains_home) - x1_home.astype(F32) * (factor**3 * inner)
    grad_home = (g_home.astype(F32) + back).astype(BF16)
    mine = gather_chips(after(grad_home, x2_home))
    below = gather_core(after(mine, result))
    grad_down = dot(
        jnp.concatenate([hidden_1, hidden_2], axis=0),
        jnp.concatenate([below, g], axis=0),
        ((0,), (0,)),
    ).astype(BF16)
    return (result, grad_down)


def solution(mesh):
    n_node, n_local = mesh.shape["node"], mesh.shape["local"]

    def per_device(*arrays):
        return body(n_node, n_local, *arrays)

    in_specs = (
        P("local", "node"),
        P("local", "node"),
        P(None, "node"),
        P("local", "node"),
        P("local", "node"),
        P("node", "local"),
        P("node", "local"),
    )
    out_specs = (P("local", "node"), P("node", "local"))
    return jax.shard_map(
        per_device, mesh=mesh, in_specs=in_specs, out_specs=out_specs, check_vma=False
    )
```

```python
import jax
import jax.numpy as jnp
from jax import lax
from jax.sharding import PartitionSpec as P

LANES = 128
PAD = 16
CHUNKS = 2
epsilon = 1e-05
F32 = jnp.float32
BF16 = jnp.bfloat16


def dequant_rows(quanta, scales):
    blocks = scales.shape[0]
    widened = quanta.astype(F32).reshape(blocks, quanta.shape[0] // blocks, quanta.shape[1])
    return (widened * scales.astype(F32)[:, None, :]).reshape(quanta.shape).astype(BF16)


def dequant_cols(quanta, scales):
    blocks = scales.shape[1]
    widened = quanta.astype(F32).reshape(quanta.shape[0], blocks, quanta.shape[1] // blocks)
    return (widened * scales.astype(F32)[:, :, None]).reshape(quanta.shape).astype(BF16)


def dot(left, right, dims):
    return lax.dot_general(left, right, (dims, ((), ())), preferred_element_type=F32)


def split_pair(column):
    high = column.astype(BF16)
    low = (column - high.astype(F32)).astype(BF16)
    shape = (column.shape[0], LANES // 2)
    return [jnp.broadcast_to(high, shape), jnp.broadcast_to(low, shape)]


def join_pair(lanes):
    lanes = lanes.astype(F32)
    return lanes[:, :1] + lanes[:, -1:]


def body(n_node, n_local, tokens, cotangent, gain, up_q, up_scale, down_q, down_scale):
    rows, cols = tokens.shape
    part = rows // CHUNKS
    hidden_units = up_q.shape[1]
    halves = n_node // n_local
    chips = n_local
    features = cols * n_node
    z = lax.axis_index("local")
    node = lax.axis_index("node")
    chip, core = node // halves, node % halves
    last = n_local - 1

    swap = [
        ((halves * c + j) * n_local + l, (halves * l + j) * n_local + c)
        for c in range(n_local)
        for j in range(halves)
        for l in range(n_local)
    ]

    def exchange(block):
        return lax.ppermute(block, ("node", "local"), swap)

    def core_swap(block):
        return lax.ppermute(block, "node", [(n, n ^ 1) for n in range(n_node)])

    def chip_swap(block, shift):
        return lax.ppermute(block, "node", [(n, n ^ (2 * shift)) for n in range(n_node)])

    even = z % 2 == 0

    def pair_swap(block, low):
        pairs = [(s, s + 1) for s in range(low, last, 2)]
        return lax.ppermute(block, "local", pairs + [(t, s) for s, t in pairs])

    def after(value, *others):
        return lax.optimization_barrier((value,) + others)[0]

    def take(array, index):
        width = array.shape[1]
        array = array.reshape(-1, n_local, part, width)
        return lax.dynamic_slice_in_dim(array, index, 1, 1).reshape(-1, width)

    def put(array, block, index):
        width = array.shape[1]
        stacked = array.reshape(-1, n_local, part, width)
        block = block.reshape(-1, 1, part, width)
        return lax.dynamic_update_slice_in_dim(stacked, block, index, 1).reshape(array.shape)

    def order(own, other):
        return jnp.where(
            core == 0,
            jnp.concatenate([own, other], axis=1),
            jnp.concatenate([other, own], axis=1),
        )

    def gather_chips(block):
        mine = jnp.zeros((block.shape[0] * chips, block.shape[1]), block.dtype)
        mine = put(mine, block, chip)
        for shift in range(1, chips):
            mine = put(mine, chip_swap(block, shift), chip ^ shift)
        return mine

    def gather_core(mine):
        return order(mine, core_swap(mine))

    def gather_node(block):
        return gather_core(gather_chips(block))

    def scatter_core(partial, tail=()):
        first, second = partial[:, :cols], partial[:, cols:]
        keep = jnp.where(core == 0, first, second)
        send = jnp.where(core == 0, second, first)
        if tail:
            keep = jnp.concatenate([keep, *tail], axis=1)
            send = jnp.concatenate([send, *tail], axis=1)
        return (keep.astype(F32) + core_swap(send).astype(F32)).astype(BF16)

    def scatter_chips(both):
        total = take(both, chip).astype(F32)
        for shift in range(1, chips):
            total = total + chip_swap(take(both, chip ^ shift), shift).astype(F32)
        return total

    def scatter_node(partial):
        return scatter_chips(scatter_core(partial))

    def line(block, partial):
        first = second = None
        firsts, seconds = [], []
        if block is not None:
            first, second = pair_swap(block, 0), pair_swap(block, 1)
            firsts.append(first)
            seconds.append(second)
        for step in range(1, n_local if partial is not None else last):
            to_first, to_second = second, first
            if partial is not None:
                right = jnp.minimum(z + n_local - step, last)
                left = jnp.maximum(z - n_local + step, 0)
                to_first = take(partial, jnp.where(even, right, left))
                to_second = take(partial, jnp.where(even, left, right))
                if first is not None:
                    zero = jnp.zeros((), F32)
                    adds_right, adds_left = z < step, last - z < step
                    adds = jnp.where(even, adds_right, adds_left)
                    to_first = jnp.where(adds, to_first.astype(F32), zero)
                    to_first = (second.astype(F32) + to_first).astype(BF16)
                    adds = jnp.where(even, adds_left, adds_right)
                    to_second = jnp.where(adds, to_second.astype(F32), zero)
                    to_second = (first.astype(F32) + to_second).astype(BF16)
            first, second = pair_swap(to_first, 0), pair_swap(to_second, 1)
            firsts.append(first)
            seconds.append(second)
        total = None
        if partial is not None:
            total = take(partial, z).astype(F32) + first.astype(F32) + second.astype(F32)
        out = None
        if block is not None:
            out = jnp.zeros((part * n_local, block.shape[1]), block.dtype)
            out = put(out, block, z)
            for ahead in range(1, n_local):
                behind = n_local - ahead
                right = jnp.where(even, seconds[behind - 1], firsts[behind - 1])
                left = jnp.where(even, firsts[ahead - 1], seconds[ahead - 1])
                piece = jnp.where(z >= behind, right, left)
                out = put(out, piece, (z + ahead) % n_local)
        return out, total

    def widen(block):
        return jnp.pad(block, ((0, 0), (0, LANES)))

    def chunk_of(array, h):
        size = part * n_local
        return array[h * size : (h + 1) * size]

    def up_partial(values):
        widened = values.astype(F32)
        squares = jnp.sum((widened * widened).reshape(values.shape[0], -1, LANES), axis=1)
        product = dot((widened * gains).astype(BF16), up_weight, ((1,), (0,)))
        return jnp.concatenate([product.astype(BF16), squares.astype(BF16)], axis=1)

    def finish_pre(total):
        mean = jnp.sum(total[:, hidden_units:], axis=-1, keepdims=True) / features
        factor = lax.rsqrt(mean + epsilon)
        return total[:, :hidden_units] * factor, factor

    first = exchange(jnp.concatenate([tokens, jnp.broadcast_to(gain, (PAD, cols))], axis=0))
    g_home = exchange(cotangent)
    up_weight = dequant_rows(up_q, up_scale)
    down_weight = dequant_cols(down_q, down_scale)
    first, up_weight, down_weight = lax.optimization_barrier((first, up_weight, down_weight))
    x_home, gain_rows = first[:rows], first[rows:]
    gains = order(gain_rows, core_swap(gain_rows))[:1].astype(F32)
    gains_home = gain_rows[:1].astype(F32)

    halves_of = range(CHUNKS)

    x_mine = after(gather_chips(x_home), g_home)
    x = gather_core(x_mine)
    partials = [up_partial(chunk_of(x, h)) for h in halves_of]
    totals = [line(None, partial)[1] for partial in partials]
    g = gather_node(after(g_home, *partials))
    slopes = [
        dot(chunk_of(g, h), down_weight, ((1,), (1,))).astype(BF16) for h in halves_of
    ]
    hiddens, x1_homes = [], []
    for h in halves_of:
        hidden = jax.nn.silu(finish_pre(totals[h])[0]).astype(BF16)
        hidden, total = line(hidden, slopes[h])
        hiddens.append(hidden)
        slopes[h] = total.astype(BF16)
        update = scatter_node(dot(hidden, down_weight, ((1,), (0,))).astype(BF16))
        x1_homes.append((chunk_home(x_home, h, part).astype(F32) + update).astype(BF16))

    packed = []
    for h in halves_of:
        slope, total = line(widen(slopes[h]), up_partial(gather_node(x1_homes[h])))
        slopes[h] = slope[:, :hidden_units]
        pre, factor = finish_pre(total)
        packed.append(
            line(jnp.concatenate([pre.astype(BF16)] + split_pair(factor), axis=1), None)[0]
        )
    x1_home = jnp.concatenate(x1_homes, axis=0)

    hidden_second, updates, backs, inners = [], [], [], []
    for h in halves_of:
        pre = packed[h][:, :hidden_units].astype(F32)
        hidden_second.append((pre * jax.nn.sigmoid(pre)).astype(BF16))
        updates.append(dot(hidden_second[h], down_weight, ((1,), (0,))).astype(BF16))
    for h in halves_of:
        pre = packed[h][:, :hidden_units].astype(F32)
        sigma = jax.nn.sigmoid(pre)
        pre_grad = after(slopes[h], *updates).astype(F32) * sigma * (1.0 + pre * (1.0 - sigma))
        inners.append(jnp.sum(pre_grad * pre, axis=-1, keepdims=True))
        backs.append(dot(pre_grad.astype(BF16), up_weight, ((1,), (1,))).astype(BF16))
    update = scatter_core(jnp.concatenate(updates, axis=0))
    both = scatter_core(
        jnp.concatenate(backs, axis=0), split_pair(jnp.concatenate(inners, axis=0))
    )
    both = after(both, update)
    x2_home = (x1_home.astype(F32) + scatter_chips(update)).astype(BF16)
    result = exchange(x2_home)
    total = scatter_chips(both)
    factor = jnp.concatenate(
        [join_pair(take(half[:, hidden_units:], chip)) for half in packed], axis=0
    )
    inner = join_pair(total[:, cols:]) / (features * factor)
    back = factor * (total[:, :cols] * gains_home) - x1_home.astype(F32) * (factor**3 * inner)
    grad_home = (g_home.astype(F32) + back).astype(BF16)
    mine = gather_chips(after(grad_home, x2_home))
    below = gather_core(after(mine, result))
    grad_down = dot(
        jnp.concatenate(hiddens + hidden_second, axis=0),
        jnp.concatenate([below, g], axis=0),
        ((0,), (0,)),
    ).astype(BF16)
    return (result, grad_down)


def chunk_home(array, h, part):
    return array[h * part : (h + 1) * part]


def solution(mesh):
    n_node, n_local = mesh.shape["node"], mesh.shape["local"]

    def per_device(*arrays):
        return body(n_node, n_local, *arrays)

    in_specs = (
        P("local", "node"),
        P("local", "node"),
        P(None, "node"),
        P("local", "node"),
        P("local", "node"),
        P("node", "local"),
        P("node", "local"),
    )
    out_specs = (P("local", "node"), P("node", "local"))
    return jax.shard_map(
        per_device, mesh=mesh, in_specs=in_specs, out_specs=out_specs, check_vma=False
    )
```

```python
import jax
import jax.numpy as jnp
from jax import lax
from jax.sharding import PartitionSpec as P

LANES = 128
PAD = 16
CHUNKS = 2
epsilon = 1e-05
F32 = jnp.float32
BF16 = jnp.bfloat16


def dequant_rows(quanta, scales):
    blocks = scales.shape[0]
    widened = quanta.astype(F32).reshape(blocks, quanta.shape[0] // blocks, quanta.shape[1])
    return (widened * scales.astype(F32)[:, None, :]).reshape(quanta.shape).astype(BF16)


def dequant_cols(quanta, scales):
    blocks = scales.shape[1]
    widened = quanta.astype(F32).reshape(quanta.shape[0], blocks, quanta.shape[1] // blocks)
    return (widened * scales.astype(F32)[:, :, None]).reshape(quanta.shape).astype(BF16)


def dot(left, right, dims):
    return lax.dot_general(left, right, (dims, ((), ())), preferred_element_type=F32)


def split_pair(column):
    high = column.astype(BF16)
    low = (column - high.astype(F32)).astype(BF16)
    shape = (column.shape[0], LANES // 2)
    return [jnp.broadcast_to(high, shape), jnp.broadcast_to(low, shape)]


def join_pair(lanes):
    lanes = lanes.astype(F32)
    return lanes[:, :1] + lanes[:, -1:]


def body(n_node, n_local, tokens, cotangent, gain, up_q, up_scale, down_q, down_scale):
    rows, cols = tokens.shape
    part = rows // CHUNKS
    hidden_units = up_q.shape[1]
    halves = n_node // n_local
    chips = n_local
    features = cols * n_node
    z = lax.axis_index("local")
    node = lax.axis_index("node")
    chip, core = node // halves, node % halves
    last = n_local - 1

    swap = [
        ((halves * c + j) * n_local + l, (halves * l + j) * n_local + c)
        for c in range(n_local)
        for j in range(halves)
        for l in range(n_local)
    ]

    def exchange(block):
        return lax.ppermute(block, ("node", "local"), swap)

    def core_swap(block):
        return lax.ppermute(block, "node", [(n, n ^ 1) for n in range(n_node)])

    def chip_swap(block, shift):
        return lax.ppermute(block, "node", [(n, n ^ (2 * shift)) for n in range(n_node)])

    even = z % 2 == 0

    def pair_swap(block, low):
        pairs = [(s, s + 1) for s in range(low, last, 2)]
        return lax.ppermute(block, "local", pairs + [(t, s) for s, t in pairs])

    def after(value, *others):
        return lax.optimization_barrier((value,) + others)[0]

    def take(array, index):
        width = array.shape[1]
        array = array.reshape(-1, n_local, part, width)
        return lax.dynamic_slice_in_dim(array, index, 1, 1).reshape(-1, width)

    def put(array, block, index):
        width = array.shape[1]
        stacked = array.reshape(-1, n_local, part, width)
        block = block.reshape(-1, 1, part, width)
        return lax.dynamic_update_slice_in_dim(stacked, block, index, 1).reshape(array.shape)

    def order(own, other):
        return jnp.where(
            core == 0,
            jnp.concatenate([own, other], axis=1),
            jnp.concatenate([other, own], axis=1),
        )

    def gather_chips(block):
        mine = jnp.zeros((block.shape[0] * chips, block.shape[1]), block.dtype)
        mine = put(mine, block, chip)
        for shift in range(1, chips):
            mine = put(mine, chip_swap(block, shift), chip ^ shift)
        return mine

    def gather_core(mine):
        return order(mine, core_swap(mine))

    def gather_node(block):
        return gather_core(gather_chips(block))

    def scatter_core(partial, tail=()):
        first, second = partial[:, :cols], partial[:, cols:]
        keep = jnp.where(core == 0, first, second)
        send = jnp.where(core == 0, second, first)
        if tail:
            keep = jnp.concatenate([keep, *tail], axis=1)
            send = jnp.concatenate([send, *tail], axis=1)
        return (keep.astype(F32) + core_swap(send).astype(F32)).astype(BF16)

    def scatter_chips(both):
        total = take(both, chip).astype(F32)
        for shift in range(1, chips):
            total = total + chip_swap(take(both, chip ^ shift), shift).astype(F32)
        return total

    def scatter_node(partial):
        return scatter_chips(scatter_core(partial))

    def line(block, partial):
        first = second = None
        firsts, seconds = [], []
        if block is not None:
            first, second = pair_swap(block, 0), pair_swap(block, 1)
            firsts.append(first)
            seconds.append(second)
        for step in range(1, n_local if partial is not None else last):
            to_first, to_second = second, first
            if partial is not None:
                right = jnp.minimum(z + n_local - step, last)
                left = jnp.maximum(z - n_local + step, 0)
                to_first = take(partial, jnp.where(even, right, left))
                to_second = take(partial, jnp.where(even, left, right))
                if first is not None:
                    zero = jnp.zeros((), F32)
                    adds_right, adds_left = z < step, last - z < step
                    adds = jnp.where(even, adds_right, adds_left)
                    to_first = jnp.where(adds, to_first.astype(F32), zero)
                    to_first = (second.astype(F32) + to_first).astype(BF16)
                    adds = jnp.where(even, adds_left, adds_right)
                    to_second = jnp.where(adds, to_second.astype(F32), zero)
                    to_second = (first.astype(F32) + to_second).astype(BF16)
            first, second = pair_swap(to_first, 0), pair_swap(to_second, 1)
            firsts.append(first)
            seconds.append(second)
        total = None
        if partial is not None:
            total = take(partial, z).astype(F32) + first.astype(F32) + second.astype(F32)
        out = None
        if block is not None:
            out = jnp.zeros((part * n_local, block.shape[1]), block.dtype)
            out = put(out, block, z)
            for ahead in range(1, n_local):
                behind = n_local - ahead
                right = jnp.where(even, seconds[behind - 1], firsts[behind - 1])
                left = jnp.where(even, firsts[ahead - 1], seconds[ahead - 1])
                piece = jnp.where(z >= behind, right, left)
                out = put(out, piece, (z + ahead) % n_local)
        return out, total

    def widen(block):
        return jnp.pad(block, ((0, 0), (0, LANES)))

    def chunk_of(array, h):
        size = part * n_local
        return array[h * size : (h + 1) * size]

    def up_partial(values):
        widened = values.astype(F32)
        squares = jnp.sum((widened * widened).reshape(values.shape[0], -1, LANES), axis=1)
        product = dot((widened * gains).astype(BF16), up_weight, ((1,), (0,)))
        return jnp.concatenate([product.astype(BF16), squares.astype(BF16)], axis=1)

    def finish_pre(total):
        mean = jnp.sum(total[:, hidden_units:], axis=-1, keepdims=True) / features
        factor = lax.rsqrt(mean + epsilon)
        return total[:, :hidden_units] * factor, factor

    first = exchange(jnp.concatenate([tokens, jnp.broadcast_to(gain, (PAD, cols))], axis=0))
    g_home = exchange(cotangent)
    up_weight = dequant_rows(up_q, up_scale)
    down_weight = dequant_cols(down_q, down_scale)
    first, up_weight, down_weight = lax.optimization_barrier((first, up_weight, down_weight))
    x_home, gain_rows = first[:rows], first[rows:]
    gains = order(gain_rows, core_swap(gain_rows))[:1].astype(F32)
    gains_home = gain_rows[:1].astype(F32)

    halves_of = range(CHUNKS)

    x = after(gather_node(x_home), g_home)
    partials = [up_partial(chunk_of(x, h)) for h in halves_of]
    totals = [line(None, partial)[1] for partial in partials]
    g = gather_node(after(g_home, *partials))
    slopes = [
        dot(chunk_of(g, h), down_weight, ((1,), (1,))).astype(BF16) for h in halves_of
    ]
    hiddens = []
    for h in halves_of:
        hidden = jax.nn.silu(finish_pre(totals[h])[0]).astype(BF16)
        hidden, total = line(hidden, slopes[h])
        hiddens.append(hidden)
        slopes[h] = total.astype(BF16)
    updates = [dot(hidden, down_weight, ((1,), (0,))).astype(BF16) for hidden in hiddens]
    update = scatter_node(jnp.concatenate(updates, axis=0))
    x1_home = (x_home.astype(F32) + update).astype(BF16)

    x = gather_node(x1_home)
    packed = []
    for h in halves_of:
        slope, total = line(widen(slopes[h]), up_partial(chunk_of(x, h)))
        slopes[h] = slope[:, :hidden_units]
        pre, factor = finish_pre(total)
        packed.append(
            line(jnp.concatenate([pre.astype(BF16)] + split_pair(factor), axis=1), None)[0]
        )

    hidden_second, updates = [], []
    for half in packed:
        pre = half[:, :hidden_units].astype(F32)
        hidden_second.append((pre * jax.nn.sigmoid(pre)).astype(BF16))
        updates.append(dot(hidden_second[-1], down_weight, ((1,), (0,))).astype(BF16))
    update = scatter_core(jnp.concatenate(updates, axis=0))
    backs, tails = [], []
    for h in halves_of:
        slope = after(slopes[h], *(updates if h == 0 else [update]))
        pre = packed[h][:, :hidden_units].astype(F32)
        sigma = jax.nn.sigmoid(pre)
        pre_grad = slope.astype(F32) * sigma * (1.0 + pre * (1.0 - sigma))
        inner = jnp.sum(pre_grad * pre, axis=-1, keepdims=True)
        tails.append(jnp.concatenate(split_pair(inner), axis=1))
        backs.append(dot(pre_grad.astype(BF16), up_weight, ((1,), (1,))).astype(BF16))
    both = scatter_core(jnp.concatenate(backs, axis=0), [jnp.concatenate(tails, axis=0)])
    x2_home = (x1_home.astype(F32) + scatter_chips(update)).astype(BF16)
    result = exchange(x2_home)
    total = scatter_chips(after(both, x2_home))
    lanes = [take(half[:, hidden_units:], chip) for half in packed]
    factor = join_pair(jnp.concatenate(lanes, axis=0))
    inner = join_pair(total[:, cols:]) / (features * factor)
    back = factor * (total[:, :cols] * gains_home) - x1_home.astype(F32) * (factor**3 * inner)
    grad_home = (g_home.astype(F32) + back).astype(BF16)
    below = gather_node(after(grad_home, result))
    grad_down = dot(
        jnp.concatenate(hiddens + hidden_second, axis=0),
        jnp.concatenate([below, g], axis=0),
        ((0,), (0,)),
    ).astype(BF16)
    return (result, grad_down)


def solution(mesh):
    n_node, n_local = mesh.shape["node"], mesh.shape["local"]

    def per_device(*arrays):
        return body(n_node, n_local, *arrays)

    in_specs = (
        P("local", "node"),
        P("local", "node"),
        P(None, "node"),
        P("local", "node"),
        P("local", "node"),
        P("node", "local"),
        P("node", "local"),
    )
    out_specs = (P("local", "node"), P("node", "local"))
    return jax.shard_map(
        per_device, mesh=mesh, in_specs=in_specs, out_specs=out_specs, check_vma=False
    )
```

```python
import jax
import jax.numpy as jnp
from jax import lax
from jax.sharding import PartitionSpec as P

LANES = 128
PAD = 16
CHUNKS = 2
epsilon = 1e-05
F32 = jnp.float32
BF16 = jnp.bfloat16


def dequant_rows(quanta, scales):
    blocks = scales.shape[0]
    widened = quanta.astype(F32).reshape(blocks, quanta.shape[0] // blocks, quanta.shape[1])
    return (widened * scales.astype(F32)[:, None, :]).reshape(quanta.shape).astype(BF16)


def dequant_cols(quanta, scales):
    blocks = scales.shape[1]
    widened = quanta.astype(F32).reshape(quanta.shape[0], blocks, quanta.shape[1] // blocks)
    return (widened * scales.astype(F32)[:, :, None]).reshape(quanta.shape).astype(BF16)


def dot(left, right, dims):
    return lax.dot_general(left, right, (dims, ((), ())), preferred_element_type=F32)


def split_pair(column):
    high = column.astype(BF16)
    low = (column - high.astype(F32)).astype(BF16)
    shape = (column.shape[0], LANES // 2)
    return [jnp.broadcast_to(high, shape), jnp.broadcast_to(low, shape)]


def join_pair(lanes):
    lanes = lanes.astype(F32)
    return lanes[:, :1] + lanes[:, -1:]


def body(n_node, n_local, tokens, cotangent, gain, up_q, up_scale, down_q, down_scale):
    rows, cols = tokens.shape
    part = rows // CHUNKS
    hidden_units = up_q.shape[1]
    halves = n_node // n_local
    chips = n_local
    features = cols * n_node
    z = lax.axis_index("local")
    node = lax.axis_index("node")
    chip, core = node // halves, node % halves
    last = n_local - 1

    swap = [
        ((halves * c + j) * n_local + l, (halves * l + j) * n_local + c)
        for c in range(n_local)
        for j in range(halves)
        for l in range(n_local)
    ]

    def exchange(block):
        return lax.ppermute(block, ("node", "local"), swap)

    def core_swap(block):
        return lax.ppermute(block, "node", [(n, n ^ 1) for n in range(n_node)])

    def chip_swap(block, shift):
        return lax.ppermute(block, "node", [(n, n ^ (2 * shift)) for n in range(n_node)])

    even = z % 2 == 0

    def pair_swap(block, low):
        pairs = [(s, s + 1) for s in range(low, last, 2)]
        return lax.ppermute(block, "local", pairs + [(t, s) for s, t in pairs])

    def after(value, *others):
        return lax.optimization_barrier((value,) + others)[0]

    def take(array, index):
        width = array.shape[1]
        array = array.reshape(-1, n_local, part, width)
        return lax.dynamic_slice_in_dim(array, index, 1, 1).reshape(-1, width)

    def put(array, block, index):
        width = array.shape[1]
        stacked = array.reshape(-1, n_local, part, width)
        block = block.reshape(-1, 1, part, width)
        return lax.dynamic_update_slice_in_dim(stacked, block, index, 1).reshape(array.shape)

    def order(own, other):
        return jnp.where(
            core == 0,
            jnp.concatenate([own, other], axis=1),
            jnp.concatenate([other, own], axis=1),
        )

    def gather_chips(block):
        mine = jnp.zeros((block.shape[0] * chips, block.shape[1]), block.dtype)
        mine = put(mine, block, chip)
        for shift in range(1, chips):
            mine = put(mine, chip_swap(block, shift), chip ^ shift)
        return mine

    def gather_core(mine):
        return order(mine, core_swap(mine))

    def gather_node(block):
        return gather_core(gather_chips(block))

    def scatter_core(partial, tail=()):
        first, second = partial[:, :cols], partial[:, cols:]
        keep = jnp.where(core == 0, first, second)
        send = jnp.where(core == 0, second, first)
        if tail:
            keep = jnp.concatenate([keep, *tail], axis=1)
            send = jnp.concatenate([send, *tail], axis=1)
        return (keep.astype(F32) + core_swap(send).astype(F32)).astype(BF16)

    def scatter_chips(both):
        total = take(both, chip).astype(F32)
        for shift in range(1, chips):
            total = total + chip_swap(take(both, chip ^ shift), shift).astype(F32)
        return total

    def scatter_node(partial):
        return scatter_chips(scatter_core(partial))

    def line(block, partial):
        first = second = None
        firsts, seconds = [], []
        if block is not None:
            first, second = pair_swap(block, 0), pair_swap(block, 1)
            firsts.append(first)
            seconds.append(second)
        for step in range(1, n_local if partial is not None else last):
            to_first, to_second = second, first
            if partial is not None:
                right = jnp.minimum(z + n_local - step, last)
                left = jnp.maximum(z - n_local + step, 0)
                to_first = take(partial, jnp.where(even, right, left))
                to_second = take(partial, jnp.where(even, left, right))
                if first is not None:
                    zero = jnp.zeros((), F32)
                    adds_right, adds_left = z < step, last - z < step
                    adds = jnp.where(even, adds_right, adds_left)
                    to_first = jnp.where(adds, to_first.astype(F32), zero)
                    to_first = (second.astype(F32) + to_first).astype(BF16)
                    adds = jnp.where(even, adds_left, adds_right)
                    to_second = jnp.where(adds, to_second.astype(F32), zero)
                    to_second = (first.astype(F32) + to_second).astype(BF16)
            first, second = pair_swap(to_first, 0), pair_swap(to_second, 1)
            firsts.append(first)
            seconds.append(second)
        total = None
        if partial is not None:
            total = take(partial, z).astype(F32) + first.astype(F32) + second.astype(F32)
        out = None
        if block is not None:
            out = jnp.zeros((part * n_local, block.shape[1]), block.dtype)
            out = put(out, block, z)
            for ahead in range(1, n_local):
                behind = n_local - ahead
                right = jnp.where(even, seconds[behind - 1], firsts[behind - 1])
                left = jnp.where(even, firsts[ahead - 1], seconds[ahead - 1])
                piece = jnp.where(z >= behind, right, left)
                out = put(out, piece, (z + ahead) % n_local)
        return out, total, firsts[0]

    def widen(block):
        return jnp.pad(block, ((0, 0), (0, LANES)))

    def chunk_of(array, h):
        size = part * n_local
        return array[h * size : (h + 1) * size]

    def up_partial(values):
        widened = values.astype(F32)
        squares = jnp.sum((widened * widened).reshape(values.shape[0], -1, LANES), axis=1)
        product = dot((widened * gains).astype(BF16), up_weight, ((1,), (0,)))
        return jnp.concatenate([product.astype(BF16), squares.astype(BF16)], axis=1)

    def finish_pre(total):
        mean = jnp.sum(total[:, hidden_units:], axis=-1, keepdims=True) / features
        factor = lax.rsqrt(mean + epsilon)
        return total[:, :hidden_units] * factor, factor

    first = exchange(jnp.concatenate([tokens, jnp.pad(gain, ((0, PAD - 1), (0, 0)))], axis=0))
    g_home = exchange(cotangent)
    up_weight = dequant_rows(up_q, up_scale)
    down_weight = dequant_cols(down_q, down_scale)
    first, up_weight, down_weight = lax.optimization_barrier((first, up_weight, down_weight))
    x_home, gain_rows = first[:rows], first[rows:]
    gains = order(gain_rows, core_swap(gain_rows))[:1].astype(F32)
    gains_home = gain_rows[:1].astype(F32)

    halves_of = range(CHUNKS)

    x = gather_core(after(gather_chips(x_home), g_home))
    partials = [up_partial(chunk_of(x, h)) for h in halves_of]
    totals, seen = [], []
    for partial in partials:
        _, total, arrived = line(None, partial)
        totals.append(total)
        seen.append(arrived)
    g = gather_node(after(g_home, seen[0]))
    slopes = [
        dot(chunk_of(g, h), down_weight, ((1,), (1,))).astype(BF16) for h in halves_of
    ]
    hiddens = []
    for h in halves_of:
        hidden = jax.nn.silu(finish_pre(totals[h])[0]).astype(BF16)
        hidden, total, _ = line(hidden, slopes[h])
        hiddens.append(hidden)
        slopes[h] = total.astype(BF16)
    updates = [dot(hidden, down_weight, ((1,), (0,))).astype(BF16) for hidden in hiddens]
    update = scatter_node(jnp.concatenate(updates, axis=0))
    x1_home = (x_home.astype(F32) + update).astype(BF16)

    x = gather_node(x1_home)
    packed = []
    for h in halves_of:
        slope, total, _ = line(widen(slopes[h]), up_partial(chunk_of(x, h)))
        slopes[h] = slope[:, :hidden_units]
        pre, factor = finish_pre(total)
        packed.append(
            line(jnp.concatenate([pre.astype(BF16)] + split_pair(factor), axis=1), None)[0]
        )

    hidden_second, updates = [], []
    for half in packed:
        pre = half[:, :hidden_units].astype(F32)
        hidden_second.append((pre * jax.nn.sigmoid(pre)).astype(BF16))
        updates.append(dot(hidden_second[-1], down_weight, ((1,), (0,))).astype(BF16))
    update = scatter_core(jnp.concatenate(updates, axis=0))
    backs, tails = [], []
    for h in halves_of:
        slope = slopes[h] if h == 0 else after(slopes[h], update)
        pre = packed[h][:, :hidden_units].astype(F32)
        sigma = jax.nn.sigmoid(pre)
        pre_grad = slope.astype(F32) * sigma * (1.0 + pre * (1.0 - sigma))
        inner = jnp.sum(pre_grad * pre, axis=-1, keepdims=True)
        tails.append(jnp.concatenate(split_pair(inner), axis=1))
        backs.append(dot(pre_grad.astype(BF16), up_weight, ((1,), (1,))).astype(BF16))
    both = scatter_core(jnp.concatenate(backs, axis=0), [jnp.concatenate(tails, axis=0)])
    x2_home = (x1_home.astype(F32) + scatter_chips(update)).astype(BF16)
    result = exchange(x2_home)
    total = scatter_chips(after(both, x2_home))
    lanes = [take(half[:, hidden_units:], chip) for half in packed]
    factor = join_pair(jnp.concatenate(lanes, axis=0))
    inner = join_pair(total[:, cols:]) / (features * factor)
    back = factor * (total[:, :cols] * gains_home) - x1_home.astype(F32) * (factor**3 * inner)
    grad_home = (g_home.astype(F32) + back).astype(BF16)
    grad_second = dot(jnp.concatenate(hidden_second, axis=0), g, ((0,), (0,))).astype(BF16)
    below = gather_node(after(grad_home, result, grad_second))
    grad_first = dot(jnp.concatenate(hiddens, axis=0), below, ((0,), (0,)))
    grad_down = (grad_first + grad_second.astype(F32)).astype(BF16)
    return (result, grad_down)


def solution(mesh):
    n_node, n_local = mesh.shape["node"], mesh.shape["local"]

    def per_device(*arrays):
        return body(n_node, n_local, *arrays)

    in_specs = (
        P("local", "node"),
        P("local", "node"),
        P(None, "node"),
        P("local", "node"),
        P("local", "node"),
        P("node", "local"),
        P("node", "local"),
    )
    out_specs = (P("local", "node"), P("node", "local"))
    return jax.shard_map(
        per_device, mesh=mesh, in_specs=in_specs, out_specs=out_specs, check_vma=False
    )
```

```python
import jax
import jax.numpy as jnp
from jax import lax
from jax.sharding import PartitionSpec as P

LANES = 128
PAD = 16
CHUNKS = 2
epsilon = 1e-05
F32 = jnp.float32
BF16 = jnp.bfloat16


def dequant_rows(quanta, scales):
    blocks = scales.shape[0]
    widened = quanta.astype(F32).reshape(blocks, quanta.shape[0] // blocks, quanta.shape[1])
    return (widened * scales.astype(F32)[:, None, :]).reshape(quanta.shape).astype(BF16)


def dequant_cols(quanta, scales):
    blocks = scales.shape[1]
    widened = quanta.astype(F32).reshape(quanta.shape[0], blocks, quanta.shape[1] // blocks)
    return (widened * scales.astype(F32)[:, :, None]).reshape(quanta.shape).astype(BF16)


def dot(left, right, dims):
    return lax.dot_general(left, right, (dims, ((), ())), preferred_element_type=F32)


def split_pair(column):
    high = column.astype(BF16)
    low = (column - high.astype(F32)).astype(BF16)
    shape = (column.shape[0], LANES // 2)
    return [jnp.broadcast_to(high, shape), jnp.broadcast_to(low, shape)]


def join_pair(lanes):
    lanes = lanes.astype(F32)
    return lanes[:, :1] + lanes[:, -1:]


def body(n_node, n_local, tokens, cotangent, gain, up_q, up_scale, down_q, down_scale):
    rows, cols = tokens.shape
    part = rows // CHUNKS
    hidden_units = up_q.shape[1]
    halves = n_node // n_local
    chips = n_local
    features = cols * n_node
    z = lax.axis_index("local")
    node = lax.axis_index("node")
    chip, core = node // halves, node % halves
    last = n_local - 1

    swap = [
        ((halves * c + j) * n_local + l, (halves * l + j) * n_local + c)
        for c in range(n_local)
        for j in range(halves)
        for l in range(n_local)
    ]

    def exchange(block):
        return lax.ppermute(block, ("node", "local"), swap)

    def core_swap(block):
        return lax.ppermute(block, "node", [(n, n ^ 1) for n in range(n_node)])

    def chip_swap(block, shift):
        return lax.ppermute(block, "node", [(n, n ^ (2 * shift)) for n in range(n_node)])

    even = z % 2 == 0

    def pair_swap(block, low):
        pairs = [(s, s + 1) for s in range(low, last, 2)]
        return lax.ppermute(block, "local", pairs + [(t, s) for s, t in pairs])

    def after(value, *others):
        return lax.optimization_barrier((value,) + others)[0]

    def take(array, index):
        width = array.shape[1]
        array = array.reshape(-1, n_local, part, width)
        return lax.dynamic_slice_in_dim(array, index, 1, 1).reshape(-1, width)

    def put(array, block, index):
        width = array.shape[1]
        stacked = array.reshape(-1, n_local, part, width)
        block = block.reshape(-1, 1, part, width)
        return lax.dynamic_update_slice_in_dim(stacked, block, index, 1).reshape(array.shape)

    def order(own, other):
        return jnp.where(
            core == 0,
            jnp.concatenate([own, other], axis=1),
            jnp.concatenate([other, own], axis=1),
        )

    def gather_chips(block):
        mine = jnp.zeros((block.shape[0] * chips, block.shape[1]), block.dtype)
        mine = put(mine, block, chip)
        for shift in range(1, chips):
            mine = put(mine, chip_swap(block, shift), chip ^ shift)
        return mine

    def gather_core(mine):
        return order(mine, core_swap(mine))

    def gather_node(block):
        return gather_core(gather_chips(block))

    def gather_call(block):
        parts = lax.all_gather(block, "node", axis=0, tiled=False)
        parts = parts.reshape(chips, halves, CHUNKS, part, cols).transpose(2, 0, 3, 1, 4)
        return parts.reshape(rows * chips, halves * cols)

    def scatter_core(partial, tail=()):
        first, second = partial[:, :cols], partial[:, cols:]
        keep = jnp.where(core == 0, first, second)
        send = jnp.where(core == 0, second, first)
        if tail:
            keep = jnp.concatenate([keep, *tail], axis=1)
            send = jnp.concatenate([send, *tail], axis=1)
        return (keep.astype(F32) + core_swap(send).astype(F32)).astype(BF16)

    def scatter_chips(both):
        total = take(both, chip).astype(F32)
        for shift in range(1, chips):
            total = total + chip_swap(take(both, chip ^ shift), shift).astype(F32)
        return total

    def scatter_node(partial):
        return scatter_chips(scatter_core(partial))

    def line(block, partial):
        first = second = None
        firsts, seconds = [], []
        if block is not None:
            first, second = pair_swap(block, 0), pair_swap(block, 1)
            firsts.append(first)
            seconds.append(second)
        for step in range(1, n_local if partial is not None else last):
            to_first, to_second = second, first
            if partial is not None:
                right = jnp.minimum(z + n_local - step, last)
                left = jnp.maximum(z - n_local + step, 0)
                to_first = take(partial, jnp.where(even, right, left))
                to_second = take(partial, jnp.where(even, left, right))
                if first is not None:
                    zero = jnp.zeros((), F32)
                    adds_right, adds_left = z < step, last - z < step
                    adds = jnp.where(even, adds_right, adds_left)
                    to_first = jnp.where(adds, to_first.astype(F32), zero)
                    to_first = (second.astype(F32) + to_first).astype(BF16)
                    adds = jnp.where(even, adds_left, adds_right)
                    to_second = jnp.where(adds, to_second.astype(F32), zero)
                    to_second = (first.astype(F32) + to_second).astype(BF16)
            first, second = pair_swap(to_first, 0), pair_swap(to_second, 1)
            firsts.append(first)
            seconds.append(second)
        total = None
        if partial is not None:
            total = take(partial, z).astype(F32) + first.astype(F32) + second.astype(F32)
        out = None
        if block is not None:
            out = jnp.zeros((part * n_local, block.shape[1]), block.dtype)
            out = put(out, block, z)
            for ahead in range(1, n_local):
                behind = n_local - ahead
                right = jnp.where(even, seconds[behind - 1], firsts[behind - 1])
                left = jnp.where(even, firsts[ahead - 1], seconds[ahead - 1])
                piece = jnp.where(z >= behind, right, left)
                out = put(out, piece, (z + ahead) % n_local)
        return out, total

    def widen(block):
        return jnp.pad(block, ((0, 0), (0, LANES)))

    def chunk_of(array, h):
        size = part * n_local
        return array[h * size : (h + 1) * size]

    def up_partial(values):
        widened = values.astype(F32)
        squares = jnp.sum((widened * widened).reshape(values.shape[0], -1, LANES), axis=1)
        product = dot((widened * gains).astype(BF16), up_weight, ((1,), (0,)))
        return jnp.concatenate([product.astype(BF16), squares.astype(BF16)], axis=1)

    def finish_pre(total):
        mean = jnp.sum(total[:, hidden_units:], axis=-1, keepdims=True) / features
        factor = lax.rsqrt(mean + epsilon)
        return total[:, :hidden_units] * factor, factor

    first = exchange(jnp.concatenate([tokens, jnp.pad(gain, ((0, PAD - 1), (0, 0)))], axis=0))
    g_home = exchange(cotangent)
    up_weight = dequant_rows(up_q, up_scale)
    down_weight = dequant_cols(down_q, down_scale)
    first, up_weight, down_weight = lax.optimization_barrier((first, up_weight, down_weight))
    x_home, gain_rows = first[:rows], first[rows:]
    gains = order(gain_rows, core_swap(gain_rows))[:1].astype(F32)
    gains_home = gain_rows[:1].astype(F32)

    halves_of = range(CHUNKS)

    x = gather_core(after(gather_chips(x_home), g_home))
    partials = [up_partial(chunk_of(x, h)) for h in halves_of]
    g = gather_call(after(g_home, *partials))
    totals = [line(None, partial)[1] for partial in partials]
    slopes = [
        dot(chunk_of(g, h), down_weight, ((1,), (1,))).astype(BF16) for h in halves_of
    ]
    hiddens = []
    for h in halves_of:
        hidden = jax.nn.silu(finish_pre(totals[h])[0]).astype(BF16)
        hidden, total = line(hidden, slopes[h])
        hiddens.append(hidden)
        slopes[h] = total.astype(BF16)
    updates = [dot(hidden, down_weight, ((1,), (0,))).astype(BF16) for hidden in hiddens]
    update = scatter_node(jnp.concatenate(updates, axis=0))
    x1_home = (x_home.astype(F32) + update).astype(BF16)

    x = gather_node(x1_home)
    packed = []
    for h in halves_of:
        slope, total = line(widen(slopes[h]), up_partial(chunk_of(x, h)))
        slopes[h] = slope[:, :hidden_units]
        pre, factor = finish_pre(total)
        packed.append(
            line(jnp.concatenate([pre.astype(BF16)] + split_pair(factor), axis=1), None)[0]
        )

    hidden_second, updates = [], []
    for half in packed:
        pre = half[:, :hidden_units].astype(F32)
        hidden_second.append((pre * jax.nn.sigmoid(pre)).astype(BF16))
        updates.append(dot(hidden_second[-1], down_weight, ((1,), (0,))).astype(BF16))
    update = scatter_core(jnp.concatenate(updates, axis=0))
    backs, tails = [], []
    for h in halves_of:
        slope = slopes[h] if h == 0 else after(slopes[h], update)
        pre = packed[h][:, :hidden_units].astype(F32)
        sigma = jax.nn.sigmoid(pre)
        pre_grad = slope.astype(F32) * sigma * (1.0 + pre * (1.0 - sigma))
        inner = jnp.sum(pre_grad * pre, axis=-1, keepdims=True)
        tails.append(jnp.concatenate(split_pair(inner), axis=1))
        backs.append(dot(pre_grad.astype(BF16), up_weight, ((1,), (1,))).astype(BF16))
    both = scatter_core(jnp.concatenate(backs, axis=0), [jnp.concatenate(tails, axis=0)])
    x2_home = (x1_home.astype(F32) + scatter_chips(update)).astype(BF16)
    result = exchange(x2_home)
    total = scatter_chips(after(both, x2_home))
    lanes = [take(half[:, hidden_units:], chip) for half in packed]
    factor = join_pair(jnp.concatenate(lanes, axis=0))
    inner = join_pair(total[:, cols:]) / (features * factor)
    back = factor * (total[:, :cols] * gains_home) - x1_home.astype(F32) * (factor**3 * inner)
    grad_home = (g_home.astype(F32) + back).astype(BF16)
    grad_second = dot(jnp.concatenate(hidden_second, axis=0), g, ((0,), (0,))).astype(BF16)
    mine = gather_chips(after(grad_home, result))
    below = gather_core(after(mine, grad_second))
    grad_first = dot(jnp.concatenate(hiddens, axis=0), below, ((0,), (0,)))
    grad_down = (grad_first + grad_second.astype(F32)).astype(BF16)
    return (result, grad_down)


def solution(mesh):
    n_node, n_local = mesh.shape["node"], mesh.shape["local"]

    def per_device(*arrays):
        return body(n_node, n_local, *arrays)

    in_specs = (
        P("local", "node"),
        P("local", "node"),
        P(None, "node"),
        P("local", "node"),
        P("local", "node"),
        P("node", "local"),
        P("node", "local"),
    )
    out_specs = (P("local", "node"), P("node", "local"))
    return jax.shard_map(
        per_device, mesh=mesh, in_specs=in_specs, out_specs=out_specs, check_vma=False
    )
```

```python
import jax
import jax.numpy as jnp
from jax import lax
from jax.sharding import PartitionSpec as P

LANES = 128
PAD = 16
CHUNKS = 2
epsilon = 1e-05
F32 = jnp.float32
BF16 = jnp.bfloat16


def dequant_rows(quanta, scales):
    blocks = scales.shape[0]
    widened = quanta.astype(F32).reshape(blocks, quanta.shape[0] // blocks, quanta.shape[1])
    return (widened * scales.astype(F32)[:, None, :]).reshape(quanta.shape).astype(BF16)


def dequant_cols(quanta, scales):
    blocks = scales.shape[1]
    widened = quanta.astype(F32).reshape(quanta.shape[0], blocks, quanta.shape[1] // blocks)
    return (widened * scales.astype(F32)[:, :, None]).reshape(quanta.shape).astype(BF16)


def dot(left, right, dims):
    return lax.dot_general(left, right, (dims, ((), ())), preferred_element_type=F32)


def split_pair(column):
    high = column.astype(BF16)
    low = (column - high.astype(F32)).astype(BF16)
    shape = (column.shape[0], LANES // 2)
    return [jnp.broadcast_to(high, shape), jnp.broadcast_to(low, shape)]


def join_pair(lanes):
    lanes = lanes.astype(F32)
    return lanes[:, :1] + lanes[:, -1:]


def body(n_node, n_local, tokens, cotangent, gain, up_q, up_scale, down_q, down_scale):
    rows, cols = tokens.shape
    part = rows // CHUNKS
    hidden_units = up_q.shape[1]
    halves = n_node // n_local
    chips = n_local
    features = cols * n_node
    z = lax.axis_index("local")
    node = lax.axis_index("node")
    chip, core = node // halves, node % halves
    last = n_local - 1

    swap = [
        ((halves * c + j) * n_local + l, (halves * l + j) * n_local + c)
        for c in range(n_local)
        for j in range(halves)
        for l in range(n_local)
    ]

    def exchange(block):
        return lax.ppermute(block, ("node", "local"), swap)

    def core_swap(block):
        return lax.ppermute(block, "node", [(n, n ^ 1) for n in range(n_node)])

    def chip_swap(block, shift):
        return lax.ppermute(block, "node", [(n, n ^ (2 * shift)) for n in range(n_node)])

    even = z % 2 == 0

    def pair_swap(block, low):
        pairs = [(s, s + 1) for s in range(low, last, 2)]
        return lax.ppermute(block, "local", pairs + [(t, s) for s, t in pairs])

    def after(value, *others):
        return lax.optimization_barrier((value,) + others)[0]

    def take(array, index):
        width = array.shape[1]
        array = array.reshape(-1, n_local, part, width)
        return lax.dynamic_slice_in_dim(array, index, 1, 1).reshape(-1, width)

    def put(array, block, index):
        width = array.shape[1]
        stacked = array.reshape(-1, n_local, part, width)
        block = block.reshape(-1, 1, part, width)
        return lax.dynamic_update_slice_in_dim(stacked, block, index, 1).reshape(array.shape)

    def order(own, other):
        return jnp.where(
            core == 0,
            jnp.concatenate([own, other], axis=1),
            jnp.concatenate([other, own], axis=1),
        )

    def gather_chips(block):
        mine = jnp.zeros((block.shape[0] * chips, block.shape[1]), block.dtype)
        mine = put(mine, block, chip)
        for shift in range(1, chips):
            mine = put(mine, chip_swap(block, shift), chip ^ shift)
        return mine

    def gather_core(mine):
        return order(mine, core_swap(mine))

    def gather_node(block):
        return gather_core(gather_chips(block))

    def scatter_core(partial, tail=()):
        first, second = partial[:, :cols], partial[:, cols:]
        keep = jnp.where(core == 0, first, second)
        send = jnp.where(core == 0, second, first)
        if tail:
            keep = jnp.concatenate([keep, *tail], axis=1)
            send = jnp.concatenate([send, *tail], axis=1)
        return (keep.astype(F32) + core_swap(send).astype(F32)).astype(BF16)

    def swap_chips(both):
        return [chip_swap(take(both, chip ^ shift), shift) for shift in range(1, chips)]

    def scatter_chips(both):
        return sum_chips(both, swap_chips(both))

    def sum_chips(both, others):
        total = take(both, chip).astype(F32)
        for other in others:
            total = total + other.astype(F32)
        return total

    def scatter_node(partial):
        return scatter_chips(scatter_core(partial))

    def line(block, partial):
        first = second = None
        firsts, seconds = [], []
        if block is not None:
            first, second = pair_swap(block, 0), pair_swap(block, 1)
            firsts.append(first)
            seconds.append(second)
        for step in range(1, n_local if partial is not None else last):
            to_first, to_second = second, first
            if partial is not None:
                right = jnp.minimum(z + n_local - step, last)
                left = jnp.maximum(z - n_local + step, 0)
                to_first = take(partial, jnp.where(even, right, left))
                to_second = take(partial, jnp.where(even, left, right))
                if first is not None:
                    zero = jnp.zeros((), F32)
                    adds_right, adds_left = z < step, last - z < step
                    adds = jnp.where(even, adds_right, adds_left)
                    to_first = jnp.where(adds, to_first.astype(F32), zero)
                    to_first = (second.astype(F32) + to_first).astype(BF16)
                    adds = jnp.where(even, adds_left, adds_right)
                    to_second = jnp.where(adds, to_second.astype(F32), zero)
                    to_second = (first.astype(F32) + to_second).astype(BF16)
            first, second = pair_swap(to_first, 0), pair_swap(to_second, 1)
            firsts.append(first)
            seconds.append(second)
        total = None
        if partial is not None:
            total = take(partial, z).astype(F32) + first.astype(F32) + second.astype(F32)
        out = None
        if block is not None:
            out = jnp.zeros((part * n_local, block.shape[1]), block.dtype)
            out = put(out, block, z)
            for ahead in range(1, n_local):
                behind = n_local - ahead
                right = jnp.where(even, seconds[behind - 1], firsts[behind - 1])
                left = jnp.where(even, firsts[ahead - 1], seconds[ahead - 1])
                piece = jnp.where(z >= behind, right, left)
                out = put(out, piece, (z + ahead) % n_local)
        return out, total

    def widen(block):
        return jnp.pad(block, ((0, 0), (0, LANES)))

    def chunk_of(array, h):
        size = part * n_local
        return array[h * size : (h + 1) * size]

    def up_partial(values):
        widened = values.astype(F32)
        squares = jnp.sum((widened * widened).reshape(values.shape[0], -1, LANES), axis=1)
        product = dot((widened * gains).astype(BF16), up_weight, ((1,), (0,)))
        return jnp.concatenate([product.astype(BF16), squares.astype(BF16)], axis=1)

    def finish_pre(total):
        mean = jnp.sum(total[:, hidden_units:], axis=-1, keepdims=True) / features
        factor = lax.rsqrt(mean + epsilon)
        return total[:, :hidden_units] * factor, factor

    first = exchange(jnp.concatenate([tokens, jnp.pad(gain, ((0, PAD - 1), (0, 0)))], axis=0))
    g_home = exchange(cotangent)
    up_weight = dequant_rows(up_q, up_scale)
    down_weight = dequant_cols(down_q, down_scale)
    first, up_weight, down_weight = lax.optimization_barrier((first, up_weight, down_weight))
    x_home, gain_rows = first[:rows], first[rows:]
    gains = order(gain_rows, core_swap(gain_rows))[:1].astype(F32)
    gains_home = gain_rows[:1].astype(F32)

    halves_of = range(CHUNKS)

    x = gather_core(after(gather_chips(x_home), g_home))
    partials = [up_partial(chunk_of(x, h)) for h in halves_of]
    totals = [line(None, partial)[1] for partial in partials]
    g = gather_node(after(g_home, *partials))
    slopes = [
        dot(chunk_of(g, h), down_weight, ((1,), (1,))).astype(BF16) for h in halves_of
    ]
    hiddens = []
    for h in halves_of:
        hidden = jax.nn.silu(finish_pre(totals[h])[0]).astype(BF16)
        hidden, total = line(hidden, slopes[h])
        hiddens.append(hidden)
        slopes[h] = total.astype(BF16)
    updates = [dot(hidden, down_weight, ((1,), (0,))).astype(BF16) for hidden in hiddens]
    update = scatter_node(jnp.concatenate(updates, axis=0))
    x1_home = (x_home.astype(F32) + update).astype(BF16)

    x = gather_node(x1_home)
    packed = []
    for h in halves_of:
        slope, total = line(widen(slopes[h]), up_partial(chunk_of(x, h)))
        slopes[h] = slope[:, :hidden_units]
        pre, factor = finish_pre(total)
        packed.append(
            line(jnp.concatenate([pre.astype(BF16)] + split_pair(factor), axis=1), None)[0]
        )

    hidden_second, updates = [], []
    for half in packed:
        pre = half[:, :hidden_units].astype(F32)
        hidden_second.append((pre * jax.nn.sigmoid(pre)).astype(BF16))
        updates.append(dot(hidden_second[-1], down_weight, ((1,), (0,))).astype(BF16))
    update = scatter_core(jnp.concatenate(updates, axis=0))
    backs, tails = [], []
    for h in halves_of:
        slope = slopes[h] if h == 0 else after(slopes[h], update)
        pre = packed[h][:, :hidden_units].astype(F32)
        sigma = jax.nn.sigmoid(pre)
        pre_grad = slope.astype(F32) * sigma * (1.0 + pre * (1.0 - sigma))
        inner = jnp.sum(pre_grad * pre, axis=-1, keepdims=True)
        tails.append(jnp.concatenate(split_pair(inner), axis=1))
        backs.append(dot(pre_grad.astype(BF16), up_weight, ((1,), (1,))).astype(BF16))
    both = scatter_core(jnp.concatenate(backs, axis=0), [jnp.concatenate(tails, axis=0)])
    others = swap_chips(update)
    x2_home = (x1_home.astype(F32) + sum_chips(update, others)).astype(BF16)
    result = exchange(x2_home)
    total = scatter_chips(after(both, x2_home))
    lanes = [take(half[:, hidden_units:], chip) for half in packed]
    factor = join_pair(jnp.concatenate(lanes, axis=0))
    inner = join_pair(total[:, cols:]) / (features * factor)
    back = factor * (total[:, :cols] * gains_home) - x1_home.astype(F32) * (factor**3 * inner)
    grad_home = (g_home.astype(F32) + back).astype(BF16)
    below = gather_node(after(grad_home, result))
    grad_down = dot(
        jnp.concatenate(hiddens + hidden_second, axis=0),
        jnp.concatenate([below, g], axis=0),
        ((0,), (0,)),
    ).astype(BF16)
    return (result, grad_down)


def solution(mesh):
    n_node, n_local = mesh.shape["node"], mesh.shape["local"]

    def per_device(*arrays):
        return body(n_node, n_local, *arrays)

    in_specs = (
        P("local", "node"),
        P("local", "node"),
        P(None, "node"),
        P("local", "node"),
        P("local", "node"),
        P("node", "local"),
        P("node", "local"),
    )
    out_specs = (P("local", "node"), P("node", "local"))
    return jax.shard_map(
        per_device, mesh=mesh, in_specs=in_specs, out_specs=out_specs, check_vma=False
    )
```

```python
import jax
import jax.numpy as jnp
from jax import lax
from jax.sharding import PartitionSpec as P

LANES = 128
PAD = 16
CHUNKS = 2
epsilon = 1e-05
F32 = jnp.float32
BF16 = jnp.bfloat16


def dequant_rows(quanta, scales):
    blocks = scales.shape[0]
    widened = quanta.astype(F32).reshape(blocks, quanta.shape[0] // blocks, quanta.shape[1])
    return (widened * scales.astype(F32)[:, None, :]).reshape(quanta.shape).astype(BF16)


def dequant_cols(quanta, scales):
    blocks = scales.shape[1]
    widened = quanta.astype(F32).reshape(quanta.shape[0], blocks, quanta.shape[1] // blocks)
    return (widened * scales.astype(F32)[:, :, None]).reshape(quanta.shape).astype(BF16)


def dot(left, right, dims):
    return lax.dot_general(left, right, (dims, ((), ())), preferred_element_type=F32)


def split_pair(column):
    high = column.astype(BF16)
    low = (column - high.astype(F32)).astype(BF16)
    shape = (column.shape[0], LANES // 2)
    return [jnp.broadcast_to(high, shape), jnp.broadcast_to(low, shape)]


def join_pair(lanes):
    lanes = lanes.astype(F32)
    return lanes[:, :1] + lanes[:, -1:]


def body(n_node, n_local, tokens, cotangent, gain, up_q, up_scale, down_q, down_scale):
    rows, cols = tokens.shape
    part = rows // CHUNKS
    hidden_units = up_q.shape[1]
    halves = n_node // n_local
    chips = n_local
    features = cols * n_node
    z = lax.axis_index("local")
    node = lax.axis_index("node")
    chip, core = node // halves, node % halves
    last = n_local - 1

    swap = [
        ((halves * c + j) * n_local + l, (halves * l + j) * n_local + c)
        for c in range(n_local)
        for j in range(halves)
        for l in range(n_local)
    ]

    def exchange(block):
        return lax.ppermute(block, ("node", "local"), swap)

    def core_swap(block):
        return lax.ppermute(block, "node", [(n, n ^ 1) for n in range(n_node)])

    def chip_swap(block, shift):
        return lax.ppermute(block, "node", [(n, n ^ (2 * shift)) for n in range(n_node)])

    even = z % 2 == 0

    def pair_swap(block, low, used=None):
        pairs = [(s, s + 1) for s in range(low, last, 2) if used is None or used(s)]
        if not pairs:
            return jnp.zeros_like(block)
        return lax.ppermute(block, "local", pairs + [(t, s) for s, t in pairs])

    def after(value, *others):
        return lax.optimization_barrier((value,) + others)[0]

    def take(array, index):
        width = array.shape[1]
        array = array.reshape(-1, n_local, part, width)
        return lax.dynamic_slice_in_dim(array, index, 1, 1).reshape(-1, width)

    def put(array, block, index):
        width = array.shape[1]
        stacked = array.reshape(-1, n_local, part, width)
        block = block.reshape(-1, 1, part, width)
        return lax.dynamic_update_slice_in_dim(stacked, block, index, 1).reshape(array.shape)

    def order(own, other):
        return jnp.where(
            core == 0,
            jnp.concatenate([own, other], axis=1),
            jnp.concatenate([other, own], axis=1),
        )

    def gather_chips(block):
        mine = jnp.zeros((block.shape[0] * chips, block.shape[1]), block.dtype)
        mine = put(mine, block, chip)
        for shift in range(1, chips):
            mine = put(mine, chip_swap(block, shift), chip ^ shift)
        return mine

    def gather_core(mine):
        return order(mine, core_swap(mine))

    def gather_node(block):
        return gather_core(gather_chips(block))

    def scatter_core(partial, tail=()):
        first, second = partial[:, :cols], partial[:, cols:]
        keep = jnp.where(core == 0, first, second)
        send = jnp.where(core == 0, second, first)
        if tail:
            keep = jnp.concatenate([keep, *tail], axis=1)
            send = jnp.concatenate([send, *tail], axis=1)
        return (keep.astype(F32) + core_swap(send).astype(F32)).astype(BF16)

    def swap_chips(both):
        return [chip_swap(take(both, chip ^ shift), shift) for shift in range(1, chips)]

    def scatter_chips(both):
        return sum_chips(both, swap_chips(both))

    def sum_chips(both, others):
        total = take(both, chip).astype(F32)
        for other in others:
            total = total + other.astype(F32)
        return total

    def scatter_node(partial):
        return scatter_chips(scatter_core(partial))

    def line(block, partial):
        first = second = None
        firsts, seconds = [], []
        if block is not None:
            first, second = pair_swap(block, 0), pair_swap(block, 1)
            firsts.append(first)
            seconds.append(second)
        for step in range(1, n_local if partial is not None else last):
            to_first, to_second = second, first
            if partial is not None:
                right = jnp.minimum(z + n_local - step, last)
                left = jnp.maximum(z - n_local + step, 0)
                to_first = take(partial, jnp.where(even, right, left))
                to_second = take(partial, jnp.where(even, left, right))
                if first is not None:
                    zero = jnp.zeros((), F32)
                    adds_right, adds_left = z < step, last - z < step
                    adds = jnp.where(even, adds_right, adds_left)
                    to_first = jnp.where(adds, to_first.astype(F32), zero)
                    to_first = (second.astype(F32) + to_first).astype(BF16)
                    adds = jnp.where(even, adds_left, adds_right)
                    to_second = jnp.where(adds, to_second.astype(F32), zero)
                    to_second = (first.astype(F32) + to_second).astype(BF16)
            used = None
            if block is None:
                used = lambda s, step=step: s < step or s + 1 > last - step
            elif partial is None:
                used = lambda s, step=step: s >= step or s + 1 <= last - step
            first, second = pair_swap(to_first, 0, used), pair_swap(to_second, 1, used)
            firsts.append(first)
            seconds.append(second)
        total = None
        if partial is not None:
            total = take(partial, z).astype(F32) + first.astype(F32) + second.astype(F32)
        out = None
        if block is not None:
            out = jnp.zeros((part * n_local, block.shape[1]), block.dtype)
            out = put(out, block, z)
            for ahead in range(1, n_local):
                behind = n_local - ahead
                right = jnp.where(even, seconds[behind - 1], firsts[behind - 1])
                left = jnp.where(even, firsts[ahead - 1], seconds[ahead - 1])
                piece = jnp.where(z >= behind, right, left)
                out = put(out, piece, (z + ahead) % n_local)
        return out, total

    def widen(block):
        return jnp.pad(block, ((0, 0), (0, LANES)))

    def chunk_of(array, h):
        size = part * n_local
        return array[h * size : (h + 1) * size]

    def up_partial(values):
        widened = values.astype(F32)
        squares = jnp.sum((widened * widened).reshape(values.shape[0], -1, LANES), axis=1)
        product = dot((widened * gains).astype(BF16), up_weight, ((1,), (0,)))
        return jnp.concatenate([product.astype(BF16), squares.astype(BF16)], axis=1)

    def finish_pre(total):
        mean = jnp.sum(total[:, hidden_units:], axis=-1, keepdims=True) / features
        factor = lax.rsqrt(mean + epsilon)
        return total[:, :hidden_units] * factor, factor

    x_home = exchange(tokens)
    other = exchange(jnp.concatenate([cotangent, jnp.pad(gain, ((0, PAD - 1), (0, 0)))], axis=0))
    g_home, gain_rows = other[:rows], other[rows:]
    up_weight = dequant_rows(up_q, up_scale)
    down_weight = dequant_cols(down_q, down_scale)
    x_home, up_weight, down_weight = lax.optimization_barrier((x_home, up_weight, down_weight))
    gains = order(gain_rows, core_swap(gain_rows))[:1].astype(F32)
    gains_home = gain_rows[:1].astype(F32)

    halves_of = range(CHUNKS)

    x = gather_core(after(gather_chips(x_home), g_home))
    partials = [up_partial(chunk_of(x, h)) for h in halves_of]
    totals = [line(None, partial)[1] for partial in partials]
    g = gather_node(after(g_home, *partials))
    slopes = [
        dot(chunk_of(g, h), down_weight, ((1,), (1,))).astype(BF16) for h in halves_of
    ]
    hiddens = []
    for h in halves_of:
        hidden = jax.nn.silu(finish_pre(totals[h])[0]).astype(BF16)
        hidden, total = line(hidden, slopes[h])
        hiddens.append(hidden)
        slopes[h] = total.astype(BF16)
    updates = [dot(hidden, down_weight, ((1,), (0,))).astype(BF16) for hidden in hiddens]
    update = scatter_node(jnp.concatenate(updates, axis=0))
    x1_home = (x_home.astype(F32) + update).astype(BF16)

    x = gather_node(x1_home)
    packed = []
    for h in halves_of:
        slope, total = line(widen(slopes[h]), up_partial(chunk_of(x, h)))
        slopes[h] = slope[:, :hidden_units]
        pre, factor = finish_pre(total)
        packed.append(
            line(jnp.concatenate([pre.astype(BF16)] + split_pair(factor), axis=1), None)[0]
        )

    hidden_second, updates, backs, tails = [], [], [], []

    def hidden_of(half):
        pre = half[:, :hidden_units].astype(F32)
        hidden_second.append((pre * jax.nn.sigmoid(pre)).astype(BF16))
        updates.append(dot(hidden_second[-1], down_weight, ((1,), (0,))).astype(BF16))

    def back_of(half, slope):
        pre = half[:, :hidden_units].astype(F32)
        sigma = jax.nn.sigmoid(pre)
        pre_grad = slope.astype(F32) * sigma * (1.0 + pre * (1.0 - sigma))
        inner = jnp.sum(pre_grad * pre, axis=-1, keepdims=True)
        tails.append(jnp.concatenate(split_pair(inner), axis=1))
        backs.append(dot(pre_grad.astype(BF16), up_weight, ((1,), (1,))).astype(BF16))

    hidden_of(packed[0])
    back_of(packed[0], slopes[0])
    packed[1] = after(packed[1], backs[0])
    hidden_of(packed[1])
    update = scatter_core(jnp.concatenate(updates, axis=0))
    back_of(packed[1], after(slopes[1], update))
    both = scatter_core(jnp.concatenate(backs, axis=0), [jnp.concatenate(tails, axis=0)])
    others = swap_chips(update)
    x2_home = (x1_home.astype(F32) + sum_chips(update, others)).astype(BF16)
    result = exchange(x2_home)
    total = scatter_chips(after(both, x2_home))
    lanes = [take(half[:, hidden_units:], chip) for half in packed]
    factor = join_pair(jnp.concatenate(lanes, axis=0))
    inner = join_pair(total[:, cols:]) / (features * factor)
    back = factor * (total[:, :cols] * gains_home) - x1_home.astype(F32) * (factor**3 * inner)
    grad_home = (g_home.astype(F32) + back).astype(BF16)
    below = gather_node(after(grad_home, result))
    grad_down = dot(
        jnp.concatenate(hiddens + hidden_second, axis=0),
        jnp.concatenate([below, g], axis=0),
        ((0,), (0,)),
    ).astype(BF16)
    return (result, grad_down)


def solution(mesh):
    n_node, n_local = mesh.shape["node"], mesh.shape["local"]

    def per_device(*arrays):
        return body(n_node, n_local, *arrays)

    in_specs = (
        P("local", "node"),
        P("local", "node"),
        P(None, "node"),
        P("local", "node"),
        P("local", "node"),
        P("node", "local"),
        P("node", "local"),
    )
    out_specs = (P("local", "node"), P("node", "local"))
    return jax.shard_map(
        per_device, mesh=mesh, in_specs=in_specs, out_specs=out_specs, check_vma=False
    )
```

```python
import jax
import jax.numpy as jnp
from jax import lax
from jax.experimental import pallas as pl
from jax.sharding import PartitionSpec as P

LANES = 128
PAD = 16
ROW_TILE = 256
CHUNKS = 2
epsilon = 1e-05
F32 = jnp.float32
BF16 = jnp.bfloat16


def dequant_rows(quanta, scales):
    blocks = scales.shape[0]
    widened = quanta.astype(F32).reshape(blocks, quanta.shape[0] // blocks, quanta.shape[1])
    return (widened * scales.astype(F32)[:, None, :]).reshape(quanta.shape).astype(BF16)


def scale_columns(quanta_ref, scales_ref, out_ref):
    blocks = scales_ref.shape[1]
    width = quanta_ref.shape[1] // blocks
    for block in range(blocks):
        columns = slice(block * width, (block + 1) * width)
        scale = scales_ref[:, block : block + 1].astype(F32)
        out_ref[:, columns] = (quanta_ref[:, columns].astype(F32) * scale).astype(BF16)


def dequant_cols(quanta, scales):
    rows, columns = quanta.shape
    tile = ROW_TILE if rows % ROW_TILE == 0 else rows
    return pl.pallas_call(
        scale_columns,
        grid=(rows // tile,),
        in_specs=[
            pl.BlockSpec((tile, columns), lambda i: (i, 0)),
            pl.BlockSpec((tile, scales.shape[1]), lambda i: (i, 0)),
        ],
        out_specs=pl.BlockSpec((tile, columns), lambda i: (i, 0)),
        out_shape=jax.ShapeDtypeStruct((rows, columns), BF16),
        cost_estimate=pl.CostEstimate(
            flops=rows * columns, bytes_accessed=4 * rows * columns, transcendentals=0
        ),
    )(quanta, scales)


def dot(left, right, dims):
    return lax.dot_general(left, right, (dims, ((), ())), preferred_element_type=F32)


def split_pair(column):
    high = column.astype(BF16)
    low = (column - high.astype(F32)).astype(BF16)
    shape = (column.shape[0], LANES // 2)
    return [jnp.broadcast_to(high, shape), jnp.broadcast_to(low, shape)]


def join_pair(lanes):
    lanes = lanes.astype(F32)
    return lanes[:, :1] + lanes[:, -1:]


def body(n_node, n_local, tokens, cotangent, gain, up_q, up_scale, down_q, down_scale):
    rows, cols = tokens.shape
    part = rows // CHUNKS
    hidden_units = up_q.shape[1]
    halves = n_node // n_local
    chips = n_local
    features = cols * n_node
    z = lax.axis_index("local")
    node = lax.axis_index("node")
    chip, core = node // halves, node % halves
    last = n_local - 1

    swap = [
        ((halves * c + j) * n_local + l, (halves * l + j) * n_local + c)
        for c in range(n_local)
        for j in range(halves)
        for l in range(n_local)
    ]

    def exchange(block):
        return lax.ppermute(block, ("node", "local"), swap)

    def core_swap(block):
        return lax.ppermute(block, "node", [(n, n ^ 1) for n in range(n_node)])

    def chip_swap(block, shift):
        return lax.ppermute(block, "node", [(n, n ^ (2 * shift)) for n in range(n_node)])

    even = z % 2 == 0

    def pair_swap(block, low, used=None):
        pairs = [(s, s + 1) for s in range(low, last, 2) if used is None or used(s)]
        if not pairs:
            return jnp.zeros_like(block)
        return lax.ppermute(block, "local", pairs + [(t, s) for s, t in pairs])

    def after(value, *others):
        return lax.optimization_barrier((value,) + others)[0]

    def take(array, index):
        width = array.shape[1]
        array = array.reshape(-1, n_local, part, width)
        return lax.dynamic_slice_in_dim(array, index, 1, 1).reshape(-1, width)

    def put(array, block, index):
        width = array.shape[1]
        stacked = array.reshape(-1, n_local, part, width)
        block = block.reshape(-1, 1, part, width)
        return lax.dynamic_update_slice_in_dim(stacked, block, index, 1).reshape(array.shape)

    def order(own, other):
        return jnp.where(
            core == 0,
            jnp.concatenate([own, other], axis=1),
            jnp.concatenate([other, own], axis=1),
        )

    def gather_chips(block):
        mine = jnp.zeros((block.shape[0] * chips, block.shape[1]), block.dtype)
        mine = put(mine, block, chip)
        for shift in range(1, chips):
            mine = put(mine, chip_swap(block, shift), chip ^ shift)
        return mine

    def gather_core(mine):
        return order(mine, core_swap(mine))

    def gather_node(block):
        return gather_core(gather_chips(block))

    def scatter_core(partial, tail=()):
        first, second = partial[:, :cols], partial[:, cols:]
        keep = jnp.where(core == 0, first, second)
        send = jnp.where(core == 0, second, first)
        if tail:
            keep = jnp.concatenate([keep, *tail], axis=1)
            send = jnp.concatenate([send, *tail], axis=1)
        return (keep.astype(F32) + core_swap(send).astype(F32)).astype(BF16)

    def swap_chips(both):
        return [chip_swap(take(both, chip ^ shift), shift) for shift in range(1, chips)]

    def scatter_chips(both):
        return sum_chips(both, swap_chips(both))

    def sum_chips(both, others):
        total = take(both, chip).astype(F32)
        for other in others:
            total = total + other.astype(F32)
        return total

    def scatter_node(partial):
        return scatter_chips(scatter_core(partial))

    def line(block, partial):
        first = second = None
        firsts, seconds = [], []
        if block is not None:
            first, second = pair_swap(block, 0), pair_swap(block, 1)
            firsts.append(first)
            seconds.append(second)
        for step in range(1, n_local if partial is not None else last):
            to_first, to_second = second, first
            if partial is not None:
                right = jnp.minimum(z + n_local - step, last)
                left = jnp.maximum(z - n_local + step, 0)
                to_first = take(partial, jnp.where(even, right, left))
                to_second = take(partial, jnp.where(even, left, right))
                if first is not None:
                    zero = jnp.zeros((), F32)
                    adds_right, adds_left = z < step, last - z < step
                    adds = jnp.where(even, adds_right, adds_left)
                    to_first = jnp.where(adds, to_first.astype(F32), zero)
                    to_first = (second.astype(F32) + to_first).astype(BF16)
                    adds = jnp.where(even, adds_left, adds_right)
                    to_second = jnp.where(adds, to_second.astype(F32), zero)
                    to_second = (first.astype(F32) + to_second).astype(BF16)
            used = None
            if block is None:
                used = lambda s, step=step: s < step or s + 1 > last - step
            elif partial is None:
                used = lambda s, step=step: s >= step or s + 1 <= last - step
            first, second = pair_swap(to_first, 0, used), pair_swap(to_second, 1, used)
            firsts.append(first)
            seconds.append(second)
        total = None
        if partial is not None:
            total = take(partial, z).astype(F32) + first.astype(F32) + second.astype(F32)
        out = None
        if block is not None:
            out = jnp.zeros((part * n_local, block.shape[1]), block.dtype)
            out = put(out, block, z)
            for ahead in range(1, n_local):
                behind = n_local - ahead
                right = jnp.where(even, seconds[behind - 1], firsts[behind - 1])
                left = jnp.where(even, firsts[ahead - 1], seconds[ahead - 1])
                piece = jnp.where(z >= behind, right, left)
                out = put(out, piece, (z + ahead) % n_local)
        return out, total

    def widen(block):
        return jnp.pad(block, ((0, 0), (0, LANES)))

    def chunk_of(array, h):
        size = part * n_local
        return array[h * size : (h + 1) * size]

    def up_partial(values):
        widened = values.astype(F32)
        squares = 0.0
        for start in range(0, values.shape[1], LANES):
            lanes = widened[:, start : start + LANES]
            squares = squares + lanes * lanes
        product = dot((widened * gains).astype(BF16), up_weight, ((1,), (0,)))
        return jnp.concatenate([product.astype(BF16), squares.astype(BF16)], axis=1)

    def finish_pre(total):
        mean = jnp.sum(total[:, hidden_units:], axis=-1, keepdims=True) / features
        factor = lax.rsqrt(mean + epsilon)
        return total[:, :hidden_units] * factor, factor

    x_home = exchange(tokens)
    other = exchange(jnp.concatenate([cotangent, jnp.pad(gain, ((0, PAD - 1), (0, 0)))], axis=0))
    g_home, gain_rows = other[:rows], other[rows:]
    down_weight = dequant_cols(down_q, down_scale)
    x_home = after(x_home, down_weight)
    up_weight = dequant_rows(after(up_q, x_home), up_scale)
    gains = order(gain_rows, core_swap(gain_rows))[:1].astype(F32)
    gains_home = gain_rows[:1].astype(F32)

    halves_of = range(CHUNKS)

    x = gather_core(after(gather_chips(x_home), g_home))
    partials = [up_partial(chunk_of(x, h)) for h in halves_of]
    totals = [line(None, partial)[1] for partial in partials]
    g = gather_node(after(g_home, *partials))
    slopes = [
        dot(chunk_of(g, h), down_weight, ((1,), (1,))).astype(BF16) for h in halves_of
    ]
    hiddens = []
    for h in halves_of:
        hidden = jax.nn.silu(finish_pre(totals[h])[0]).astype(BF16)
        hidden, total = line(hidden, slopes[h])
        hiddens.append(hidden)
        slopes[h] = total.astype(BF16)
    updates = [dot(hidden, down_weight, ((1,), (0,))).astype(BF16) for hidden in hiddens]
    update = scatter_node(jnp.concatenate(updates, axis=0))
    x1_home = (x_home.astype(F32) + update).astype(BF16)

    x = gather_node(x1_home)
    packed = []
    for h in halves_of:
        slope, total = line(widen(slopes[h]), up_partial(chunk_of(x, h)))
        slopes[h] = slope[:, :hidden_units]
        pre, factor = finish_pre(total)
        packed.append(
            line(jnp.concatenate([pre.astype(BF16)] + split_pair(factor), axis=1), None)[0]
        )

    hidden_second, updates, backs, tails = [], [], [], []

    def hidden_of(half):
        pre = half[:, :hidden_units].astype(F32)
        hidden_second.append((pre * jax.nn.sigmoid(pre)).astype(BF16))
        updates.append(dot(hidden_second[-1], down_weight, ((1,), (0,))).astype(BF16))

    def back_of(half, slope):
        pre = half[:, :hidden_units].astype(F32)
        sigma = jax.nn.sigmoid(pre)
        pre_grad = slope.astype(F32) * sigma * (1.0 + pre * (1.0 - sigma))
        inner = jnp.sum(pre_grad * pre, axis=-1, keepdims=True)
        tails.append(jnp.concatenate(split_pair(inner), axis=1))
        backs.append(dot(pre_grad.astype(BF16), up_weight, ((1,), (1,))).astype(BF16))

    hidden_of(packed[0])
    back_of(packed[0], slopes[0])
    packed[1] = after(packed[1], backs[0])
    hidden_of(packed[1])
    update = scatter_core(jnp.concatenate(updates, axis=0))
    back_of(packed[1], after(slopes[1], update))
    both = scatter_core(jnp.concatenate(backs, axis=0), [jnp.concatenate(tails, axis=0)])
    others = swap_chips(update)
    x2_home = (x1_home.astype(F32) + sum_chips(update, others)).astype(BF16)
    result = exchange(x2_home)
    total = scatter_chips(after(both, x2_home))
    lanes = [take(half[:, hidden_units:], chip) for half in packed]
    factor = join_pair(jnp.concatenate(lanes, axis=0))
    inner = join_pair(total[:, cols:]) / (features * factor)
    back = factor * (total[:, :cols] * gains_home) - x1_home.astype(F32) * (factor**3 * inner)
    grad_home = (g_home.astype(F32) + back).astype(BF16)
    below = gather_node(after(grad_home, result))
    grad_down = dot(
        jnp.concatenate(hiddens + hidden_second, axis=0),
        jnp.concatenate([below, g], axis=0),
        ((0,), (0,)),
    ).astype(BF16)
    return (result, grad_down)


def solution(mesh):
    n_node, n_local = mesh.shape["node"], mesh.shape["local"]

    def per_device(*arrays):
        return body(n_node, n_local, *arrays)

    in_specs = (
        P("local", "node"),
        P("local", "node"),
        P(None, "node"),
        P("local", "node"),
        P("local", "node"),
        P("node", "local"),
        P("node", "local"),
    )
    out_specs = (P("local", "node"), P("node", "local"))
    return jax.shard_map(
        per_device, mesh=mesh, in_specs=in_specs, out_specs=out_specs, check_vma=False
    )
```

```python
import jax
import jax.numpy as jnp
from jax import lax
from jax.experimental import pallas as pl
from jax.sharding import PartitionSpec as P

LANES = 128
PAD = 16
ROW_TILE = 256
CHUNKS = 2
epsilon = 1e-05
F32 = jnp.float32
BF16 = jnp.bfloat16


def dequant_rows(quanta, scales):
    blocks = scales.shape[0]
    widened = quanta.astype(F32).reshape(blocks, quanta.shape[0] // blocks, quanta.shape[1])
    return (widened * scales.astype(F32)[:, None, :]).reshape(quanta.shape).astype(BF16)


def scale_columns(quanta_ref, scales_ref, out_ref):
    blocks = scales_ref.shape[1]
    width = quanta_ref.shape[1] // blocks
    for block in range(blocks):
        columns = slice(block * width, (block + 1) * width)
        scale = scales_ref[:, block : block + 1].astype(F32)
        out_ref[:, columns] = (quanta_ref[:, columns].astype(F32) * scale).astype(BF16)


def dequant_cols(quanta, scales):
    rows, columns = quanta.shape
    tile = ROW_TILE if rows % ROW_TILE == 0 else rows
    return pl.pallas_call(
        scale_columns,
        grid=(rows // tile,),
        in_specs=[
            pl.BlockSpec((tile, columns), lambda i: (i, 0)),
            pl.BlockSpec((tile, scales.shape[1]), lambda i: (i, 0)),
        ],
        out_specs=pl.BlockSpec((tile, columns), lambda i: (i, 0)),
        out_shape=jax.ShapeDtypeStruct((rows, columns), BF16),
        cost_estimate=pl.CostEstimate(
            flops=rows * columns, bytes_accessed=4 * rows * columns, transcendentals=0
        ),
    )(quanta, scales)


def dot(left, right, dims):
    return lax.dot_general(left, right, (dims, ((), ())), preferred_element_type=F32)


def split_pair(column):
    high = column.astype(BF16)
    low = (column - high.astype(F32)).astype(BF16)
    shape = (column.shape[0], LANES // 2)
    return [jnp.broadcast_to(high, shape), jnp.broadcast_to(low, shape)]


def join_pair(lanes):
    lanes = lanes.astype(F32)
    return lanes[:, :1] + lanes[:, -1:]


def body(n_node, n_local, tokens, cotangent, gain, up_q, up_scale, down_q, down_scale):
    rows, cols = tokens.shape
    part = rows // CHUNKS
    hidden_units = up_q.shape[1]
    halves = n_node // n_local
    chips = n_local
    features = cols * n_node
    z = lax.axis_index("local")
    node = lax.axis_index("node")
    chip, core = node // halves, node % halves
    last = n_local - 1

    swap = [
        ((halves * c + j) * n_local + l, (halves * l + j) * n_local + c)
        for c in range(n_local)
        for j in range(halves)
        for l in range(n_local)
    ]

    def exchange(block):
        return lax.ppermute(block, ("node", "local"), swap)

    def core_swap(block):
        return lax.ppermute(block, "node", [(n, n ^ 1) for n in range(n_node)])

    def chip_swap(block, shift):
        return lax.ppermute(block, "node", [(n, n ^ (2 * shift)) for n in range(n_node)])

    even = z % 2 == 0

    def pair_swap(block, low, used=None):
        pairs = [(s, s + 1) for s in range(low, last, 2) if used is None or used(s)]
        if not pairs:
            return jnp.zeros_like(block)
        return lax.ppermute(block, "local", pairs + [(t, s) for s, t in pairs])

    def after(value, *others):
        return lax.optimization_barrier((value,) + others)[0]

    def take(array, index):
        width = array.shape[1]
        array = array.reshape(-1, n_local, part, width)
        return lax.dynamic_slice_in_dim(array, index, 1, 1).reshape(-1, width)

    def put(array, block, index):
        width = array.shape[1]
        stacked = array.reshape(-1, n_local, part, width)
        block = block.reshape(-1, 1, part, width)
        return lax.dynamic_update_slice_in_dim(stacked, block, index, 1).reshape(array.shape)

    def order(own, other):
        return jnp.where(
            core == 0,
            jnp.concatenate([own, other], axis=1),
            jnp.concatenate([other, own], axis=1),
        )

    def gather_chips(block):
        mine = jnp.zeros((block.shape[0] * chips, block.shape[1]), block.dtype)
        mine = put(mine, block, chip)
        for shift in range(1, chips):
            mine = put(mine, chip_swap(block, shift), chip ^ shift)
        return mine

    def gather_core(mine):
        return order(mine, core_swap(mine))

    def gather_node(block):
        return gather_core(gather_chips(block))

    def scatter_core(partial, tail=()):
        first, second = partial[:, :cols], partial[:, cols:]
        keep = jnp.where(core == 0, first, second)
        send = jnp.where(core == 0, second, first)
        if tail:
            keep = jnp.concatenate([keep, *tail], axis=1)
            send = jnp.concatenate([send, *tail], axis=1)
        return (keep.astype(F32) + core_swap(send).astype(F32)).astype(BF16)

    def swap_chips(both):
        return [chip_swap(take(both, chip ^ shift), shift) for shift in range(1, chips)]

    def scatter_chips(both):
        return sum_chips(both, swap_chips(both))

    def sum_chips(both, others):
        total = take(both, chip).astype(F32)
        for other in others:
            total = total + other.astype(F32)
        return total

    def scatter_node(partial):
        return scatter_chips(scatter_core(partial))

    def line(block, partial):
        first = second = None
        firsts, seconds = [], []
        if block is not None:
            first, second = pair_swap(block, 0), pair_swap(block, 1)
            firsts.append(first)
            seconds.append(second)
        for step in range(1, n_local if partial is not None else last):
            to_first, to_second = second, first
            if partial is not None:
                right = jnp.minimum(z + n_local - step, last)
                left = jnp.maximum(z - n_local + step, 0)
                to_first = take(partial, jnp.where(even, right, left))
                to_second = take(partial, jnp.where(even, left, right))
                if first is not None:
                    zero = jnp.zeros((), F32)
                    adds_right, adds_left = z < step, last - z < step
                    adds = jnp.where(even, adds_right, adds_left)
                    to_first = jnp.where(adds, to_first.astype(F32), zero)
                    to_first = (second.astype(F32) + to_first).astype(BF16)
                    adds = jnp.where(even, adds_left, adds_right)
                    to_second = jnp.where(adds, to_second.astype(F32), zero)
                    to_second = (first.astype(F32) + to_second).astype(BF16)
            if first is not None and step == (2 if block is None else last - 1 if partial is None else 0):
                to_first = after(to_first, first)
            used = None
            if block is None:
                used = lambda s, step=step: s < step or s + 1 > last - step
            elif partial is None:
                used = lambda s, step=step: s >= step or s + 1 <= last - step
            first, second = pair_swap(to_first, 0, used), pair_swap(to_second, 1, used)
            firsts.append(first)
            seconds.append(second)
        total = None
        if partial is not None:
            total = take(partial, z).astype(F32) + first.astype(F32) + second.astype(F32)
        out = None
        if block is not None:
            out = jnp.zeros((part * n_local, block.shape[1]), block.dtype)
            out = put(out, block, z)
            for ahead in range(1, n_local):
                behind = n_local - ahead
                right = jnp.where(even, seconds[behind - 1], firsts[behind - 1])
                left = jnp.where(even, firsts[ahead - 1], seconds[ahead - 1])
                piece = jnp.where(z >= behind, right, left)
                out = put(out, piece, (z + ahead) % n_local)
        return out, total

    def widen(block):
        return jnp.pad(block, ((0, 0), (0, LANES)))

    def chunk_of(array, h):
        size = part * n_local
        return array[h * size : (h + 1) * size]

    def up_partial(values):
        widened = values.astype(F32)
        squares = 0.0
        for start in range(0, values.shape[1], LANES):
            lanes = widened[:, start : start + LANES]
            squares = squares + lanes * lanes
        product = dot((widened * gains).astype(BF16), up_weight, ((1,), (0,)))
        return jnp.concatenate([product.astype(BF16), squares.astype(BF16)], axis=1)

    def finish_pre(total):
        mean = jnp.sum(total[:, hidden_units:], axis=-1, keepdims=True) / features
        factor = lax.rsqrt(mean + epsilon)
        return total[:, :hidden_units] * factor, factor

    x_home = exchange(tokens)
    other = exchange(jnp.concatenate([cotangent, jnp.pad(gain, ((0, PAD - 1), (0, 0)))], axis=0))
    g_home, gain_rows = other[:rows], other[rows:]
    down_weight = dequant_cols(down_q, down_scale)
    x_home = after(x_home, down_weight)
    up_weight = dequant_rows(after(up_q, x_home), up_scale)
    gains = order(gain_rows, core_swap(gain_rows))[:1].astype(F32)
    gains_home = gain_rows[:1].astype(F32)

    halves_of = range(CHUNKS)

    x = gather_core(after(gather_chips(x_home), g_home))
    partials = [up_partial(chunk_of(x, h)) for h in halves_of]
    totals = [line(None, partial)[1] for partial in partials]
    g = gather_node(after(g_home, *partials))
    slopes = [
        dot(chunk_of(g, h), down_weight, ((1,), (1,))).astype(BF16) for h in halves_of
    ]
    hiddens = []
    for h in halves_of:
        hidden = jax.nn.silu(finish_pre(totals[h])[0]).astype(BF16)
        hidden, total = line(hidden, slopes[h])
        hiddens.append(hidden)
        slopes[h] = total.astype(BF16)
    updates = [dot(hidden, down_weight, ((1,), (0,))).astype(BF16) for hidden in hiddens]
    update = scatter_node(jnp.concatenate(updates, axis=0))
    x1_home = (x_home.astype(F32) + update).astype(BF16)

    x = gather_node(x1_home)
    packed = []
    for h in halves_of:
        slope, total = line(widen(slopes[h]), up_partial(chunk_of(x, h)))
        slopes[h] = slope[:, :hidden_units]
        pre, factor = finish_pre(total)
        packed.append(
            line(jnp.concatenate([pre.astype(BF16)] + split_pair(factor), axis=1), None)[0]
        )

    hidden_second, updates, backs, tails = [], [], [], []

    def hidden_of(half):
        pre = half[:, :hidden_units].astype(F32)
        hidden_second.append((pre * jax.nn.sigmoid(pre)).astype(BF16))
        updates.append(dot(hidden_second[-1], down_weight, ((1,), (0,))).astype(BF16))

    def back_of(half, slope):
        pre = half[:, :hidden_units].astype(F32)
        sigma = jax.nn.sigmoid(pre)
        pre_grad = slope.astype(F32) * sigma * (1.0 + pre * (1.0 - sigma))
        inner = jnp.sum(pre_grad * pre, axis=-1, keepdims=True)
        tails.append(jnp.concatenate(split_pair(inner), axis=1))
        backs.append(dot(pre_grad.astype(BF16), up_weight, ((1,), (1,))).astype(BF16))

    hidden_of(packed[0])
    back_of(packed[0], slopes[0])
    packed[1] = after(packed[1], backs[0])
    hidden_of(packed[1])
    update = scatter_core(jnp.concatenate(updates, axis=0))
    back_of(packed[1], after(slopes[1], update))
    both = scatter_core(jnp.concatenate(backs, axis=0), [jnp.concatenate(tails, axis=0)])
    others = swap_chips(update)
    x2_home = (x1_home.astype(F32) + sum_chips(update, others)).astype(BF16)
    result = exchange(x2_home)
    total = scatter_chips(after(both, x2_home))
    lanes = [take(half[:, hidden_units:], chip) for half in packed]
    factor = join_pair(jnp.concatenate(lanes, axis=0))
    inner = join_pair(total[:, cols:]) / (features * factor)
    back = factor * (total[:, :cols] * gains_home) - x1_home.astype(F32) * (factor**3 * inner)
    grad_home = (g_home.astype(F32) + back).astype(BF16)
    below = gather_node(after(grad_home, result))
    grad_down = dot(
        jnp.concatenate(hiddens + hidden_second, axis=0),
        jnp.concatenate([below, g], axis=0),
        ((0,), (0,)),
    ).astype(BF16)
    return (result, grad_down)


def solution(mesh):
    n_node, n_local = mesh.shape["node"], mesh.shape["local"]

    def per_device(*arrays):
        return body(n_node, n_local, *arrays)

    in_specs = (
        P("local", "node"),
        P("local", "node"),
        P(None, "node"),
        P("local", "node"),
        P("local", "node"),
        P("node", "local"),
        P("node", "local"),
    )
    out_specs = (P("local", "node"), P("node", "local"))
    return jax.shard_map(
        per_device, mesh=mesh, in_specs=in_specs, out_specs=out_specs, check_vma=False
    )
```

```python
import jax
import jax.numpy as jnp
from jax import lax
from jax.experimental import pallas as pl
from jax.sharding import PartitionSpec as P

LANES = 128
PAD = 16
ROW_TILE = 256
CHUNKS = 2
epsilon = 1e-05
F32 = jnp.float32
BF16 = jnp.bfloat16


def dequant_rows(quanta, scales):
    blocks = scales.shape[0]
    widened = quanta.astype(F32).reshape(blocks, quanta.shape[0] // blocks, quanta.shape[1])
    return (widened * scales.astype(F32)[:, None, :]).reshape(quanta.shape).astype(BF16)


def scale_columns(quanta_ref, scales_ref, out_ref):
    blocks = scales_ref.shape[1]
    width = quanta_ref.shape[1] // blocks
    for block in range(blocks):
        columns = slice(block * width, (block + 1) * width)
        scale = scales_ref[:, block : block + 1].astype(F32)
        out_ref[:, columns] = (quanta_ref[:, columns].astype(F32) * scale).astype(BF16)


def dequant_cols(quanta, scales):
    rows, columns = quanta.shape
    tile = ROW_TILE if rows % ROW_TILE == 0 else rows
    return pl.pallas_call(
        scale_columns,
        grid=(rows // tile,),
        in_specs=[
            pl.BlockSpec((tile, columns), lambda i: (i, 0)),
            pl.BlockSpec((tile, scales.shape[1]), lambda i: (i, 0)),
        ],
        out_specs=pl.BlockSpec((tile, columns), lambda i: (i, 0)),
        out_shape=jax.ShapeDtypeStruct((rows, columns), BF16),
        cost_estimate=pl.CostEstimate(
            flops=rows * columns, bytes_accessed=4 * rows * columns, transcendentals=0
        ),
    )(quanta, scales)


def dot(left, right, dims):
    return lax.dot_general(left, right, (dims, ((), ())), preferred_element_type=F32)


def split_pair(column):
    high = column.astype(BF16)
    low = (column - high.astype(F32)).astype(BF16)
    shape = (column.shape[0], LANES // 2)
    return [jnp.broadcast_to(high, shape), jnp.broadcast_to(low, shape)]


def join_pair(lanes):
    lanes = lanes.astype(F32)
    return lanes[:, :1] + lanes[:, -1:]


def body(n_node, n_local, tokens, cotangent, gain, up_q, up_scale, down_q, down_scale):
    rows, cols = tokens.shape
    part = rows // CHUNKS
    hidden_units = up_q.shape[1]
    halves = n_node // n_local
    chips = n_local
    features = cols * n_node
    z = lax.axis_index("local")
    node = lax.axis_index("node")
    chip, core = node // halves, node % halves
    last = n_local - 1

    swap = [
        ((halves * c + j) * n_local + l, (halves * l + j) * n_local + c)
        for c in range(n_local)
        for j in range(halves)
        for l in range(n_local)
    ]

    def exchange(block):
        return lax.ppermute(block, ("node", "local"), swap)

    def core_swap(block):
        return lax.ppermute(block, "node", [(n, n ^ 1) for n in range(n_node)])

    def chip_swap(block, shift):
        return lax.ppermute(block, "node", [(n, n ^ (2 * shift)) for n in range(n_node)])

    even = z % 2 == 0

    def pair_swap(block, low, used=None):
        pairs = [(s, s + 1) for s in range(low, last, 2) if used is None or used(s)]
        if not pairs:
            return jnp.zeros_like(block)
        return lax.ppermute(block, "local", pairs + [(t, s) for s, t in pairs])

    def after(value, *others):
        return lax.optimization_barrier((value,) + others)[0]

    def take(array, index):
        width = array.shape[1]
        array = array.reshape(-1, n_local, part, width)
        return lax.dynamic_slice_in_dim(array, index, 1, 1).reshape(-1, width)

    def put(array, block, index):
        width = array.shape[1]
        stacked = array.reshape(-1, n_local, part, width)
        block = block.reshape(-1, 1, part, width)
        return lax.dynamic_update_slice_in_dim(stacked, block, index, 1).reshape(array.shape)

    def order(own, other):
        return jnp.where(
            core == 0,
            jnp.concatenate([own, other], axis=1),
            jnp.concatenate([other, own], axis=1),
        )

    def gather_chips(block):
        mine = jnp.zeros((block.shape[0] * chips, block.shape[1]), block.dtype)
        mine = put(mine, block, chip)
        for shift in range(1, chips):
            mine = put(mine, chip_swap(block, shift), chip ^ shift)
        return mine

    def gather_core(mine):
        return order(mine, core_swap(mine))

    def gather_node(block):
        return gather_core(gather_chips(block))

    def scatter_core(partial, tail=()):
        first, second = partial[:, :cols], partial[:, cols:]
        keep = jnp.where(core == 0, first, second)
        send = jnp.where(core == 0, second, first)
        if tail:
            keep = jnp.concatenate([keep, *tail], axis=1)
            send = jnp.concatenate([send, *tail], axis=1)
        return (keep.astype(F32) + core_swap(send).astype(F32)).astype(BF16)

    def swap_chips(both):
        return [chip_swap(take(both, chip ^ shift), shift) for shift in range(1, chips)]

    def scatter_chips(both):
        return sum_chips(both, swap_chips(both))

    def sum_chips(both, others):
        total = take(both, chip).astype(F32)
        for other in others:
            total = total + other.astype(F32)
        return total

    def scatter_node(partial):
        return scatter_chips(scatter_core(partial))

    def line(block, partial):
        first = second = None
        firsts, seconds = [], []
        if block is not None:
            first, second = pair_swap(block, 0), pair_swap(block, 1)
            firsts.append(first)
            seconds.append(second)
        for step in range(1, n_local if partial is not None else last):
            to_first, to_second = second, first
            if partial is not None:
                right = jnp.minimum(z + n_local - step, last)
                left = jnp.maximum(z - n_local + step, 0)
                to_first = take(partial, jnp.where(even, right, left))
                to_second = take(partial, jnp.where(even, left, right))
                if first is not None:
                    zero = jnp.zeros((), F32)
                    adds_right, adds_left = z < step, last - z < step
                    adds = jnp.where(even, adds_right, adds_left)
                    to_first = jnp.where(adds, to_first.astype(F32), zero)
                    to_first = (second.astype(F32) + to_first).astype(BF16)
                    adds = jnp.where(even, adds_left, adds_right)
                    to_second = jnp.where(adds, to_second.astype(F32), zero)
                    to_second = (first.astype(F32) + to_second).astype(BF16)
            if first is not None and step == (2 if block is None else last - 1 if partial is None else 0):
                to_first = after(to_first, first)
            used = None
            if block is None:
                used = lambda s, step=step: s < step or s + 1 > last - step
            elif partial is None:
                used = lambda s, step=step: s >= step or s + 1 <= last - step
            first, second = pair_swap(to_first, 0, used), pair_swap(to_second, 1, used)
            firsts.append(first)
            seconds.append(second)
        total = None
        if partial is not None:
            total = take(partial, z).astype(F32) + first.astype(F32) + second.astype(F32)
        out = None
        if block is not None:
            out = jnp.zeros((part * n_local, block.shape[1]), block.dtype)
            out = put(out, block, z)
            for ahead in range(1, n_local):
                behind = n_local - ahead
                right = jnp.where(even, seconds[behind - 1], firsts[behind - 1])
                left = jnp.where(even, firsts[ahead - 1], seconds[ahead - 1])
                piece = jnp.where(z >= behind, right, left)
                out = put(out, piece, (z + ahead) % n_local)
        return out, total

    def widen(block):
        return jnp.pad(block, ((0, 0), (0, LANES)))

    def chunk_of(array, h):
        size = part * n_local
        return array[h * size : (h + 1) * size]

    def up_partial(values):
        widened = values.astype(F32)
        squares = 0.0
        for start in range(0, values.shape[1], LANES):
            lanes = widened[:, start : start + LANES]
            squares = squares + lanes * lanes
        product = dot((widened * gains).astype(BF16), up_weight, ((1,), (0,)))
        return jnp.concatenate([product.astype(BF16), squares.astype(BF16)], axis=1)

    def finish_pre(total):
        mean = jnp.sum(total[:, hidden_units:], axis=-1, keepdims=True) / features
        factor = lax.rsqrt(mean + epsilon)
        return total[:, :hidden_units] * factor, factor

    x_home = exchange(tokens)
    other = exchange(jnp.concatenate([cotangent, jnp.pad(gain, ((0, PAD - 1), (0, 0)))], axis=0))
    g_home, gain_rows = other[:rows], other[rows:]
    down_weight = dequant_cols(down_q, down_scale)
    x_home = after(x_home, down_weight)
    up_weight = dequant_rows(after(up_q, x_home), up_scale)
    gains = order(gain_rows, core_swap(gain_rows))[:1].astype(F32)
    gains_home = gain_rows[:1].astype(F32)

    halves_of = range(CHUNKS)

    x_mine = after(gather_chips(x_home), g_home, up_weight)
    x = gather_core(x_mine)
    partials = [up_partial(chunk_of(x, h)) for h in halves_of]
    totals = [line(None, partial)[1] for partial in partials]
    g = gather_node(after(g_home, x_mine))
    slopes = [
        dot(chunk_of(g, h), down_weight, ((1,), (1,))).astype(BF16) for h in halves_of
    ]
    hiddens = []
    for h in halves_of:
        hidden = jax.nn.silu(finish_pre(totals[h])[0]).astype(BF16)
        hidden, total = line(hidden, slopes[h])
        hiddens.append(hidden)
        slopes[h] = total.astype(BF16)
    updates = [dot(hidden, down_weight, ((1,), (0,))).astype(BF16) for hidden in hiddens]
    update = scatter_node(jnp.concatenate(updates, axis=0))
    x1_home = (x_home.astype(F32) + update).astype(BF16)

    x = gather_node(x1_home)
    packed = []
    for h in halves_of:
        slope, total = line(widen(slopes[h]), up_partial(chunk_of(x, h)))
        slopes[h] = slope[:, :hidden_units]
        pre, factor = finish_pre(total)
        packed.append(
            line(jnp.concatenate([pre.astype(BF16)] + split_pair(factor), axis=1), None)[0]
        )

    hidden_second, updates, backs, tails = [], [], [], []

    def hidden_of(half):
        pre = half[:, :hidden_units].astype(F32)
        hidden_second.append((pre * jax.nn.sigmoid(pre)).astype(BF16))
        updates.append(dot(hidden_second[-1], down_weight, ((1,), (0,))).astype(BF16))

    def back_of(half, slope):
        pre = half[:, :hidden_units].astype(F32)
        sigma = jax.nn.sigmoid(pre)
        pre_grad = slope.astype(F32) * sigma * (1.0 + pre * (1.0 - sigma))
        inner = jnp.sum(pre_grad * pre, axis=-1, keepdims=True)
        tails.append(jnp.concatenate(split_pair(inner), axis=1))
        backs.append(dot(pre_grad.astype(BF16), up_weight, ((1,), (1,))).astype(BF16))

    hidden_of(packed[0])
    back_of(packed[0], slopes[0])
    packed[1] = after(packed[1], backs[0])
    hidden_of(packed[1])
    update = scatter_core(jnp.concatenate(updates, axis=0))
    back_of(packed[1], after(slopes[1], update))
    both = scatter_core(jnp.concatenate(backs, axis=0), [jnp.concatenate(tails, axis=0)])
    others = swap_chips(update)
    grad_second = dot(jnp.concatenate(hidden_second, axis=0), g, ((0,), (0,))).astype(BF16)
    others[-1] = after(others[-1], grad_second)
    x2_home = (x1_home.astype(F32) + sum_chips(update, others)).astype(BF16)
    result = exchange(x2_home)
    total = scatter_chips(after(both, x2_home))
    lanes = [take(half[:, hidden_units:], chip) for half in packed]
    factor = join_pair(jnp.concatenate(lanes, axis=0))
    inner = join_pair(total[:, cols:]) / (features * factor)
    back = factor * (total[:, :cols] * gains_home) - x1_home.astype(F32) * (factor**3 * inner)
    grad_home = (g_home.astype(F32) + back).astype(BF16)
    below = gather_node(after(grad_home, result))
    grad_first = dot(jnp.concatenate(hiddens, axis=0), below, ((0,), (0,)))
    grad_down = (grad_first + grad_second.astype(F32)).astype(BF16)
    return (result, grad_down)


def solution(mesh):
    n_node, n_local = mesh.shape["node"], mesh.shape["local"]

    def per_device(*arrays):
        return body(n_node, n_local, *arrays)

    in_specs = (
        P("local", "node"),
        P("local", "node"),
        P(None, "node"),
        P("local", "node"),
        P("local", "node"),
        P("node", "local"),
        P("node", "local"),
    )
    out_specs = (P("local", "node"), P("node", "local"))
    return jax.shard_map(
        per_device, mesh=mesh, in_specs=in_specs, out_specs=out_specs, check_vma=False
    )
```

```python
import jax
import jax.numpy as jnp
from jax import lax
from jax.experimental import pallas as pl
from jax.sharding import PartitionSpec as P

LANES = 128
PAD = 16
ROW_TILE = 256
CHUNKS = 2
epsilon = 1e-05
F32 = jnp.float32
BF16 = jnp.bfloat16


def scale_rows(quanta_ref, scales_ref, out_ref):
    out_ref[...] = (quanta_ref[...].astype(F32) * scales_ref[0]).astype(BF16)


def dequant_rows(quanta, scales):
    rows, columns = quanta.shape
    blocks = scales.shape[0]
    tile = rows // blocks
    return pl.pallas_call(
        scale_rows,
        grid=(blocks,),
        in_specs=[
            pl.BlockSpec((tile, columns), lambda i: (i, 0)),
            pl.BlockSpec((1, 1, columns), lambda i: (i, 0, 0)),
        ],
        out_specs=pl.BlockSpec((tile, columns), lambda i: (i, 0)),
        out_shape=jax.ShapeDtypeStruct((rows, columns), BF16),
        cost_estimate=pl.CostEstimate(
            flops=rows * columns, bytes_accessed=4 * rows * columns, transcendentals=0
        ),
    )(quanta, scales.astype(F32).reshape(blocks, 1, columns))


def scale_columns(quanta_ref, scales_ref, out_ref):
    blocks = scales_ref.shape[1]
    width = quanta_ref.shape[1] // blocks
    for block in range(blocks):
        columns = slice(block * width, (block + 1) * width)
        scale = scales_ref[:, block : block + 1].astype(F32)
        out_ref[:, columns] = (quanta_ref[:, columns].astype(F32) * scale).astype(BF16)


def scale_columns_across(quanta_ref, scales_ref, out_ref):
    blocks = scales_ref.shape[0]
    width = quanta_ref.shape[1] // blocks
    scales = scales_ref[...].astype(F32).T
    for block in range(blocks):
        columns = slice(block * width, (block + 1) * width)
        scale = scales[:, block : block + 1]
        out_ref[:, columns] = (quanta_ref[:, columns].astype(F32) * scale).astype(BF16)


def dequant_cols(quanta, scales):
    rows, columns = quanta.shape
    blocks = scales.shape[1]
    if rows % ROW_TILE == 0 and blocks % 8 == 0:
        tile, kernel, scales = ROW_TILE, scale_columns_across, scales.T
        scales_spec = pl.BlockSpec((blocks, tile), lambda i: (0, i))
    else:
        tile, kernel = rows, scale_columns
        scales_spec = pl.BlockSpec((tile, blocks), lambda i: (i, 0))
    return pl.pallas_call(
        kernel,
        grid=(rows // tile,),
        in_specs=[pl.BlockSpec((tile, columns), lambda i: (i, 0)), scales_spec],
        out_specs=pl.BlockSpec((tile, columns), lambda i: (i, 0)),
        out_shape=jax.ShapeDtypeStruct((rows, columns), BF16),
        cost_estimate=pl.CostEstimate(
            flops=rows * columns, bytes_accessed=4 * rows * columns, transcendentals=0
        ),
    )(quanta, scales)


def dot(left, right, dims):
    return lax.dot_general(left, right, (dims, ((), ())), preferred_element_type=F32)


def split_pair(column):
    high = column.astype(BF16)
    low = (column - high.astype(F32)).astype(BF16)
    shape = (column.shape[0], LANES // 2)
    return [jnp.broadcast_to(high, shape), jnp.broadcast_to(low, shape)]


def join_pair(lanes):
    lanes = lanes.astype(F32)
    return lanes[:, :1] + lanes[:, -1:]


def body(n_node, n_local, tokens, cotangent, gain, up_q, up_scale, down_q, down_scale):
    rows, cols = tokens.shape
    part = rows // CHUNKS
    hidden_units = up_q.shape[1]
    halves = n_node // n_local
    chips = n_local
    features = cols * n_node
    z = lax.axis_index("local")
    node = lax.axis_index("node")
    chip, core = node // halves, node % halves
    last = n_local - 1

    swap = [
        ((halves * c + j) * n_local + l, (halves * l + j) * n_local + c)
        for c in range(n_local)
        for j in range(halves)
        for l in range(n_local)
    ]

    def exchange(block):
        return lax.ppermute(block, ("node", "local"), swap)

    def core_swap(block):
        return lax.ppermute(block, "node", [(n, n ^ 1) for n in range(n_node)])

    def chip_swap(block, shift):
        return lax.ppermute(block, "node", [(n, n ^ (2 * shift)) for n in range(n_node)])

    even = z % 2 == 0

    def pair_swap(block, low, used=None):
        pairs = [(s, s + 1) for s in range(low, last, 2) if used is None or used(s)]
        if not pairs:
            return jnp.zeros_like(block)
        return lax.ppermute(block, "local", pairs + [(t, s) for s, t in pairs])

    def after(value, *others):
        return lax.optimization_barrier((value,) + others)[0]

    def take(array, index):
        width = array.shape[1]
        array = array.reshape(-1, n_local, part, width)
        return lax.dynamic_slice_in_dim(array, index, 1, 1).reshape(-1, width)

    def put(array, block, index):
        width = array.shape[1]
        stacked = array.reshape(-1, n_local, part, width)
        block = block.reshape(-1, 1, part, width)
        return lax.dynamic_update_slice_in_dim(stacked, block, index, 1).reshape(array.shape)

    def order(own, other):
        return jnp.where(
            core == 0,
            jnp.concatenate([own, other], axis=1),
            jnp.concatenate([other, own], axis=1),
        )

    def gather_chips(block):
        mine = jnp.zeros((block.shape[0] * chips, block.shape[1]), block.dtype)
        mine = put(mine, block, chip)
        for shift in range(1, chips):
            mine = put(mine, chip_swap(block, shift), chip ^ shift)
        return mine

    def gather_core(mine):
        return order(mine, core_swap(mine))

    def gather_node(block):
        return gather_core(gather_chips(block))

    def scatter_core(partial, tail=()):
        first, second = partial[:, :cols], partial[:, cols:]
        keep = jnp.where(core == 0, first, second)
        send = jnp.where(core == 0, second, first)
        if tail:
            keep = jnp.concatenate([keep, *tail], axis=1)
            send = jnp.concatenate([send, *tail], axis=1)
        return (keep.astype(F32) + core_swap(send).astype(F32)).astype(BF16)

    def swap_chips(both):
        return [chip_swap(take(both, chip ^ shift), shift) for shift in range(1, chips)]

    def scatter_chips(both):
        return sum_chips(both, swap_chips(both))

    def sum_chips(both, others):
        total = take(both, chip).astype(F32)
        for other in others:
            total = total + other.astype(F32)
        return total

    def scatter_node(partial):
        return scatter_chips(scatter_core(partial))

    def line(block, partial):
        first = second = None
        firsts, seconds = [], []
        if block is not None:
            first, second = pair_swap(block, 0), pair_swap(block, 1)
            firsts.append(first)
            seconds.append(second)
        for step in range(1, n_local if partial is not None else last):
            to_first, to_second = second, first
            if partial is not None:
                right = jnp.minimum(z + n_local - step, last)
                left = jnp.maximum(z - n_local + step, 0)
                to_first = take(partial, jnp.where(even, right, left))
                to_second = take(partial, jnp.where(even, left, right))
                if first is not None:
                    zero = jnp.zeros((), F32)
                    adds_right, adds_left = z < step, last - z < step
                    adds = jnp.where(even, adds_right, adds_left)
                    to_first = jnp.where(adds, to_first.astype(F32), zero)
                    to_first = (second.astype(F32) + to_first).astype(BF16)
                    adds = jnp.where(even, adds_left, adds_right)
                    to_second = jnp.where(adds, to_second.astype(F32), zero)
                    to_second = (first.astype(F32) + to_second).astype(BF16)
            if first is not None and step == (2 if block is None else last - 1 if partial is None else 0):
                to_first = after(to_first, first)
            used = None
            if block is None:
                used = lambda s, step=step: s < step or s + 1 > last - step
            elif partial is None:
                used = lambda s, step=step: s >= step or s + 1 <= last - step
            first, second = pair_swap(to_first, 0, used), pair_swap(to_second, 1, used)
            firsts.append(first)
            seconds.append(second)
        total = None
        if partial is not None:
            total = take(partial, z).astype(F32) + first.astype(F32) + second.astype(F32)
        out = None
        if block is not None:
            out = jnp.zeros((part * n_local, block.shape[1]), block.dtype)
            out = put(out, block, z)
            for ahead in range(1, n_local):
                behind = n_local - ahead
                right = jnp.where(even, seconds[behind - 1], firsts[behind - 1])
                left = jnp.where(even, firsts[ahead - 1], seconds[ahead - 1])
                piece = jnp.where(z >= behind, right, left)
                out = put(out, piece, (z + ahead) % n_local)
        return out, total

    def widen(block):
        return jnp.pad(block, ((0, 0), (0, LANES)))

    def chunk_of(array, h):
        size = part * n_local
        return array[h * size : (h + 1) * size]

    def up_partial(values):
        widened = values.astype(F32)
        squares = 0.0
        for start in range(0, values.shape[1], LANES):
            lanes = widened[:, start : start + LANES]
            squares = squares + lanes * lanes
        product = dot((widened * gains).astype(BF16), up_weight, ((1,), (0,)))
        return jnp.concatenate([product.astype(BF16), squares.astype(BF16)], axis=1)

    def finish_pre(total):
        mean = jnp.sum(total[:, hidden_units:], axis=-1, keepdims=True) / features
        factor = lax.rsqrt(mean + epsilon)
        return total[:, :hidden_units] * factor, factor

    x_home = exchange(tokens)
    other = exchange(jnp.concatenate([cotangent, jnp.pad(gain, ((0, PAD - 1), (0, 0)))], axis=0))
    g_home, gain_rows = other[:rows], other[rows:]
    down_weight = dequant_cols(down_q, down_scale)
    x_home = after(x_home, down_weight)
    up_weight = dequant_rows(after(up_q, x_home), up_scale)
    gains = order(gain_rows, core_swap(gain_rows))[:1].astype(F32)
    gains_home = gain_rows[:1].astype(F32)

    halves_of = range(CHUNKS)

    x = gather_core(after(gather_chips(x_home), g_home))
    partials = [up_partial(chunk_of(x, h)) for h in halves_of]
    totals = [line(None, partial)[1] for partial in partials]
    g = gather_node(after(g_home, *partials))
    slopes = [
        dot(chunk_of(g, h), down_weight, ((1,), (1,))).astype(BF16) for h in halves_of
    ]
    hiddens = []
    for h in halves_of:
        hidden = jax.nn.silu(finish_pre(totals[h])[0]).astype(BF16)
        hidden, total = line(hidden, slopes[h])
        hiddens.append(hidden)
        slopes[h] = total.astype(BF16)
    updates = [dot(hidden, down_weight, ((1,), (0,))).astype(BF16) for hidden in hiddens]
    update = scatter_node(jnp.concatenate(updates, axis=0))
    x1_home = (x_home.astype(F32) + update).astype(BF16)

    x = gather_node(x1_home)
    packed = []
    for h in halves_of:
        slope, total = line(widen(slopes[h]), up_partial(chunk_of(x, h)))
        slopes[h] = slope[:, :hidden_units]
        pre, factor = finish_pre(total)
        packed.append(
            line(jnp.concatenate([pre.astype(BF16)] + split_pair(factor), axis=1), None)[0]
        )

    hidden_second, updates, backs, tails = [], [], [], []

    def hidden_of(half):
        pre = half[:, :hidden_units].astype(F32)
        hidden_second.append((pre * jax.nn.sigmoid(pre)).astype(BF16))
        updates.append(dot(hidden_second[-1], down_weight, ((1,), (0,))).astype(BF16))

    def back_of(half, slope):
        pre = half[:, :hidden_units].astype(F32)
        sigma = jax.nn.sigmoid(pre)
        pre_grad = slope.astype(F32) * sigma * (1.0 + pre * (1.0 - sigma))
        inner = jnp.sum(pre_grad * pre, axis=-1, keepdims=True)
        tails.append(jnp.concatenate(split_pair(inner), axis=1))
        backs.append(dot(pre_grad.astype(BF16), up_weight, ((1,), (1,))).astype(BF16))

    hidden_of(packed[0])
    back_of(packed[0], slopes[0])
    packed[1] = after(packed[1], backs[0])
    hidden_of(packed[1])
    update = scatter_core(jnp.concatenate(updates, axis=0))
    back_of(packed[1], after(slopes[1], update))
    both = scatter_core(jnp.concatenate(backs, axis=0), [jnp.concatenate(tails, axis=0)])
    others = swap_chips(update)
    x2_home = (x1_home.astype(F32) + sum_chips(update, others)).astype(BF16)
    result = exchange(x2_home)
    total = scatter_chips(after(both, x2_home))
    lanes = [take(half[:, hidden_units:], chip) for half in packed]
    factor = join_pair(jnp.concatenate(lanes, axis=0))
    inner = join_pair(total[:, cols:]) / (features * factor)
    back = factor * (total[:, :cols] * gains_home) - x1_home.astype(F32) * (factor**3 * inner)
    grad_home = (g_home.astype(F32) + back).astype(BF16)
    below = gather_node(after(grad_home, result))
    grad_down = dot(
        jnp.concatenate(hiddens + hidden_second, axis=0),
        jnp.concatenate([below, g], axis=0),
        ((0,), (0,)),
    ).astype(BF16)
    return (result, grad_down)


def solution(mesh):
    n_node, n_local = mesh.shape["node"], mesh.shape["local"]

    def per_device(*arrays):
        return body(n_node, n_local, *arrays)

    in_specs = (
        P("local", "node"),
        P("local", "node"),
        P(None, "node"),
        P("local", "node"),
        P("local", "node"),
        P("node", "local"),
        P("node", "local"),
    )
    out_specs = (P("local", "node"), P("node", "local"))
    return jax.shard_map(
        per_device, mesh=mesh, in_specs=in_specs, out_specs=out_specs, check_vma=False
    )
```

```python
import jax
import jax.numpy as jnp
from jax import lax
from jax.experimental import pallas as pl
from jax.sharding import PartitionSpec as P

LANES = 128
PAD = 16
ROW_TILE = 256
CHUNKS = 2
epsilon = 1e-05
F32 = jnp.float32
BF16 = jnp.bfloat16


def dequant_rows(quanta, scales):
    blocks = scales.shape[0]
    widened = quanta.astype(F32).reshape(blocks, quanta.shape[0] // blocks, quanta.shape[1])
    return (widened * scales.astype(F32)[:, None, :]).reshape(quanta.shape).astype(BF16)


def scale_columns(quanta_ref, scales_ref, out_ref):
    blocks = scales_ref.shape[1]
    width = quanta_ref.shape[1] // blocks
    for block in range(blocks):
        columns = slice(block * width, (block + 1) * width)
        scale = scales_ref[:, block : block + 1].astype(F32)
        out_ref[:, columns] = (quanta_ref[:, columns].astype(F32) * scale).astype(BF16)


def dequant_cols(quanta, scales):
    rows, columns = quanta.shape
    tile = ROW_TILE if rows % ROW_TILE == 0 else rows
    return pl.pallas_call(
        scale_columns,
        grid=(rows // tile,),
        in_specs=[
            pl.BlockSpec((tile, columns), lambda i: (i, 0)),
            pl.BlockSpec((tile, scales.shape[1]), lambda i: (i, 0)),
        ],
        out_specs=pl.BlockSpec((tile, columns), lambda i: (i, 0)),
        out_shape=jax.ShapeDtypeStruct((rows, columns), BF16),
        cost_estimate=pl.CostEstimate(
            flops=rows * columns, bytes_accessed=4 * rows * columns, transcendentals=0
        ),
    )(quanta, scales)


def dot(left, right, dims):
    return lax.dot_general(left, right, (dims, ((), ())), preferred_element_type=F32)


def split_pair(column):
    high = column.astype(BF16)
    low = (column - high.astype(F32)).astype(BF16)
    shape = (column.shape[0], LANES // 2)
    return [jnp.broadcast_to(high, shape), jnp.broadcast_to(low, shape)]


def join_pair(lanes):
    lanes = lanes.astype(F32)
    return lanes[:, :1] + lanes[:, -1:]


def body(n_node, n_local, tokens, cotangent, gain, up_q, up_scale, down_q, down_scale):
    rows, cols = tokens.shape
    part = rows // CHUNKS
    hidden_units = up_q.shape[1]
    halves = n_node // n_local
    chips = n_local
    features = cols * n_node
    z = lax.axis_index("local")
    node = lax.axis_index("node")
    chip, core = node // halves, node % halves
    last = n_local - 1

    swap = [
        ((halves * c + j) * n_local + l, (halves * l + j) * n_local + c)
        for c in range(n_local)
        for j in range(halves)
        for l in range(n_local)
    ]

    def exchange(block):
        return lax.ppermute(block, ("node", "local"), swap)

    def core_swap(block):
        return lax.ppermute(block, "node", [(n, n ^ 1) for n in range(n_node)])

    def chip_swap(block, shift):
        return lax.ppermute(block, "node", [(n, n ^ (2 * shift)) for n in range(n_node)])

    even = z % 2 == 0

    def pair_swap(block, low, used=None):
        pairs = [(s, s + 1) for s in range(low, last, 2) if used is None or used(s)]
        if not pairs:
            return jnp.zeros_like(block)
        return lax.ppermute(block, "local", pairs + [(t, s) for s, t in pairs])

    def after(value, *others):
        return lax.optimization_barrier((value,) + others)[0]

    def take(array, index):
        width = array.shape[1]
        array = array.reshape(-1, n_local, part, width)
        return lax.dynamic_slice_in_dim(array, index, 1, 1).reshape(-1, width)

    def put(array, block, index):
        width = array.shape[1]
        stacked = array.reshape(-1, n_local, part, width)
        block = block.reshape(-1, 1, part, width)
        return lax.dynamic_update_slice_in_dim(stacked, block, index, 1).reshape(array.shape)

    def order(own, other):
        return jnp.where(
            core == 0,
            jnp.concatenate([own, other], axis=1),
            jnp.concatenate([other, own], axis=1),
        )

    def gather_chips(block, *others):
        mine = jnp.zeros((block.shape[0] * chips, block.shape[1]), block.dtype)
        mine = put(mine, block, chip)
        for shift in range(1, chips):
            arrived = chip_swap(block, shift)
            if others:
                arrived = after(arrived, *others)
            mine = put(mine, arrived, chip ^ shift)
        return mine

    def gather_core(mine):
        return order(mine, core_swap(mine))

    def gather_node(block):
        return gather_core(gather_chips(block))

    def scatter_core(partial, tail=()):
        first, second = partial[:, :cols], partial[:, cols:]
        keep = jnp.where(core == 0, first, second)
        send = jnp.where(core == 0, second, first)
        if tail:
            keep = jnp.concatenate([keep, *tail], axis=1)
            send = jnp.concatenate([send, *tail], axis=1)
        return (keep.astype(F32) + core_swap(send).astype(F32)).astype(BF16)

    def swap_chips(both):
        return [chip_swap(take(both, chip ^ shift), shift) for shift in range(1, chips)]

    def scatter_chips(both):
        return sum_chips(both, swap_chips(both))

    def sum_chips(both, others):
        total = take(both, chip).astype(F32)
        for other in others:
            total = total + other.astype(F32)
        return total

    def scatter_node(partial):
        return scatter_chips(scatter_core(partial))

    def line(block, partial):
        first = second = None
        firsts, seconds = [], []
        if block is not None:
            first, second = pair_swap(block, 0), pair_swap(block, 1)
            firsts.append(first)
            seconds.append(second)
        for step in range(1, n_local if partial is not None else last):
            to_first, to_second = second, first
            if partial is not None:
                right = jnp.minimum(z + n_local - step, last)
                left = jnp.maximum(z - n_local + step, 0)
                to_first = take(partial, jnp.where(even, right, left))
                to_second = take(partial, jnp.where(even, left, right))
                if first is not None:
                    zero = jnp.zeros((), F32)
                    adds_right, adds_left = z < step, last - z < step
                    adds = jnp.where(even, adds_right, adds_left)
                    to_first = jnp.where(adds, to_first.astype(F32), zero)
                    to_first = (second.astype(F32) + to_first).astype(BF16)
                    adds = jnp.where(even, adds_left, adds_right)
                    to_second = jnp.where(adds, to_second.astype(F32), zero)
                    to_second = (first.astype(F32) + to_second).astype(BF16)
            if first is not None and step == (2 if block is None else last - 1 if partial is None else 0):
                to_first = after(to_first, first)
            used = None
            if block is None:
                used = lambda s, step=step: s < step or s + 1 > last - step
            elif partial is None:
                used = lambda s, step=step: s >= step or s + 1 <= last - step
            first, second = pair_swap(to_first, 0, used), pair_swap(to_second, 1, used)
            firsts.append(first)
            seconds.append(second)
        total = None
        if partial is not None:
            total = take(partial, z).astype(F32) + first.astype(F32) + second.astype(F32)
        out = None
        if block is not None:
            out = jnp.zeros((part * n_local, block.shape[1]), block.dtype)
            out = put(out, block, z)
            for ahead in range(1, n_local):
                behind = n_local - ahead
                right = jnp.where(even, seconds[behind - 1], firsts[behind - 1])
                left = jnp.where(even, firsts[ahead - 1], seconds[ahead - 1])
                piece = jnp.where(z >= behind, right, left)
                out = put(out, piece, (z + ahead) % n_local)
        return out, total, firsts[0]

    def widen(block):
        return jnp.pad(block, ((0, 0), (0, LANES)))

    def chunk_of(array, h):
        size = part * n_local
        return array[h * size : (h + 1) * size]

    def up_partial(values):
        widened = values.astype(F32)
        squares = 0.0
        for start in range(0, values.shape[1], LANES):
            lanes = widened[:, start : start + LANES]
            squares = squares + lanes * lanes
        product = dot((widened * gains).astype(BF16), up_weight, ((1,), (0,)))
        return jnp.concatenate([product.astype(BF16), squares.astype(BF16)], axis=1)

    def finish_pre(total):
        mean = jnp.sum(total[:, hidden_units:], axis=-1, keepdims=True) / features
        factor = lax.rsqrt(mean + epsilon)
        return total[:, :hidden_units] * factor, factor

    x_home = exchange(tokens)
    other = exchange(jnp.concatenate([cotangent, jnp.pad(gain, ((0, PAD - 1), (0, 0)))], axis=0))
    g_home, gain_rows = other[:rows], other[rows:]
    down_weight = dequant_cols(down_q, down_scale)
    x_home = after(x_home, down_weight)
    up_weight = dequant_rows(after(up_q, x_home), up_scale)
    gains = order(gain_rows, core_swap(gain_rows))[:1].astype(F32)
    gains_home = gain_rows[:1].astype(F32)

    halves_of = range(CHUNKS)

    x = gather_core(after(gather_chips(x_home), g_home))
    partials = [up_partial(chunk_of(x, h)) for h in halves_of]
    totals, seen = [], []
    for partial in partials:
        _, total, arrived = line(None, partial)
        totals.append(total)
        seen.append(arrived)
    g = gather_core(gather_chips(after(g_home, *partials), *seen))
    slopes = [
        dot(chunk_of(g, h), down_weight, ((1,), (1,))).astype(BF16) for h in halves_of
    ]
    hiddens = []
    for h in halves_of:
        hidden = jax.nn.silu(finish_pre(totals[h])[0]).astype(BF16)
        hidden, total, _ = line(hidden, slopes[h])
        hiddens.append(hidden)
        slopes[h] = total.astype(BF16)
    updates = [dot(hidden, down_weight, ((1,), (0,))).astype(BF16) for hidden in hiddens]
    update = scatter_node(jnp.concatenate(updates, axis=0))
    x1_home = (x_home.astype(F32) + update).astype(BF16)

    x = gather_node(x1_home)
    packed = []
    for h in halves_of:
        slope, total, _ = line(widen(slopes[h]), up_partial(chunk_of(x, h)))
        slopes[h] = slope[:, :hidden_units]
        pre, factor = finish_pre(total)
        packed.append(
            line(jnp.concatenate([pre.astype(BF16)] + split_pair(factor), axis=1), None)[0]
        )

    hidden_second, updates, backs, tails = [], [], [], []

    def hidden_of(half):
        pre = half[:, :hidden_units].astype(F32)
        hidden_second.append((pre * jax.nn.sigmoid(pre)).astype(BF16))
        updates.append(dot(hidden_second[-1], down_weight, ((1,), (0,))).astype(BF16))

    def back_of(half, slope):
        pre = half[:, :hidden_units].astype(F32)
        sigma = jax.nn.sigmoid(pre)
        pre_grad = slope.astype(F32) * sigma * (1.0 + pre * (1.0 - sigma))
        inner = jnp.sum(pre_grad * pre, axis=-1, keepdims=True)
        tails.append(jnp.concatenate(split_pair(inner), axis=1))
        backs.append(dot(pre_grad.astype(BF16), up_weight, ((1,), (1,))).astype(BF16))

    hidden_of(packed[0])
    back_of(packed[0], slopes[0])
    packed[1] = after(packed[1], backs[0])
    hidden_of(packed[1])
    update = scatter_core(jnp.concatenate(updates, axis=0))
    back_of(packed[1], after(slopes[1], update))
    both = scatter_core(jnp.concatenate(backs, axis=0), [jnp.concatenate(tails, axis=0)])
    others = swap_chips(update)
    x2_home = (x1_home.astype(F32) + sum_chips(update, others)).astype(BF16)
    result = exchange(x2_home)
    total = sum_chips(both, [after(other, x2_home) for other in swap_chips(both)])
    lanes = [take(half[:, hidden_units:], chip) for half in packed]
    factor = join_pair(jnp.concatenate(lanes, axis=0))
    inner = join_pair(total[:, cols:]) / (features * factor)
    back = factor * (total[:, :cols] * gains_home) - x1_home.astype(F32) * (factor**3 * inner)
    grad_home = (g_home.astype(F32) + back).astype(BF16)
    below = gather_node(after(grad_home, result))
    grad_down = dot(
        jnp.concatenate(hiddens + hidden_second, axis=0),
        jnp.concatenate([below, g], axis=0),
        ((0,), (0,)),
    ).astype(BF16)
    return (result, grad_down)


def solution(mesh):
    n_node, n_local = mesh.shape["node"], mesh.shape["local"]

    def per_device(*arrays):
        return body(n_node, n_local, *arrays)

    in_specs = (
        P("local", "node"),
        P("local", "node"),
        P(None, "node"),
        P("local", "node"),
        P("local", "node"),
        P("node", "local"),
        P("node", "local"),
    )
    out_specs = (P("local", "node"), P("node", "local"))
    return jax.shard_map(
        per_device, mesh=mesh, in_specs=in_specs, out_specs=out_specs, check_vma=False
    )
```

```python
import jax
import jax.numpy as jnp
from jax import lax
from jax.experimental import pallas as pl
from jax.sharding import PartitionSpec as P

LANES = 128
PAD = 16
ROW_TILE = 256
CHUNKS = 2
epsilon = 1e-05
F32 = jnp.float32
BF16 = jnp.bfloat16


def dequant_rows(quanta, scales):
    blocks = scales.shape[0]
    widened = quanta.astype(F32).reshape(blocks, quanta.shape[0] // blocks, quanta.shape[1])
    return (widened * scales.astype(F32)[:, None, :]).reshape(quanta.shape).astype(BF16)


def scale_columns(quanta_ref, scales_ref, out_ref):
    blocks = scales_ref.shape[1]
    width = quanta_ref.shape[1] // blocks
    for block in range(blocks):
        columns = slice(block * width, (block + 1) * width)
        scale = scales_ref[:, block : block + 1].astype(F32)
        out_ref[:, columns] = (quanta_ref[:, columns].astype(F32) * scale).astype(BF16)


def dequant_cols(quanta, scales):
    rows, columns = quanta.shape
    tile = ROW_TILE if rows % ROW_TILE == 0 else rows
    return pl.pallas_call(
        scale_columns,
        grid=(rows // tile,),
        in_specs=[
            pl.BlockSpec((tile, columns), lambda i: (i, 0)),
            pl.BlockSpec((tile, scales.shape[1]), lambda i: (i, 0)),
        ],
        out_specs=pl.BlockSpec((tile, columns), lambda i: (i, 0)),
        out_shape=jax.ShapeDtypeStruct((rows, columns), BF16),
        cost_estimate=pl.CostEstimate(
            flops=rows * columns, bytes_accessed=4 * rows * columns, transcendentals=0
        ),
    )(quanta, scales)


def dot(left, right, dims):
    return lax.dot_general(left, right, (dims, ((), ())), preferred_element_type=F32)


def split_pair(column):
    high = column.astype(BF16)
    low = (column - high.astype(F32)).astype(BF16)
    shape = (column.shape[0], LANES // 2)
    return [jnp.broadcast_to(high, shape), jnp.broadcast_to(low, shape)]


def join_pair(lanes):
    lanes = lanes.astype(F32)
    return lanes[:, :1] + lanes[:, -1:]


def body(n_node, n_local, tokens, cotangent, gain, up_q, up_scale, down_q, down_scale):
    rows, cols = tokens.shape
    part = rows // CHUNKS
    hidden_units = up_q.shape[1]
    halves = n_node // n_local
    chips = n_local
    features = cols * n_node
    z = lax.axis_index("local")
    node = lax.axis_index("node")
    chip, core = node // halves, node % halves
    last = n_local - 1

    swap = [
        ((halves * c + j) * n_local + l, (halves * l + j) * n_local + c)
        for c in range(n_local)
        for j in range(halves)
        for l in range(n_local)
    ]

    def exchange(block):
        return lax.ppermute(block, ("node", "local"), swap)

    def core_swap(block):
        return lax.ppermute(block, "node", [(n, n ^ 1) for n in range(n_node)])

    def chip_swap(block, shift):
        return lax.ppermute(block, "node", [(n, n ^ (2 * shift)) for n in range(n_node)])

    even = z % 2 == 0

    def pair_swap(block, low, used=None):
        pairs = [(s, s + 1) for s in range(low, last, 2) if used is None or used(s)]
        if not pairs:
            return jnp.zeros_like(block)
        return lax.ppermute(block, "local", pairs + [(t, s) for s, t in pairs])

    def after(value, *others):
        return lax.optimization_barrier((value,) + others)[0]

    def take(array, index):
        width = array.shape[1]
        array = array.reshape(-1, n_local, part, width)
        return lax.dynamic_slice_in_dim(array, index, 1, 1).reshape(-1, width)

    def put(array, block, index):
        width = array.shape[1]
        stacked = array.reshape(-1, n_local, part, width)
        block = block.reshape(-1, 1, part, width)
        return lax.dynamic_update_slice_in_dim(stacked, block, index, 1).reshape(array.shape)

    def order(own, other):
        return jnp.where(
            core == 0,
            jnp.concatenate([own, other], axis=1),
            jnp.concatenate([other, own], axis=1),
        )

    def gather_chips(block):
        mine = jnp.zeros((block.shape[0] * chips, block.shape[1]), block.dtype)
        mine = put(mine, block, chip)
        for shift in range(1, chips):
            mine = put(mine, chip_swap(block, shift), chip ^ shift)
        return mine

    def gather_core(mine):
        return order(mine, core_swap(mine))

    def gather_node(block):
        return gather_core(gather_chips(block))

    def scatter_core(partial, tail=()):
        first, second = partial[:, :cols], partial[:, cols:]
        keep = jnp.where(core == 0, first, second)
        send = jnp.where(core == 0, second, first)
        if tail:
            keep = jnp.concatenate([keep, *tail], axis=1)
            send = jnp.concatenate([send, *tail], axis=1)
        return (keep.astype(F32) + core_swap(send).astype(F32)).astype(BF16)

    def swap_chips(both):
        return [chip_swap(take(both, chip ^ shift), shift) for shift in range(1, chips)]

    def scatter_chips(both):
        return sum_chips(both, swap_chips(both))

    def sum_chips(both, others):
        total = take(both, chip).astype(F32)
        for other in others:
            total = total + other.astype(F32)
        return total

    def scatter_node(partial):
        return scatter_chips(scatter_core(partial))

    def line(block, partial):
        first = second = None
        firsts, seconds = [], []
        if block is not None:
            first, second = pair_swap(block, 0), pair_swap(block, 1)
            firsts.append(first)
            seconds.append(second)
        for step in range(1, n_local if partial is not None else last):
            to_first, to_second = second, first
            if partial is not None:
                right = jnp.minimum(z + n_local - step, last)
                left = jnp.maximum(z - n_local + step, 0)
                to_first = take(partial, jnp.where(even, right, left))
                to_second = take(partial, jnp.where(even, left, right))
                if first is not None:
                    zero = jnp.zeros((), F32)
                    adds_right, adds_left = z < step, last - z < step
                    adds = jnp.where(even, adds_right, adds_left)
                    to_first = jnp.where(adds, to_first.astype(F32), zero)
                    to_first = (second.astype(F32) + to_first).astype(BF16)
                    adds = jnp.where(even, adds_left, adds_right)
                    to_second = jnp.where(adds, to_second.astype(F32), zero)
                    to_second = (first.astype(F32) + to_second).astype(BF16)
            if first is not None and step == (2 if block is None else last - 1 if partial is None else 0):
                to_first = after(to_first, first)
            used = None
            if block is None:
                used = lambda s, step=step: s < step or s + 1 > last - step
            elif partial is None:
                used = lambda s, step=step: s >= step or s + 1 <= last - step
            first, second = pair_swap(to_first, 0, used), pair_swap(to_second, 1, used)
            firsts.append(first)
            seconds.append(second)
        total = None
        if partial is not None:
            total = take(partial, z).astype(F32) + first.astype(F32) + second.astype(F32)
        out = None
        if block is not None:
            out = jnp.zeros((part * n_local, block.shape[1]), block.dtype)
            out = put(out, block, z)
            for ahead in range(1, n_local):
                behind = n_local - ahead
                right = jnp.where(even, seconds[behind - 1], firsts[behind - 1])
                left = jnp.where(even, firsts[ahead - 1], seconds[ahead - 1])
                piece = jnp.where(z >= behind, right, left)
                out = put(out, piece, (z + ahead) % n_local)
        return out, total

    def widen(block):
        return jnp.pad(block, ((0, 0), (0, LANES)))

    def chunk_of(array, h):
        size = part * n_local
        return array[h * size : (h + 1) * size]

    def up_partial(values):
        widened = values.astype(F32)
        squares = 0.0
        for start in range(0, values.shape[1], LANES):
            lanes = widened[:, start : start + LANES]
            squares = squares + lanes * lanes
        product = dot((widened * gains).astype(BF16), up_weight, ((1,), (0,)))
        return jnp.concatenate([product.astype(BF16), squares.astype(BF16)], axis=1)

    def finish_pre(total):
        mean = jnp.sum(total[:, hidden_units:], axis=-1, keepdims=True) / features
        factor = lax.rsqrt(mean + epsilon)
        return total[:, :hidden_units] * factor, factor

    x_home = exchange(tokens)
    other = exchange(jnp.concatenate([cotangent, jnp.pad(gain, ((0, PAD - 1), (0, 0)))], axis=0))
    g_home, gain_rows = other[:rows], other[rows:]
    down_weight = dequant_cols(down_q, down_scale)
    x_home = after(x_home, down_weight)
    up_weight = dequant_rows(after(up_q, x_home), up_scale)
    gains = order(gain_rows, core_swap(gain_rows))[:1].astype(F32)
    gains_home = gain_rows[:1].astype(F32)

    halves_of = range(CHUNKS)

    x = gather_core(after(gather_chips(x_home), g_home))
    partials = [up_partial(chunk_of(x, h)) for h in halves_of]
    totals = [line(None, partial)[1] for partial in partials]
    g = gather_node(after(g_home, *partials))
    slopes = [
        dot(chunk_of(g, h), down_weight, ((1,), (1,))).astype(BF16) for h in halves_of
    ]
    hiddens = []
    for h in halves_of:
        hidden = jax.nn.silu(finish_pre(totals[h])[0]).astype(BF16)
        hidden, total = line(hidden, slopes[h])
        hiddens.append(hidden)
        slopes[h] = total.astype(BF16)
    updates = [dot(hidden, down_weight, ((1,), (0,))).astype(BF16) for hidden in hiddens]
    update = scatter_node(jnp.concatenate(updates, axis=0))
    x1_home = (x_home.astype(F32) + update).astype(BF16)

    x = gather_node(x1_home)
    packed = []
    for h in halves_of:
        slope, total = line(widen(slopes[h]), up_partial(chunk_of(x, h)))
        slopes[h] = slope[:, :hidden_units]
        pre, factor = finish_pre(total)
        packed.append(
            line(jnp.concatenate([pre.astype(BF16)] + split_pair(factor), axis=1), None)[0]
        )

    hidden_second, updates, backs, tails = [], [], [], []

    def hidden_of(half):
        pre = half[:, :hidden_units].astype(F32)
        hidden_second.append((pre * jax.nn.sigmoid(pre)).astype(BF16))
        updates.append(dot(hidden_second[-1], down_weight, ((1,), (0,))).astype(BF16))

    def back_of(half, slope):
        pre = half[:, :hidden_units].astype(F32)
        sigma = jax.nn.sigmoid(pre)
        pre_grad = slope.astype(F32) * sigma * (1.0 + pre * (1.0 - sigma))
        inner = jnp.sum(pre_grad * pre, axis=-1, keepdims=True)
        tails.append(jnp.concatenate(split_pair(inner), axis=1))
        backs.append(dot(pre_grad.astype(BF16), up_weight, ((1,), (1,))).astype(BF16))

    hidden_of(packed[0])
    back_of(packed[0], slopes[0])
    packed[1] = after(packed[1], backs[0])
    hidden_of(packed[1])
    update = scatter_core(jnp.concatenate(updates, axis=0))
    back_of(packed[1], after(slopes[1], update))
    both = scatter_core(jnp.concatenate(backs, axis=0), [jnp.concatenate(tails, axis=0)])
    others = swap_chips(update)
    x2_home = (x1_home.astype(F32) + sum_chips(update, others)).astype(BF16)
    result = exchange(x2_home)
    total = sum_chips(both, [after(other, x2_home) for other in swap_chips(both)])
    lanes = [take(half[:, hidden_units:], chip) for half in packed]
    factor = join_pair(jnp.concatenate(lanes, axis=0))
    inner = join_pair(total[:, cols:]) / (features * factor)
    back = factor * (total[:, :cols] * gains_home) - x1_home.astype(F32) * (factor**3 * inner)
    grad_home = (g_home.astype(F32) + back).astype(BF16)
    below = gather_node(after(grad_home, result))
    grad_down = dot(
        jnp.concatenate(hiddens + hidden_second, axis=0),
        jnp.concatenate([below, g], axis=0),
        ((0,), (0,)),
    ).astype(BF16)
    return (result, grad_down)


def solution(mesh):
    n_node, n_local = mesh.shape["node"], mesh.shape["local"]

    def per_device(*arrays):
        return body(n_node, n_local, *arrays)

    in_specs = (
        P("local", "node"),
        P("local", "node"),
        P(None, "node"),
        P("local", "node"),
        P("local", "node"),
        P("node", "local"),
        P("node", "local"),
    )
    out_specs = (P("local", "node"), P("node", "local"))
    return jax.shard_map(
        per_device, mesh=mesh, in_specs=in_specs, out_specs=out_specs, check_vma=False
    )
```

```python
import jax
import jax.numpy as jnp
from jax import lax
from jax.experimental import pallas as pl
from jax.sharding import PartitionSpec as P

LANES = 128
PAD = 16
ROW_TILE = 256
CHUNKS = 2
epsilon = 1e-05
F32 = jnp.float32
BF16 = jnp.bfloat16


def dequant_rows(quanta, scales):
    blocks = scales.shape[0]
    widened = quanta.astype(F32).reshape(blocks, quanta.shape[0] // blocks, quanta.shape[1])
    return (widened * scales.astype(F32)[:, None, :]).reshape(quanta.shape).astype(BF16)


def scale_columns(quanta_ref, scales_ref, out_ref):
    blocks = scales_ref.shape[1]
    width = quanta_ref.shape[1] // blocks
    for block in range(blocks):
        columns = slice(block * width, (block + 1) * width)
        scale = scales_ref[:, block : block + 1].astype(F32)
        out_ref[:, columns] = (quanta_ref[:, columns].astype(F32) * scale).astype(BF16)


def dequant_cols(quanta, scales):
    rows, columns = quanta.shape
    tile = ROW_TILE if rows % ROW_TILE == 0 else rows
    return pl.pallas_call(
        scale_columns,
        grid=(rows // tile,),
        in_specs=[
            pl.BlockSpec((tile, columns), lambda i: (i, 0)),
            pl.BlockSpec((tile, scales.shape[1]), lambda i: (i, 0)),
        ],
        out_specs=pl.BlockSpec((tile, columns), lambda i: (i, 0)),
        out_shape=jax.ShapeDtypeStruct((rows, columns), BF16),
        cost_estimate=pl.CostEstimate(
            flops=rows * columns, bytes_accessed=4 * rows * columns, transcendentals=0
        ),
    )(quanta, scales)


def dot(left, right, dims):
    return lax.dot_general(left, right, (dims, ((), ())), preferred_element_type=F32)


def split_pair(column):
    high = column.astype(BF16)
    low = (column - high.astype(F32)).astype(BF16)
    shape = (column.shape[0], LANES // 2)
    return [jnp.broadcast_to(high, shape), jnp.broadcast_to(low, shape)]


def join_pair(lanes):
    lanes = lanes.astype(F32)
    return lanes[:, :1] + lanes[:, -1:]


def body(n_node, n_local, tokens, cotangent, gain, up_q, up_scale, down_q, down_scale):
    rows, cols = tokens.shape
    part = rows // CHUNKS
    hidden_units = up_q.shape[1]
    halves = n_node // n_local
    chips = n_local
    features = cols * n_node
    z = lax.axis_index("local")
    node = lax.axis_index("node")
    chip, core = node // halves, node % halves
    last = n_local - 1

    swap = [
        ((halves * c + j) * n_local + l, (halves * l + j) * n_local + c)
        for c in range(n_local)
        for j in range(halves)
        for l in range(n_local)
    ]

    def exchange(block):
        return lax.ppermute(block, ("node", "local"), swap)

    def core_swap(block):
        return lax.ppermute(block, "node", [(n, n ^ 1) for n in range(n_node)])

    def chip_swap(block, shift):
        return lax.ppermute(block, "node", [(n, n ^ (2 * shift)) for n in range(n_node)])

    even = z % 2 == 0

    def pair_swap(block, low, used=None):
        pairs = [(s, s + 1) for s in range(low, last, 2) if used is None or used(s)]
        if not pairs:
            return jnp.zeros_like(block)
        return lax.ppermute(block, "local", pairs + [(t, s) for s, t in pairs])

    def after(value, *others):
        return lax.optimization_barrier((value,) + others)[0]

    def take(array, index):
        width = array.shape[1]
        array = array.reshape(-1, n_local, part, width)
        return lax.dynamic_slice_in_dim(array, index, 1, 1).reshape(-1, width)

    def put(array, block, index):
        width = array.shape[1]
        stacked = array.reshape(-1, n_local, part, width)
        block = block.reshape(-1, 1, part, width)
        return lax.dynamic_update_slice_in_dim(stacked, block, index, 1).reshape(array.shape)

    def order(own, other):
        return jnp.where(
            core == 0,
            jnp.concatenate([own, other], axis=1),
            jnp.concatenate([other, own], axis=1),
        )

    def gather_chips(block, *others):
        mine = jnp.zeros((block.shape[0] * chips, block.shape[1]), block.dtype)
        mine = put(mine, block, chip)
        for shift in range(1, chips):
            arrived = chip_swap(block, shift)
            if others:
                arrived = after(arrived, *others)
            mine = put(mine, arrived, chip ^ shift)
        return mine

    def gather_core(mine):
        return order(mine, core_swap(mine))

    def gather_node(block):
        return gather_core(gather_chips(block))

    def scatter_core(partial, tail=()):
        first, second = partial[:, :cols], partial[:, cols:]
        keep = jnp.where(core == 0, first, second)
        send = jnp.where(core == 0, second, first)
        if tail:
            keep = jnp.concatenate([keep, *tail], axis=1)
            send = jnp.concatenate([send, *tail], axis=1)
        return (keep.astype(F32) + core_swap(send).astype(F32)).astype(BF16)

    def swap_chips(both):
        return [chip_swap(take(both, chip ^ shift), shift) for shift in range(1, chips)]

    def scatter_chips(both):
        return sum_chips(both, swap_chips(both))

    def sum_chips(both, others):
        total = take(both, chip).astype(F32)
        for other in others:
            total = total + other.astype(F32)
        return total

    def scatter_node(partial):
        return scatter_chips(scatter_core(partial))

    def line(block, partial):
        first = second = None
        firsts, seconds = [], []
        if block is not None:
            first, second = pair_swap(block, 0), pair_swap(block, 1)
            firsts.append(first)
            seconds.append(second)
        for step in range(1, n_local if partial is not None else last):
            to_first, to_second = second, first
            if partial is not None:
                right = jnp.minimum(z + n_local - step, last)
                left = jnp.maximum(z - n_local + step, 0)
                to_first = take(partial, jnp.where(even, right, left))
                to_second = take(partial, jnp.where(even, left, right))
                if first is not None:
                    zero = jnp.zeros((), F32)
                    adds_right, adds_left = z < step, last - z < step
                    adds = jnp.where(even, adds_right, adds_left)
                    to_first = jnp.where(adds, to_first.astype(F32), zero)
                    to_first = (second.astype(F32) + to_first).astype(BF16)
                    adds = jnp.where(even, adds_left, adds_right)
                    to_second = jnp.where(adds, to_second.astype(F32), zero)
                    to_second = (first.astype(F32) + to_second).astype(BF16)
            if first is not None and step == (2 if block is None else last - 1 if partial is None else 0):
                to_first = after(to_first, first)
            used = None
            if block is None:
                used = lambda s, step=step: s < step or s + 1 > last - step
            elif partial is None:
                used = lambda s, step=step: s >= step or s + 1 <= last - step
            first, second = pair_swap(to_first, 0, used), pair_swap(to_second, 1, used)
            firsts.append(first)
            seconds.append(second)
        total = None
        if partial is not None:
            total = take(partial, z).astype(F32) + first.astype(F32) + second.astype(F32)
        out = None
        if block is not None:
            out = jnp.zeros((part * n_local, block.shape[1]), block.dtype)
            out = put(out, block, z)
            for ahead in range(1, n_local):
                behind = n_local - ahead
                right = jnp.where(even, seconds[behind - 1], firsts[behind - 1])
                left = jnp.where(even, firsts[ahead - 1], seconds[ahead - 1])
                piece = jnp.where(z >= behind, right, left)
                out = put(out, piece, (z + ahead) % n_local)
        return out, total

    def widen(block):
        return jnp.pad(block, ((0, 0), (0, LANES)))

    def chunk_of(array, h):
        size = part * n_local
        return array[h * size : (h + 1) * size]

    def up_partial(values):
        widened = values.astype(F32)
        squares = 0.0
        for start in range(0, values.shape[1], LANES):
            lanes = widened[:, start : start + LANES]
            squares = squares + lanes * lanes
        product = dot((widened * gains).astype(BF16), up_weight, ((1,), (0,)))
        return jnp.concatenate([product.astype(BF16), squares.astype(BF16)], axis=1)

    def finish_pre(total):
        mean = jnp.sum(total[:, hidden_units:], axis=-1, keepdims=True) / features
        factor = lax.rsqrt(mean + epsilon)
        return total[:, :hidden_units] * factor, factor

    x_home = exchange(tokens)
    other = exchange(jnp.concatenate([cotangent, jnp.pad(gain, ((0, PAD - 1), (0, 0)))], axis=0))
    g_home, gain_rows = other[:rows], other[rows:]
    down_weight = dequant_cols(down_q, down_scale)
    x_home = after(x_home, down_weight)
    up_weight = dequant_rows(after(up_q, x_home), up_scale)
    gains = order(gain_rows, core_swap(gain_rows))[:1].astype(F32)
    gains_home = gain_rows[:1].astype(F32)

    halves_of = range(CHUNKS)

    x = gather_core(after(gather_chips(x_home), g_home))
    partials = [up_partial(chunk_of(x, h)) for h in halves_of]
    totals = [line(None, partial)[1] for partial in partials]
    g = gather_node(after(g_home, *partials))
    slopes = [
        dot(chunk_of(g, h), down_weight, ((1,), (1,))).astype(BF16) for h in halves_of
    ]
    hiddens = []
    for h in halves_of:
        hidden = jax.nn.silu(finish_pre(totals[h])[0]).astype(BF16)
        hidden, total = line(hidden, slopes[h])
        hiddens.append(hidden)
        slopes[h] = total.astype(BF16)
    updates = [dot(hidden, down_weight, ((1,), (0,))).astype(BF16) for hidden in hiddens]
    update = scatter_node(jnp.concatenate(updates, axis=0))
    x1_home = (x_home.astype(F32) + update).astype(BF16)

    x = gather_node(x1_home)
    packed = []
    for h in halves_of:
        slope, total = line(widen(slopes[h]), up_partial(chunk_of(x, h)))
        slopes[h] = slope[:, :hidden_units]
        pre, factor = finish_pre(total)
        packed.append(
            line(jnp.concatenate([pre.astype(BF16)] + split_pair(factor), axis=1), None)[0]
        )

    hidden_second, updates, backs, tails = [], [], [], []

    def hidden_of(half):
        pre = half[:, :hidden_units].astype(F32)
        hidden_second.append((pre * jax.nn.sigmoid(pre)).astype(BF16))
        updates.append(dot(hidden_second[-1], down_weight, ((1,), (0,))).astype(BF16))

    def back_of(half, slope):
        pre = half[:, :hidden_units].astype(F32)
        sigma = jax.nn.sigmoid(pre)
        pre_grad = slope.astype(F32) * sigma * (1.0 + pre * (1.0 - sigma))
        inner = jnp.sum(pre_grad * pre, axis=-1, keepdims=True)
        tails.append(jnp.concatenate(split_pair(inner), axis=1))
        backs.append(dot(pre_grad.astype(BF16), up_weight, ((1,), (1,))).astype(BF16))

    hidden_of(packed[0])
    back_of(packed[0], slopes[0])
    packed[1] = after(packed[1], backs[0])
    hidden_of(packed[1])
    update = scatter_core(jnp.concatenate(updates, axis=0))
    back_of(packed[1], after(slopes[1], update))
    both = scatter_core(jnp.concatenate(backs, axis=0), [jnp.concatenate(tails, axis=0)])
    others = swap_chips(update)
    x2_home = (x1_home.astype(F32) + sum_chips(update, others)).astype(BF16)
    result = exchange(x2_home)
    total = sum_chips(both, [after(other, x2_home) for other in swap_chips(both)])
    lanes = [take(half[:, hidden_units:], chip) for half in packed]
    factor = join_pair(jnp.concatenate(lanes, axis=0))
    inner = join_pair(total[:, cols:]) / (features * factor)
    back = factor * (total[:, :cols] * gains_home) - x1_home.astype(F32) * (factor**3 * inner)
    grad_home = (g_home.astype(F32) + back).astype(BF16)
    below = gather_core(gather_chips(grad_home, result))
    grad_down = dot(
        jnp.concatenate(hiddens + hidden_second, axis=0),
        jnp.concatenate([below, g], axis=0),
        ((0,), (0,)),
    ).astype(BF16)
    return (result, grad_down)


def solution(mesh):
    n_node, n_local = mesh.shape["node"], mesh.shape["local"]

    def per_device(*arrays):
        return body(n_node, n_local, *arrays)

    in_specs = (
        P("local", "node"),
        P("local", "node"),
        P(None, "node"),
        P("local", "node"),
        P("local", "node"),
        P("node", "local"),
        P("node", "local"),
    )
    out_specs = (P("local", "node"), P("node", "local"))
    return jax.shard_map(
        per_device, mesh=mesh, in_specs=in_specs, out_specs=out_specs, check_vma=False
    )
```
